32 devices in a mesh: wide: 8 (over y, x, core), narrow: 4 (over z).
Axes of the slice: x: 2, y: 2, z: 4, core: 2. Of those that a mesh axis runs over, the one named last changes fastest.
Arguments:
- patches: bfloat16 [16384, 768], P('wide'), may hold values from -6 to 6
- mask_index: int32 [32, 450], P('wide'), may hold values from 0 to 511, as said below
- mask_count: int32 [32], P('wide'), may hold values from 100 to 450, as said below
- mask_embed: float32 [768], replicated, may hold values from -5 to 5
- norm1_gain: float32 [768], replicated, may hold values from 0.5 to 1.5
- norm1_bias: float32 [768], replicated, may hold values from -1 to 1
- w_qkv: bfloat16 [3, 768, 768], P(None, None, 'narrow'), may hold values from -0.21875 to 0.21875
- b_qv: float32 [2, 768], P(None, 'narrow'), may hold values from -1.5 to 1.5
- w_out: bfloat16 [768, 768], P('narrow'), may hold values from -1.75 to 1.75
- b_out: float32 [768], replicated, may hold values from -1 to 1
- norm2_gain: float32 [768], replicated, may hold values from 0.5 to 1.5
- norm2_bias: float32 [768], replicated, may hold values from -1 to 1
- w_up: bfloat16 [768, 3072], P(None, 'narrow'), may hold values from -0.21875 to 0.21875
- b_up: float32 [3072], P('narrow'), may hold values from -2.5 to 2.5
- w_down: bfloat16 [3072, 768], P('narrow'), may hold values from -0.625 to 0.625
- b_down: float32 [768], replicated, may hold values from -1 to 1
- cotangent: bfloat16 [16384, 768], P('wide'), may hold values from -6 to 6
Outputs:
- output: bfloat16 [16384, 768], P('wide')
- patch_grad: bfloat16 [16384, 768], P('wide')
- mask_embed_grad: float32 [768], replicated
- norm1_gain_grad: float32 [768], replicated
- norm1_bias_grad: float32 [768], replicated
- qkv_grad: float32 [3, 768, 768], P(None, None, 'narrow')
- qv_bias_grad: float32 [2, 768], P(None, 'narrow')
- out_grad: float32 [768, 768], P('narrow')
- out_bias_grad: float32 [768], replicated
- norm2_gain_grad: float32 [768], replicated
- norm2_bias_grad: float32 [768], replicated
- up_grad: float32 [768, 3072], P(None, 'narrow')
- up_bias_grad: float32 [3072], P('narrow')
- down_grad: float32 [3072, 768], P('narrow')
- down_bias_grad: float32 [768], replicated
The draws below stay inside these ranges and needn't reach their ends.
Inputs may be any that keep to these rules, and one draw needn't show every extreme that they name: `mask_index`: the 450 entries of a clip are distinct patch positions; only the first mask_count of them are used. `mask_count`: in every draw one clip has exactly 450 masked patches and another exactly 100.
All inputs are finite; a program needn't handle non-finite values.
Results may differ from the reference program's by a relative error of at most 0.014.
The reference program's roundings to bfloat16 on the way count: a program that leaves them out, or rounds other values in their place, can miss the bound.
Values sent between devices are 32-bit elements; how exact they have to be, the bound alone decides.
A program may use at most 128 MiB of HBM per device.

```python
import jax
import jax.numpy as jnp
from jax import lax

D = 768
HEADS = 12
HD = 64
FF = 3072
PATCHES = 512
MASK_MAX = 450
MASK_MIN = 100
CLIPS_DEV = 4
CLIPS = 32
TOKENS = 16384
N_WIDE = 8


def draw_mask_index(key, part):
    key = jax.random.fold_in(key, 11)
    clip_keys = jax.random.split(key, CLIPS)
    orders = jax.vmap(lambda single: jax.random.permutation(single, PATCHES))(clip_keys)
    return orders[:, :MASK_MAX].astype(jnp.int32)


def draw_mask_count(key, part):
    key = jax.random.fold_in(key, 23)
    count_key, pick_key = jax.random.split(key)
    counts = jax.random.randint(count_key, (CLIPS,), MASK_MIN, MASK_MAX + 1)
    chosen = jax.random.permutation(pick_key, CLIPS)
    counts = counts.at[chosen[0]].set(MASK_MAX).at[chosen[1]].set(MASK_MIN)
    return counts.astype(jnp.int32)


def level_of(own_key, dims, pieces, least, high):
    loudness = 1.0
    for dim, shards_of in pieces:
        draws = jax.random.uniform(jax.random.fold_in(jax.random.fold_in(own_key, 6), dim), (shards_of,), jnp.float32, least / len(pieces), high / len(pieces))
        loudness = loudness * jnp.repeat(jnp.exp(draws), dims[dim] // shards_of).reshape((-1,) + (1,) * (len(dims) - 1 - dim))
    return loudness


def bell_draw(rng, shape, scale, most, cuts=(), held_as=jnp.bfloat16):
    values = jax.random.normal(rng, shape, jnp.float32) * scale
    if len(cuts) > 0:
        values = level_of(rng, shape, cuts, -0.22, 0.18) * values
    return jnp.clip(values, min=-most, max=most).astype(held_as)


def setup_inputs(seed: int = 0) -> dict:
    keys = jax.random.split(jax.random.key(seed), 18)
    patches = bell_draw(keys[0], (TOKENS, D), 1.0, 6.0, ((0, 8),))
    mask_index = draw_mask_index(jax.random.fold_in(keys[17], 71), 0)
    mask_count = draw_mask_count(jax.random.fold_in(keys[17], 71), 0)
    mask_embed = bell_draw(keys[3], (D,), 1.0, 5.0, (), jnp.float32)
    norm1_gain = jnp.clip(1.0 + 0.1 * jax.random.normal(keys[4], (D,), jnp.float32), 0.5, 1.5)
    norm1_bias = bell_draw(keys[5], (D,), 0.2, 1.0, (), jnp.float32)
    w_qkv = bell_draw(keys[6], (3, D, D), D ** -0.5, 0.21875, ((2, 4),))
    b_qv = bell_draw(keys[7], (2, D), 0.3, 1.5, ((1, 4),), jnp.float32)
    w_out = bell_draw(keys[8], (D, D), (max(D // 64, 1)) ** -0.5, 1.75, ((0, 4),))
    b_out = bell_draw(keys[9], (D,), 0.2, 1.0, (), jnp.float32)
    norm2_gain = jnp.clip(1.0 + 0.1 * jax.random.normal(keys[10], (D,), jnp.float32), 0.5, 1.5)
    norm2_bias = bell_draw(keys[11], (D,), 0.2, 1.0, (), jnp.float32)
    w_up = bell_draw(keys[12], (D, FF), D ** -0.5, 0.21875, ((1, 4),))
    b_up = bell_draw(keys[13], (FF,), 0.5, 2.5, ((0, 4),), jnp.float32)
    w_down = bell_draw(keys[14], (FF, D), (max(FF // 32, 1)) ** -0.5, 0.625, ((0, 4),))
    b_down = bell_draw(keys[15], (D,), 0.2, 1.0, (), jnp.float32)
    cotangent = bell_draw(keys[16], (TOKENS, D), 1.0, 6.0, ((0, 8),))
    return {"patches": patches, "mask_index": mask_index, "mask_count": mask_count, "mask_embed": mask_embed, "norm1_gain": norm1_gain, "norm1_bias": norm1_bias, "w_qkv": w_qkv, "b_qv": b_qv, "w_out": w_out, "b_out": b_out, "norm2_gain": norm2_gain, "norm2_bias": norm2_bias, "w_up": w_up, "b_up": b_up, "w_down": w_down, "b_down": b_down, "cotangent": cotangent}


@jax.custom_vjp
def low(v):
    return lax.optimization_barrier(v.astype(jnp.bfloat16)).astype(jnp.float32)

@jax.custom_vjp
def low_back(v):
    return v

def low_keep(v):
    return (low(v), None)

def low_pass(kept, grad):
    return (grad,)

def back_keep(v):
    return (v, None)

def back_low(kept, grad):
    return (low(grad),)
low.defvjp(low_keep, low_pass)
low_back.defvjp(back_keep, back_low)
epsilon = 1e-06
precise = lax.Precision.HIGHEST

def masked_rows(mask_index, mask_count, length):
    slot_ids = jnp.arange(mask_index.shape[1], dtype=jnp.int32)
    in_use = slot_ids[None, :] < mask_count[:, None]
    position = jnp.arange(length, dtype=jnp.int32)
    matches = (mask_index[:, :, None] == position[None, None, :]) & in_use[:, :, None]
    return jnp.any(matches, axis=1)

def layer_norm(values, norm_gain, norm_shift):
    centred = values - lax.optimization_barrier(jnp.mean(values, axis=-1, keepdims=True))
    inverse = lax.rsqrt(lax.optimization_barrier(jnp.mean(centred * centred, axis=-1, keepdims=True)) + epsilon)
    return centred * inverse * norm_gain + norm_shift

def attend(heads):
    query_heads, key_heads, value_heads = heads
    scores = low_back(jnp.einsum('qhd,khd->hqk', query_heads, key_heads, precision=precise) * HD ** (-0.5))
    weights = low(jax.nn.softmax(scores, axis=-1))
    return low(low_back(jnp.einsum('hqk,khd->qhd', weights, value_heads, precision=precise)))

def layer_forward(params, patch_rows, masked):
    mask_embed, norm1_gain, norm1_bias, w_qkv, b_qv, w_out, b_out, norm2_gain, norm2_bias, w_up, b_up, w_down, b_down = params
    replaced = jnp.where(masked[:, None], mask_embed[None, :], patch_rows)
    normed = low(layer_norm(replaced, norm1_gain, norm1_bias))
    queries = low(low_back(jnp.dot(normed, w_qkv[0], precision=precise) + b_qv[0]))
    key_rows = low(low_back(jnp.dot(normed, w_qkv[1], precision=precise)))
    value_rows = low(low_back(jnp.dot(normed, w_qkv[2], precision=precise) + b_qv[1]))
    head_shape = (-1, PATCHES, HEADS, HD)
    context = lax.map(jax.checkpoint(attend), (queries.reshape(head_shape), key_rows.reshape(head_shape), value_rows.reshape(head_shape)))
    context = context.reshape(-1, D)
    middle = replaced + low_back(jnp.dot(context, w_out, precision=precise)) + b_out
    hidden_in = low(layer_norm(middle, norm2_gain, norm2_bias))
    before = low_back(jnp.dot(hidden_in, w_up, precision=precise) + b_up)
    active = low(jax.nn.gelu(before, approximate=False))
    return middle + low_back(jnp.dot(active, w_down, precision=precise)) + b_down

def reference(patches, mask_index, mask_count, mask_embed, norm1_gain, norm1_bias, w_qkv, b_qv, w_out, b_out, norm2_gain, norm2_bias, w_up, b_up, w_down, b_down, cotangent):
    params = tuple((argument.astype(jnp.float32) for argument in (mask_embed, norm1_gain, norm1_bias, w_qkv, b_qv, w_out, b_out, norm2_gain, norm2_bias, w_up, b_up, w_down, b_down)))
    masked = masked_rows(mask_index, mask_count, PATCHES).reshape(N_WIDE, CLIPS_DEV * PATCHES)
    inputs = patches.astype(jnp.float32).reshape(N_WIDE, CLIPS_DEV * PATCHES, D)
    incoming = cotangent.astype(jnp.float32).reshape(N_WIDE, CLIPS_DEV * PATCHES, D)

    def group_step(totals, group):
        group_in, group_mask, group_cot = group

        def run_group(weights, block_in):
            return layer_forward(weights, block_in, group_mask)
        result, pullback = jax.vjp(run_group, params, group_in)
        weight_grads, input_grad = pullback(group_cot)
        totals = jax.tree.map(lambda running, update: running + update, totals, weight_grads)
        return (totals, (result.astype(jnp.bfloat16), input_grad.astype(jnp.bfloat16)))
    initial = jax.tree.map(jnp.zeros_like, params)
    totals, (result, input_grad) = lax.scan(group_step, initial, (inputs, masked, incoming))
    return (result.reshape(-1, D), input_grad.reshape(-1, D), totals[0], totals[1], totals[2], totals[3], totals[4], totals[5], totals[6], totals[7], totals[8], totals[9], totals[10], totals[11], totals[12])
```

```python
import math

import jax
import jax.numpy as jnp
from jax import lax
from jax.sharding import PartitionSpec as P

HD = 64
PATCHES = 512
epsilon = 1e-06
f32 = jnp.float32
bf16 = jnp.bfloat16


def masked_rows(mask_index, mask_count, length):
    slot_ids = jnp.arange(mask_index.shape[1], dtype=jnp.int32)
    in_use = slot_ids[None, :] < mask_count[:, None]
    position = jnp.arange(length, dtype=jnp.int32)
    matches = (mask_index[:, :, None] == position[None, None, :]) & in_use[:, :, None]
    return jnp.any(matches, axis=1)


def norm_forward(values, norm_gain, norm_shift):
    centred = values - jnp.mean(values, axis=-1, keepdims=True)
    inverse = lax.rsqrt(jnp.mean(centred * centred, axis=-1, keepdims=True) + epsilon)
    scaled = centred * inverse
    return ((scaled * norm_gain + norm_shift).astype(bf16), scaled, inverse)


def norm_backward(upstream, scaled, inverse, norm_gain):
    weighted = upstream * norm_gain
    centred_grad = (
        weighted
        - jnp.mean(weighted, axis=-1, keepdims=True)
        - scaled * jnp.mean(weighted * scaled, axis=-1, keepdims=True)
    )
    return (inverse * centred_grad, jnp.sum(upstream * scaled, axis=0), jnp.sum(upstream, axis=0))


def gelu_parts(values):
    cdf = 0.5 * (1.0 + lax.erf(values * 0.5**0.5))
    slope = cdf + values * jnp.exp(-0.5 * values * values) * (0.5 / math.pi) ** 0.5
    return values * cdf, slope


def mm(spec, a, b):
    return jnp.einsum(spec, a, b, preferred_element_type=f32)


def make(mesh):
    nw, nz = mesh.shape["wide"], mesh.shape["narrow"]

    def on_device(
        patches, mask_index, mask_count, mask_embed, norm1_gain, norm1_bias, w_qkv, b_qv, w_out, b_out,
        norm2_gain, norm2_bias, w_up, b_up, w_down, b_down, cotangent,
    ):
        w, z = lax.axis_index("wide"), lax.axis_index("narrow")
        rows, d = patches.shape
        own = rows // nz
        hs = w_qkv.shape[2]
        fs = w_up.shape[1]
        qkv_t = jnp.swapaxes(w_qkv, 1, 2).reshape(3 * hs, d)
        pieces = (qkv_t, w_out, w_up, w_down)
        one = jnp.where(mask_count[0] >= 0, 1.0, 2.0).astype(f32)
        full = []
        for piece in pieces:
            n = piece.shape[0] // nw
            part = lax.dynamic_slice_in_dim(piece, w * n, n, 0).astype(f32)
            got = lax.all_gather(part, ("narrow", "wide"), axis=0, tiled=True)
            full.append((got * one).reshape((nz,) + piece.shape).astype(bf16))
        wq = full[0].reshape(nz, 3, hs, d).transpose(1, 0, 2, 3).reshape(3, nz * hs, d)
        wo = full[1].reshape(nz * hs, d)
        wu, wd = full[2], full[3]
        bq = lax.all_gather(b_qv, "narrow", axis=1, tiled=True)
        bu = lax.all_gather(b_up, "narrow", axis=0, tiled=False)
        heads = nz * hs // HD

        clip = lambda a: lax.dynamic_slice_in_dim(a, z * own, own, 0)
        masked = clip(masked_rows(mask_index, mask_count, PATCHES).reshape(-1, 1))
        rep = jnp.where(masked, mask_embed[None, :], clip(patches).astype(f32))
        cot = clip(cotangent)
        normed, xh1, r1 = norm_forward(rep, norm1_gain, norm1_bias)
        qkv = mm("td,jed->jte", normed, wq)
        qkv = qkv + jnp.stack([bq[0], jnp.zeros_like(bq[0]), bq[1]])[:, None, :]
        qkv = qkv.astype(bf16).reshape(3, own, heads, HD)
        q, k, v = qkv[0], qkv[1], qkv[2]
        scores = mm("qhd,khd->hqk", q, k) * HD**-0.5
        probs = jax.nn.softmax(scores, axis=-1)
        att = probs.astype(bf16)
        ctx = mm("hqk,khd->qhd", att, v).astype(bf16).reshape(own, -1)
        middle = rep + mm("te,ed->td", ctx, wo) + b_out
        hid, xh2, r2 = norm_forward(middle, norm2_gain, norm2_bias)
        before = mm("td,zdf->ztf", hid, wu) + bu[:, None, :]
        act, slope = gelu_parts(before)
        act = act.astype(bf16)
        out = middle + mm("ztf,zfd->td", act, wd) + b_down
        cf = cot.astype(f32)
        down_g = mm("ztf,td->zfd", act, cot)
        bg = (mm("td,zfd->ztf", cot, wd) * slope).astype(bf16)
        up_g = mm("td,ztf->zdf", hid, bg)
        up_bias = jnp.sum(bg, axis=1, dtype=f32)
        hg = mm("ztf,zdf->td", bg, wu)
        mp, g2, b2 = norm_backward(hg, xh2, r2, norm2_gain)
        mg = cf + mp
        ml = mg.astype(bf16)
        out_g = mm("te,td->ed", ctx, ml)
        cg = mm("td,ed->te", ml, wo).astype(bf16).reshape(own, heads, HD)
        vg = mm("hqk,qhd->khd", att, cg).astype(bf16)
        pg = mm("qhd,khd->hqk", cg, v)
        sg = (probs * (pg - jnp.sum(probs * pg, axis=-1, keepdims=True))).astype(bf16)
        qg = (mm("hqk,khd->qhd", sg, k) * HD**-0.5).astype(bf16)
        kg = (mm("hqk,qhd->khd", sg, q) * HD**-0.5).astype(bf16)
        grads = jnp.stack([qg, kg, vg]).reshape(3, own, -1)
        qkv_g = mm("jte,td->jed", grads, normed)
        qv_bias = jnp.stack([jnp.sum(grads[0], axis=0, dtype=f32), jnp.sum(grads[2], axis=0, dtype=f32)])
        ng = mm("jte,jed->td", grads, wq)
        rp, g1, b1 = norm_backward(ng, xh1, r1, norm1_gain)
        rg = mg + rp
        embed = jnp.sum(jnp.where(masked, rg, 0.0), axis=0)
        pgr = jnp.where(masked, 0.0, rg)

        def rows_out(a):
            got = lax.all_gather(a, "narrow", axis=0, tiled=True)
            return (got * one).astype(bf16)

        output = rows_out(out)
        patch_grad = rows_out(pgr)

        def weight_out(a):
            nzz, n, dd = a.shape
            r = lax.psum_scatter(
                a.reshape(nzz, nw, n // nw, dd), "wide", scatter_dimension=1, tiled=True
            )
            r = lax.psum_scatter(r, "narrow", scatter_dimension=0, tiled=True)
            return lax.all_gather(r.reshape(n // nw, dd), "wide", axis=0, tiled=True)

        down_o = weight_out(down_g)
        up_o = weight_out(up_g)
        out_o = weight_out(out_g.reshape(nz, hs, d))
        qkv_o = weight_out(
            qkv_g.reshape(3, nz, hs, d).transpose(1, 0, 2, 3).reshape(nz, 3 * hs, d)
        )
        qkv_o = jnp.swapaxes(qkv_o.reshape(3, hs, d), 1, 2)
        small = jnp.concatenate(
            [jnp.stack([embed, g1, b1, jnp.sum(mg, axis=0), g2, b2, jnp.sum(cf, axis=0)]), qv_bias, up_bias.reshape(-1, d)]
        )
        small = lax.psum(small, ("wide", "narrow"))
        qvb = lax.dynamic_slice_in_dim(small[7:9], z * hs, hs, 1)
        upb = lax.dynamic_slice_in_dim(small[9:].reshape(-1), z * fs, fs, 0)
        return (
            output, patch_grad, small[0], small[1], small[2], qkv_o, qvb, out_o, small[3],
            small[4], small[5], up_o, upb, down_o, small[6],
        )

    return on_device


def solution(mesh):
    return jax.shard_map(
        make(mesh),
        mesh=mesh,
        in_specs=(
            P("wide", None), P("wide", None), P("wide"), P(), P(), P(), P(None, None, "narrow"), P(None, "narrow"),
            P("narrow", None), P(), P(), P(), P(None, "narrow"), P("narrow"), P("narrow", None), P(), P("wide", None),
        ),
        out_specs=(
            P("wide", None), P("wide", None), P(), P(), P(), P(None, None, "narrow"), P(None, "narrow"),
            P("narrow", None), P(), P(), P(), P(None, "narrow"), P("narrow"), P("narrow", None), P(),
        ),
        check_vma=False,
    )
```

```python
import functools
import math

import jax
import jax.numpy as jnp
from jax import lax
from jax.experimental import pallas as pl
from jax.experimental.pallas import tpu as pltpu
from jax.sharding import PartitionSpec as P

HD = 64
PATCHES = 512
EPS = 1e-06
f32 = jnp.float32
bf16 = jnp.bfloat16
MESH = pl.DeviceIdType.MESH
RT = 128


def masked_rows(mask_index, mask_count, length):
    slot_ids = jnp.arange(mask_index.shape[1], dtype=jnp.int32)
    in_use = slot_ids[None, :] < mask_count[:, None]
    position = jnp.arange(length, dtype=jnp.int32)
    matches = (mask_index[:, :, None] == position[None, None, :]) & in_use[:, :, None]
    return jnp.any(matches, axis=1)


def nn(a, b):
    return lax.dot_general(a, b, (((1,), (0,)), ((), ())), preferred_element_type=f32)


def nt(a, b):
    return lax.dot_general(a, b, (((1,), (1,)), ((), ())), preferred_element_type=f32)


def tn(a, b):
    return lax.dot_general(a, b, (((0,), (0,)), ((), ())), preferred_element_type=f32)


def rds(start, size, unit=8):
    if isinstance(start, int):
        return pl.ds(start, size)
    return pl.ds(pl.multiple_of(start, unit), size)


def normalise(v):
    centred = v - jnp.mean(v, axis=-1, keepdims=True)
    inverse = lax.rsqrt(jnp.mean(centred * centred, axis=-1, keepdims=True) + EPS)
    return centred * inverse, inverse


def norm_back(upstream, xhat, inverse, gain):
    weighted = upstream * gain
    return inverse * (
        weighted
        - jnp.mean(weighted, axis=-1, keepdims=True)
        - xhat * jnp.mean(weighted * xhat, axis=-1, keepdims=True)
    )


def softmax_t(scores):
    e = jnp.exp(scores - jnp.max(scores, axis=0, keepdims=True))
    return e * (1.0 / jnp.sum(e, axis=0, keepdims=True))


class Cfg:
    pass


def make_cfg(mesh, d, t, hs):
    g = Cfg()
    g.nw, g.nz = mesh.shape["wide"], mesh.shape["narrow"]
    g.groups = g.nw // 8
    g.d, g.t, g.hs = d, t, hs
    g.pr = d // 8
    g.units = 3 * g.nz
    g.wbits = g.nw.bit_length() - 1
    g.zbits = g.nz.bit_length() - 1
    n = 0
    for name, count in (
        ("agz", 3 * g.nz), ("agx", g.units), ("agy", g.units), ("agdx", g.units), ("agdy", g.units), ("agc", g.units),
        ("rc", g.units), ("rdx", g.units), ("rdy", g.units), ("rpx", g.units), ("rpy", g.units), ("rz", 3 * g.nz),
        ("fx", 3), ("fy", 3), ("fdx", 3), ("fdy", 3), ("fc", 3), ("zb", g.nz), ("pg", g.nz), ("sm", g.wbits + g.zbits),
        ("fg", 3 * g.groups),
    ):
        setattr(g, name, n)
        n += count
    g.nsem = n
    return g


def layer_kernel(
    g,
    part, zb, mask, vecs, patches, cot_hbm,
    out, pg, ga, gb, gc, small_out, wbuf, crecv, dxr, dyr, pxr, pyr, zr, grecv,
    wq, wo, ffw, res, xh1, xh2, normed, qkv, ctx, hid, act, slope, cotv, acc, hg, bg, dqkv, r1, r2, rsb, cst, dst, pst,
    zst, zball, sm, smr, fin, ss, rs, ls,
):
    nz, d, t, hs, pr, units = g.nz, g.d, g.t, g.hs, g.pr, g.units
    half = pr // 2
    ff_units = 2 * nz
    w = lax.axis_index("wide")
    z = lax.axis_index("narrow")
    c, x, y = w % 2, (w // 2) % 2, (w // 4) % 2
    sib, xn, yn = {"wide": w + 1 - 2 * c}, {"wide": w + 2 - 4 * x}, {"wide": w + 4 - 8 * y}
    yx, yx_x, yx_y, yx_d = y * 2 + x, y * 2 + 1 - x, (1 - y) * 2 + x, (1 - y) * 2 + 1 - x
    pos, pos_x, pos_y, pos_d = c * 4 + yx, c * 4 + yx_x, c * 4 + yx_y, c * 4 + yx_d
    zp = [None] + [{"narrow": (z + k) % nz} for k in range(1, nz)]
    gp = [None] + [{"wide": (w + 8 * k) % g.nw} for k in range(1, g.groups)]
    gouts = (ga, gb, gc)

    def rcopy(src, dst, si, ri, dev):
        return pltpu.make_async_remote_copy(src, dst, ss.at[si], rs.at[ri], device_id=dev, device_id_type=MESH)

    barrier = pltpu.get_barrier_semaphore()
    partners = [sib, xn, yn] + zp[1:] + gp[1:]
    for p in partners:
        pl.semaphore_signal(barrier, inc=1, device_id=p, device_id_type=MESH)

    def row(v, i):
        return v[i : i + 1, :]

    def wrow(p, zk, q):
        return (p * nz + zk) * d + q * pr

    def ag_pk(n):
        if isinstance(n, int) and n < nz:
            return 0, n
        m = n - nz
        return 1 + m % 2, m // 2

    def own_copy(p):
        return pltpu.make_async_copy(part.at[pl.ds(p * pr, pr)], wbuf.at[rds(wrow(p, z, pos), pr)], ls.at[p])

    def ag_block(n, q, lo, size):
        p, k = ag_pk(n)
        return wbuf.at[rds(wrow(p, (z + k) % nz, q) + lo, size)]

    def ag_xy(n):
        b = ag_block(n, pos, 0, pr)
        return rcopy(b, b, g.agx + n, g.agx + n, xn), rcopy(b, b, g.agy + n, g.agy + n, yn)

    def ag_d(n):
        bx, by = ag_block(n, pos_x, 0, half), ag_block(n, pos_y, half, half)
        return rcopy(bx, bx, g.agdy + n, g.agdy + n, yn), rcopy(by, by, g.agdx + n, g.agdx + n, xn)

    def ag_c(n):
        b = ag_block(n, c * 4, 0, 4 * pr)
        return rcopy(b, b, g.agc + n, g.agc + n, sib)

    def agz(p, k):
        return rcopy(
            part.at[pl.ds(p * pr, pr)], wbuf.at[rds(wrow(p, z, pos), pr)], g.agz + p * nz + k, g.agz + p * nz + nz - k, zp[k]
        )

    def ag_s1(n):
        p, k = ag_pk(n)

        def wait_z():
            b = ag_block(n, pos, 0, pr)
            rcopy(b, b, g.agz + p * nz + k, g.agz + p * nz + k, xn).wait_recv()

        if isinstance(n, int):
            if k > 0:
                wait_z()
        else:
            pl.when(k > 0)(wait_z)
        for cp in ag_xy(n):
            cp.start()

    def ag_s2(n):
        cx, cy = ag_xy(n)
        dy, dx = ag_d(n)
        cx.wait_recv()
        dy.start()
        cy.wait_recv()
        dx.start()

    def ag_s3(n):
        dy, dx = ag_d(n)
        dy.wait_recv()
        dx.wait_recv()
        ag_c(n).start()

    def ag_conv(n):
        ag_c(n).wait_recv()
        p, k = ag_pk(n)
        zk = (z + k) % nz
        cps = [
            pltpu.make_async_copy(wbuf.at[rds(wrow(p, zk, 4 * i), 4 * pr)], cst.at[pl.ds(i * 4 * pr, 4 * pr)], ls.at[3 + i])
            for i in range(2)
        ]
        for cp in cps:
            cp.start()
        for cp in cps:
            cp.wait()
        if isinstance(n, int) and n < nz:
            for j in range(3):
                wq[j, rds(zk * hs, hs, 16), :] = cst[j * hs : (j + 1) * hs, :].astype(bf16)
            wo[rds(zk * hs, hs, 16), :] = cst[3 * hs : 4 * hs, :].astype(bf16)
        else:
            ffw[n - nz] = cst[...].astype(bf16)

    def ag_step(n):
        def run(cond, fn):
            if isinstance(cond, bool):
                if cond:
                    fn()
            else:
                pl.when(cond)(fn)

        run(n + 2 < units, lambda: ag_s1(n + 2))
        run(n < units, lambda: ag_s2(n))
        if not isinstance(n, int) or n >= 1:
            run(n - 1 < units, lambda: ag_s3(n - 1))
        if not isinstance(n, int) or n >= 2:
            run(n - 2 < units, lambda: ag_conv(n - 2))

    def ru_pk(u):
        if isinstance(u, int):
            return (2 - u % 2, u // 2) if u < ff_units else (0, u - ff_units)
        late = u // ff_units
        return (1 - late) * (2 - u % 2), (1 - late) * (u // 2) + late * (u - ff_units)

    def slot_row(u):
        return (u % 4) * d

    def sum_row(u, q):
        if isinstance(u, int):
            base = 4 * d + u * 4 * pr if u < ff_units else slot_row(u - ff_units) + c * 4 * pr
        else:
            late = u // ff_units
            base = (1 - late) * (4 * d + u * 4 * pr) + late * ((u - ff_units) * d + c * 4 * pr)
        return base + q * pr

    def rs_core(u):
        return rcopy(
            rsb.at[rds(slot_row(u) + (1 - c) * 4 * pr, 4 * pr)], crecv.at[rds(u * 4 * pr, 4 * pr)], g.rc + u, g.rc + u, sib
        )

    def rs_d(u):
        a = rcopy(rsb.at[rds(sum_row(u, yx_d), half)], dxr.at[rds(u * half, half)], g.rdx + u, g.rdx + u, xn)
        b = rcopy(rsb.at[rds(sum_row(u, yx_d) + half, half)], dyr.at[rds(u * half, half)], g.rdy + u, g.rdy + u, yn)
        return a, b

    def rs_p(u):
        a = rcopy(rsb.at[rds(sum_row(u, yx_x), pr)], pxr.at[rds(u * pr, pr)], g.rpx + u, g.rpx + u, xn)
        b = rcopy(rsb.at[rds(sum_row(u, yx_y), pr)], pyr.at[rds(u * pr, pr)], g.rpy + u, g.rpy + u, yn)
        return a, b

    def rs_z(u, dev):
        p, k = ru_pk(u)
        return rcopy(
            rsb.at[rds(sum_row(u, yx), pr)], zr.at[rds((p * nz + nz - k) * pr, pr)], g.rz + p * nz + k, g.rz + p * nz + nz - k, dev
        )

    def rs_step1(u):
        rs_core(u).wait_recv()
        cp = pltpu.make_async_copy(crecv.at[rds(u * 4 * pr, 4 * pr)], cst.at[pl.ds(0, 4 * pr)], ls.at[3])
        cp.start()
        cp.wait()
        src = slot_row(u) + c * 4 * pr
        rsb[rds(sum_row(u, 0), 4 * pr), :] = rsb[rds(src, 4 * pr), :] + cst[0 : 4 * pr, :]
        for cp in rs_d(u):
            cp.start()

    def rs_step2(u):
        a, b = rs_d(u)
        a.wait_recv()
        c0 = pltpu.make_async_copy(dxr.at[rds(u * half, half)], dst.at[pl.ds(0, half)], ls.at[3])
        c0.start()
        b.wait_recv()
        c1 = pltpu.make_async_copy(dyr.at[rds(u * half, half)], dst.at[pl.ds(half, half)], ls.at[4])
        c1.start()
        c0.wait()
        rsb[rds(sum_row(u, yx_y), half), :] += dst[0:half, :]
        c1.wait()
        rsb[rds(sum_row(u, yx_x) + half, half), :] += dst[half:pr, :]
        for cp in rs_p(u):
            cp.start()

    def rs_step3(u):
        a, b = rs_p(u)
        a.wait_recv()
        c0 = pltpu.make_async_copy(pxr.at[rds(u * pr, pr)], pst.at[pl.ds(0, pr)], ls.at[3])
        c0.start()
        b.wait_recv()
        c1 = pltpu.make_async_copy(pyr.at[rds(u * pr, pr)], pst.at[pl.ds(pr, pr)], ls.at[4])
        c1.start()
        c0.wait()
        c1.wait()
        rsb[rds(sum_row(u, yx), pr), :] += pst[0:pr, :] + pst[pr : 2 * pr, :]
        p, k = ru_pk(u)
        pl.when(k > 0)(lambda: rs_z(u, {"narrow": (z + k) % nz}).start())

    own_unit = {0: ff_units, 1: 1, 2: 0}

    def fin_xy(p):
        src = fin.at[pl.ds(p * pr, pr)]
        to = gouts[p].at[rds(pos * pr, pr)]
        return rcopy(src, to, g.fx + p, g.fx + p, xn), rcopy(src, to, g.fy + p, g.fy + p, yn)

    def fin_own(p):
        return pltpu.make_async_copy(fin.at[pl.ds(p * pr, pr)], gouts[p].at[rds(pos * pr, pr)], ls.at[5 + p])

    def fin_d(p):
        bx, by = gouts[p].at[rds(pos_x * pr, half)], gouts[p].at[rds(pos_y * pr + half, half)]
        return rcopy(bx, bx, g.fdy + p, g.fdy + p, yn), rcopy(by, by, g.fdx + p, g.fdx + p, xn)

    def fin_c(p):
        b = gouts[p].at[rds(c * 4 * pr, 4 * pr)]
        return rcopy(b, b, g.fc + p, g.fc + p, sib)

    def fin_g(p, k):
        return rcopy(
            fin.at[pl.ds(p * pr, pr)], grecv.at[pl.ds((p * g.groups + g.groups - k) * pr, pr)],
            g.fg + p * g.groups + k, g.fg + p * g.groups + g.groups - k, gp[k],
        )

    def rs_step4(p):
        total = rsb[rds(sum_row(own_unit[p], yx), pr), :]
        cps = []
        for k in range(1, nz):
            src = zr.at[pl.ds((p * nz + k) * pr, pr)]
            rcopy(src, src, g.rz + p * nz + k, g.rz + p * nz + k, xn).wait_recv()
            cps.append(pltpu.make_async_copy(src, zst.at[pl.ds((k - 1) * pr, pr)], ls.at[2 + k]))
            cps[-1].start()
        for k, cp in enumerate(cps):
            cp.wait()
            total = total + zst[k * pr : (k + 1) * pr, :]
        fin[p * pr : (p + 1) * pr, :] = total
        if g.groups > 1:
            for k in range(1, g.groups):
                fin_g(p, k).start()
            for k in range(1, g.groups):
                fin_g(p, k).wait()
            for k in range(1, g.groups):
                src = grecv.at[pl.ds((p * g.groups + k) * pr, pr)]
                cp = pltpu.make_async_copy(src, zst.at[pl.ds(0, pr)], ls.at[3])
                cp.start()
                cp.wait()
                total = total + zst[0:pr, :]
            fin[p * pr : (p + 1) * pr, :] = total
        fin_own(p).start()
        for cp in fin_xy(p):
            cp.start()

    def rs_step5(p):
        cx, cy = fin_xy(p)
        dy, dx = fin_d(p)
        cx.wait_recv()
        dy.start()
        cy.wait_recv()
        dx.start()

    def rs_step6(p):
        dy, dx = fin_d(p)
        dy.wait_recv()
        dx.wait_recv()
        fin_own(p).wait()
        fin_c(p).start()

    def sm_copy(i):
        if i < g.wbits:
            b = 1 << i
            dev = {"wide": w + b - 2 * b * ((w // b) % 2)}
        else:
            b = 1 << (i - g.wbits)
            dev = {"narrow": z + b - 2 * b * ((z // b) % 2)}
        return rcopy(sm, smr.at[pl.ds(16 * i, 16)], g.sm + i, g.sm + i, dev)

    def sm_start(i):
        sm_copy(i).start()

    def sm_finish(i):
        sm_copy(i).wait()
        sm[...] += smr[16 * i : 16 * (i + 1), :]

    def tiles(fn):
        def body(i, carry):
            fn(rds(i * RT, RT, RT))
            return carry

        lax.fori_loop(0, t // RT, body, 0)

    def load_patches(clip):
        cp = pltpu.make_async_copy(patches.at[rds(clip * t, t, 16)], bg, ls.at[8])
        cp.start()
        cp.wait()

    def first_norm(clip, keep):
        embed, gain, bias = row(vecs, 0), row(vecs, 1), row(vecs, 2)

        def fn(sl):
            m = mask[rds(clip * t + sl.start, RT), :]
            v = jnp.where(m > 0.5, embed, bg[sl, :].astype(f32))
            res[sl, :] = v
            xhat, inverse = normalise(v)
            if keep:
                xh1[sl, :] = xhat
                r1[sl, :] = inverse
            normed[sl, :] = (xhat * gain + bias).astype(bf16)

        tiles(fn)

    def project():
        biases = []
        for i in (1, 2):
            total = zball[i : i + 1, :]
            for k in range(1, nz):
                total = total + zball[8 * k + i : 8 * k + i + 1, :]
            biases.append(total)
        n = normed[...]
        qkv[0] = ((nt(n, wq[0]) + biases[0]).astype(bf16) * bf16(HD**-0.5)).astype(bf16)
        qkv[1] = nt(n, wq[1]).astype(bf16)
        qkv[2] = (nt(n, wq[2]) + biases[1]).astype(bf16)

    def head_masks():
        lane = lax.broadcasted_iota(jnp.int32, (1, 2 * HD), 1)
        first = (lane < HD).astype(f32)
        return first.astype(bf16), (1.0 - first).astype(bf16)

    def attend(i):
        sl = rds(i * 2 * HD, 2 * HD, 2 * HD)
        qp, kp, vp = qkv[0, :, sl], qkv[1, :, sl], qkv[2, :, sl]
        vt = vp.T
        outs = []
        for h, hm in enumerate(head_masks()):
            probs = softmax_t(nt(kp * hm, qp)).astype(bf16)
            outs.append(nn(vt[h * HD : (h + 1) * HD, :], probs))
        ctx[:, sl] = jnp.concatenate(outs, axis=0).T.astype(bf16)

    def attend_range(lo, hi):
        def body(i, carry):
            attend(i)
            return carry

        lax.fori_loop(lo, hi, body, 0)

    def second_norm(keep):
        acc[...] = nn(ctx[...], wo[...])
        b_out, gain, bias = row(vecs, 3), row(vecs, 4), row(vecs, 5)

        def fn(sl):
            v = res[sl, :] + acc[sl, :] + b_out
            res[sl, :] = v
            xhat, inverse = normalise(v)
            if keep:
                xh2[sl, :] = xhat
                r2[sl, :] = inverse
            hid[sl, :] = (xhat * gain + bias).astype(bf16)
            acc[sl, :] = jnp.zeros((RT, d), f32)

        tiles(fn)

    def feed(k, keep):
        bias = row(zball[rds(((z + k) % nz) * 8, 8), :], 0)
        slope[...] = nn(hid[...], ffw[2 * k])

        def fn(sl):
            v = slope[sl, :] + bias
            cdf = 0.5 * (1.0 + lax.erf(v * (0.5**0.5)))
            act[sl, :] = (v * cdf).astype(bf16)
            if keep:
                slope[sl, :] = cdf + v * jnp.exp(-0.5 * v * v) * ((0.5 / math.pi) ** 0.5)

        tiles(fn)
        acc[...] += nn(act[...], ffw[2 * k + 1])

    def write_out(clip):
        b_down = row(vecs, 6)

        def fn(sl):
            act[sl, :] = (res[sl, :] + acc[sl, :] + b_down).astype(bf16)

        tiles(fn)
        cp = pltpu.make_async_copy(act, out.at[rds(clip * t, t, 16)], ls.at[8])
        cp.start()
        cp.wait()

    def feed_back(k):
        acc2 = nt(cotv[...], ffw[2 * k + 1])
        b = (acc2 * slope[...]).astype(bf16)
        bg[...] = b
        u = 9 + (z + k) % nz
        sm[pl.ds(u, 1), :] = jnp.sum(b.astype(f32), axis=0, keepdims=True)
        part_sum = nt(bg[...], ffw[2 * k])

        @pl.when(k == 0)
        def _():
            hg[...] = part_sum

        @pl.when(k > 0)
        def _():
            hg[...] += part_sum

    zero_rows = jnp.zeros((16, d), f32)
    sm[...] = zero_rows
    cot_copy = pltpu.make_async_copy(cot_hbm.at[rds(z * t, t, 16)], cotv, ls.at[9])
    cot_copy.start()
    for p in range(3):
        own_copy(p).start()
    zball[rds(z * 8, 8), :] = zb[...]
    pl.semaphore_wait(barrier, len(partners))
    for p in range(3):
        for k in range(1, nz):
            agz(p, k).start()
    zb_copies = [
        rcopy(zb, zball.at[rds(z * 8, 8)], g.zb + k, g.zb + nz - k, zp[k]) for k in range(1, nz)
    ]
    for cp in zb_copies:
        cp.start()
    for p in range(3):
        own_copy(p).wait()
    ag_s1(0)
    ag_s1(1)
    load_patches(z)
    first_norm(z, True)
    for n in range(nz + 2):
        ag_step(n)
    for k in range(1, nz):
        rcopy(zb, zball.at[rds(((z + k) % nz) * 8, 8)], g.zb + k, g.zb + k, zp[k]).wait_recv()
    pairs = nz * hs // (2 * HD)
    project()
    ag_step(nz + 2)
    attend_range(0, pairs // 2)
    ag_step(nz + 3)
    attend_range(pairs // 2, pairs)
    second_norm(True)
    cot_copy.wait()

    def ff_body(k, carry):
        u = 2 * k

        @pl.when(k >= 2)
        def _():
            rs_core(u - 4).wait_send()
            rs_core(u - 3).wait_send()

        feed(k, True)
        rsb[rds(slot_row(u), d), :] = tn(act[...], cotv[...])
        rs_core(u).start()
        ag_step(nz + 4 + 2 * k)
        feed_back(k)
        rsb[rds(slot_row(u + 1), d), :] = tn(hid[...], bg[...])
        rs_core(u + 1).start()
        ag_step(nz + 5 + 2 * k)
        rs_step1(u)
        rs_step1(u + 1)
        return carry

    lax.fori_loop(0, nz, ff_body, 0)
    write_out(z)

    gain2 = row(vecs, 4)
    g2 = jnp.zeros((1, d), f32)

    def mid_back(i, carry):
        sg, sb, so, sc = carry
        sl = rds(i * RT, RT, RT)
        up, xhat = hg[sl, :], xh2[sl, :]
        cf = cotv[sl, :].astype(f32)
        mg = cf + norm_back(up, xhat, r2[sl, :], gain2)
        res[sl, :] = mg
        act[sl, :] = mg.astype(bf16)
        return (
            sg + jnp.sum(up * xhat, axis=0, keepdims=True),
            sb + jnp.sum(up, axis=0, keepdims=True),
            so + jnp.sum(mg, axis=0, keepdims=True),
            sc + jnp.sum(cf, axis=0, keepdims=True),
        )

    sg, sb, so, sc = lax.fori_loop(0, t // RT, mid_back, (g2, g2, g2, g2))
    sm[3:4, :], sm[4:5, :], sm[5:6, :], sm[6:7, :] = so, sg, sb, sc
    bg[...] = nt(act[...], wo[...]).astype(bf16)

    def att_back(i, carry):
        sl = rds(i * 2 * HD, 2 * HD, 2 * HD)
        qp, kp, vp, cg = qkv[0, :, sl], qkv[1, :, sl], qkv[2, :, sl], bg[:, sl]
        kt = kp.T
        masks = head_masks()
        dv = dk = None
        dq = []
        for h, hm in enumerate(masks):
            probs = softmax_t(nt(kp * hm, qp))
            dp = nt(vp * hm, cg)
            delta = jnp.sum(probs * dp, axis=0, keepdims=True)
            ds = (probs * (dp - delta)).astype(bf16)
            hf = hm.astype(f32)
            dv_h = nn(probs.astype(bf16), cg) * hf
            dk_h = nn(ds, qp) * hf
            dv = dv_h if dv is None else dv + dv_h
            dk = dk_h if dk is None else dk + dk_h
            dq.append(nn(kt[h * HD : (h + 1) * HD, :], ds))
        dqkv[0, :, sl] = (jnp.concatenate(dq, axis=0).T * (HD**-0.5)).astype(bf16)
        dqkv[1, :, sl] = dk.astype(bf16)
        dqkv[2, :, sl] = dv.astype(bf16)
        rs_step2(i)
        pl.when(i > 0)(lambda: rs_step3(i - 1))
        return carry

    lax.fori_loop(0, pairs, att_back, 0)

    for u in range(ff_units - 4, ff_units):
        rs_core(u).wait_send()
    for j in range(4):
        if j < 3:
            big = tn(dqkv[j], normed[...])
        else:
            big = tn(ctx[...], act[...])
        for zz in range(nz):
            k = (zz + nz - z) % nz
            rsb[rds(k * d + j * hs, hs), :] = big[zz * hs : (zz + 1) * hs, :]
    for u in range(ff_units, units):
        rs_core(u).start()
    acc[...] = nn(dqkv[0], wq[0]) + nn(dqkv[1], wq[1]) + nn(dqkv[2], wq[2])
    for j, r in ((0, 7), (2, 8)):
        sm[r : r + 1, :] = jnp.sum(dqkv[j].astype(f32), axis=0, keepdims=True)

    gain1 = row(vecs, 1)

    def first_back(i, carry):
        se, sg, sb = carry
        sl = rds(i * RT, RT, RT)
        up, xhat = acc[sl, :], xh1[sl, :]
        m = mask[rds(z * t + i * RT, RT), :] > 0.5
        rg = res[sl, :] + norm_back(up, xhat, r1[sl, :], gain1)
        hg[sl, :] = jnp.where(m, 0.0, rg)
        return (
            se + jnp.sum(jnp.where(m, rg, 0.0), axis=0, keepdims=True),
            sg + jnp.sum(up * xhat, axis=0, keepdims=True),
            sb + jnp.sum(up, axis=0, keepdims=True),
        )

    se, sg, sb = lax.fori_loop(0, t // RT, first_back, (g2, g2, g2))
    sm[0:1, :], sm[1:2, :], sm[2:3, :] = se, sg, sb
    pg_own = pltpu.make_async_copy(hg, pg.at[rds(z * t, t)], ls.at[9])
    pg_own.start()
    pg_copies = [rcopy(hg, pg.at[rds(z * t, t)], g.pg + k, g.pg + nz - k, zp[k]) for k in range(1, nz)]
    for cp in pg_copies:
        cp.start()
    for u in range(ff_units, units):
        rs_step1(u)

    nsm = g.wbits + g.zbits

    def service(s):
        pl.when(s + pairs < units)(lambda: rs_step2(s + pairs))
        pl.when(s + pairs - 1 < units)(lambda: rs_step3(s + pairs - 1))
        for i in range(nsm + 1):
            @pl.when(s == i)
            def _():
                if i > 0:
                    sm_finish(i - 1)
                if i < nsm:
                    sm_start(i)
        first = ff_units - pairs + 1
        for p, lead in ((2, 0), (1, 1)):
            pl.when(s == first + lead)(lambda: rs_step4(p))
            pl.when(s == first + lead + 1)(lambda: rs_step5(p))
            pl.when(s == first + lead + 2)(lambda: rs_step6(p))

    def rest(s, carry):
        clip = (z + 1 + s // 4) % nz
        seg = s % 4

        @pl.when(seg == 0)
        def _():
            load_patches(clip)
            first_norm(clip, False)
            project()

        @pl.when(seg == 1)
        def _():
            attend_range(0, pairs // 2)

        @pl.when(seg == 2)
        def _():
            attend_range(pairs // 2, pairs)
            second_norm(False)

        @pl.when(seg == 3)
        def _():
            def body(k, cc):
                feed(k, False)
                return cc

            lax.fori_loop(0, nz, body, 0)
            write_out(clip)

        service(s)
        return carry

    lax.fori_loop(0, 4 * (nz - 1), rest, 0)
    rs_step4(0)
    rs_step5(0)
    rs_step6(0)
    so_copy = pltpu.make_async_copy(sm, small_out, ls.at[9])
    pg_own.wait()
    so_copy.start()

    for cp in zb_copies:
        cp.wait_send()
    for cp in pg_copies:
        cp.wait()
    for p in range(3):
        for k in range(1, nz):
            agz(p, k).wait_send()
            u = {0: ff_units + k, 1: 2 * k + 1, 2: 2 * k}[p]
            rs_z(u, zp[k]).wait_send()
        fin_c(p).wait()
        for cp in fin_xy(p) + fin_d(p):
            cp.wait_send()
    for n in range(units):
        for cp in ag_xy(n) + ag_d(n) + (ag_c(n),) + rs_d(n) + rs_p(n):
            cp.wait_send()
    for u in range(ff_units, units):
        rs_core(u).wait_send()
    so_copy.wait()


def make(mesh):
    def on_device(
        patches, mask_index, mask_count, mask_embed, norm1_gain, norm1_bias, w_qkv, b_qv, w_out, b_out,
        norm2_gain, norm2_bias, w_up, b_up, w_down, b_down, cotangent,
    ):
        rows, d = patches.shape
        nz = mesh.shape["narrow"]
        t, hs, fs = rows // nz, w_qkv.shape[2], w_up.shape[1]
        assert t == PATCHES and fs == d and 4 * hs == d
        g = make_cfg(mesh, d, t, hs)
        pr = g.pr
        w, z = lax.axis_index("wide"), lax.axis_index("narrow")
        pos = (w % 2) * 4 + (w // 2) % 4
        first_piece = jnp.concatenate([jnp.swapaxes(w_qkv, 1, 2).reshape(3 * hs, d), w_out])
        part = jnp.concatenate(
            [lax.dynamic_slice_in_dim(a, pos * pr, pr, 0) for a in (first_piece, w_up, w_down)]
        ).astype(f32)
        zb = jnp.zeros((8, d), f32).at[0].set(b_up)
        zb = lax.dynamic_update_slice(zb, b_qv, (1, z * hs))
        mask = masked_rows(mask_index, mask_count, PATCHES).reshape(-1, 1).astype(f32)
        vecs = jnp.stack(
            [mask_embed, norm1_gain, norm1_bias, b_out, norm2_gain, norm2_bias, b_down, jnp.zeros_like(b_down)]
        )
        hbm = pl.BlockSpec(memory_space=pl.ANY)
        vm = pl.BlockSpec(memory_space=pltpu.VMEM)
        u = g.units

        def o(r, dt=f32):
            return jax.ShapeDtypeStruct((r, d), dt)

        out_shape = (
            o(rows, bf16), o(rows), o(d), o(d), o(d), o(16),
            o(u * d), o(u * 4 * pr), o(u * pr // 2), o(u * pr // 2), o(u * pr), o(u * pr), o(u * pr), o(3 * g.groups * pr),
        )
        v = pltpu.VMEM
        scratch = [
            v((3, d, d), bf16), v((d, d), bf16), v((2 * nz, d, d), bf16),
            v((t, d), f32), v((t, d), f32), v((t, d), f32), v((t, d), bf16), v((3, t, d), bf16),
            v((t, d), bf16), v((t, d), bf16), v((t, d), bf16), v((t, d), f32), v((t, d), bf16), v((t, d), f32),
            v((t, d), f32), v((t, d), bf16), v((3, t, d), bf16), v((t, 1), f32), v((t, 1), f32),
            v((4 * d + 2 * nz * 4 * pr, d), f32), v((d, d), f32), v((pr, d), f32), v((2 * pr, d), f32),
            v(((nz - 1) * pr, d), f32), v((nz * 8, d), f32), v((16, d), f32), v(((g.wbits + g.zbits) * 16, d), f32),
            v((3 * pr, d), f32),
            pltpu.SemaphoreType.DMA((g.nsem,)), pltpu.SemaphoreType.DMA((g.nsem,)), pltpu.SemaphoreType.DMA((10,)),
        ]
        outs = pl.pallas_call(
            functools.partial(layer_kernel, g),
            out_shape=out_shape,
            in_specs=[hbm, vm, vm, vm, hbm, hbm],
            out_specs=[hbm] * len(out_shape),
            scratch_shapes=scratch,
            compiler_params=pltpu.CompilerParams(
                collective_id=1, has_side_effects=True, vmem_limit_bytes=64 * 2**20 - 2**17
            ),
            name="layer",
        )(part, zb, mask, vecs, patches, cotangent)
        output, pg, ga, gb, gc, small = outs[:6]
        qkv_o = jnp.swapaxes(ga[: 3 * hs].reshape(3, hs, d), 1, 2)
        qvb = lax.dynamic_slice_in_dim(small[7:9], z * hs, hs, 1)
        upb = lax.dynamic_slice_in_dim(small[9 : 9 + nz], z, 1, 0).reshape(-1)
        return (
            output, pg.astype(bf16), small[0], small[1], small[2], qkv_o, qvb, ga[3 * hs :], small[3],
            small[4], small[5], gb, upb, gc, small[6],
        )

    return on_device


def solution(mesh):
    return jax.shard_map(
        make(mesh),
        mesh=mesh,
        in_specs=(
            P("wide", None), P("wide", None), P("wide"), P(), P(), P(), P(None, None, "narrow"), P(None, "narrow"),
            P("narrow", None), P(), P(), P(), P(None, "narrow"), P("narrow"), P("narrow", None), P(), P("wide", None),
        ),
        out_specs=(
            P("wide", None), P("wide", None), P(), P(), P(), P(None, None, "narrow"), P(None, "narrow"),
            P("narrow", None), P(), P(), P(), P(None, "narrow"), P("narrow"), P("narrow", None), P(),
        ),
        check_vma=False,
    )
```

```python
import functools
import math

import jax
import jax.numpy as jnp
from jax import lax
from jax.experimental import pallas as pl
from jax.experimental.pallas import tpu as pltpu
from jax.sharding import PartitionSpec as P

HD = 64
PATCHES = 512
EPS = 1e-06
f32 = jnp.float32
bf16 = jnp.bfloat16
MESH = pl.DeviceIdType.MESH
RT = 128


def nn(a, b):
    return lax.dot_general(a, b, (((1,), (0,)), ((), ())), preferred_element_type=f32)


def nt(a, b):
    return lax.dot_general(a, b, (((1,), (1,)), ((), ())), preferred_element_type=f32)


def tn(a, b):
    return lax.dot_general(a, b, (((0,), (0,)), ((), ())), preferred_element_type=f32)


def rds(start, size, unit=8):
    if isinstance(start, int):
        return pl.ds(start, size)
    return pl.ds(pl.multiple_of(start, unit), size)


def normalise(v):
    centred = v - jnp.mean(v, axis=-1, keepdims=True)
    inverse = lax.rsqrt(jnp.mean(centred * centred, axis=-1, keepdims=True) + EPS)
    return centred * inverse, inverse


def norm_back(upstream, xhat, inverse, gain):
    weighted = upstream * gain
    return inverse * (
        weighted
        - jnp.mean(weighted, axis=-1, keepdims=True)
        - xhat * jnp.mean(weighted * xhat, axis=-1, keepdims=True)
    )


def softmax_t(scores):
    e = jnp.exp(scores - jnp.max(scores, axis=0, keepdims=True))
    return e * (1.0 / jnp.sum(e, axis=0, keepdims=True))


class Cfg:
    pass


def make_cfg(mesh, d, t, hs):
    g = Cfg()
    g.nw, g.nz = mesh.shape["wide"], mesh.shape["narrow"]
    assert g.nz == 4
    g.groups = g.nw // 8
    g.d, g.t, g.hs = d, t, hs
    g.pr = d // 8
    g.units = 3 * g.nz
    g.agu = 3 * (g.nz - 1)
    g.xr = g.pr // 3
    g.wbits = g.nw.bit_length() - 1
    g.zbits = g.nz.bit_length() - 1
    g.chunks = 4
    n = 0
    for name, count in (
        ("agz", 6 * g.nz), ("age", 6 * g.nz), ("agx", g.agu), ("agy", g.agu), ("agdx", g.agu), ("agdy", g.agu), ("agc", g.agu),
        ("rc", g.units), ("rdx", g.units), ("rdy", g.units), ("rpx", g.units), ("rpy", g.units), ("rz", 6 * g.nz),
        ("fx", 3), ("fy", 3), ("fdx", 3), ("fdy", 3), ("fc", 3), ("zb", g.nz), ("pg", 2 * g.nz * g.chunks),
        ("sm", g.wbits + g.zbits), ("fg", 3 * g.groups),
    ):
        setattr(g, name, n)
        n += count
    g.nsem = n
    return g


def when(cond, fn):
    if isinstance(cond, bool):
        if cond:
            fn()
    else:
        pl.when(cond)(fn)


def layer_kernel(
    g,
    part, first_piece, w_up, w_down, zb, midx, vecs, patches, cot_hbm,
    out, pg, ga, gb, gc, small_out, wbuf, crecv, dxr, dyr, pxr, pyr, zr, grecv,
    wq, wo, ffw, res, xh1, xh2, normed, qkv, ctx, hid, act, slope, cotv, acc, hg, bg, dqkv, r1, r2, mown, rsb, cst, rst,
    dst, pst, zst, zball, sm, smr, fin, ss, rs, ls,
):
    nz, d, t, hs, pr, units = g.nz, g.d, g.t, g.hs, g.pr, g.units
    half = pr // 2
    ff_units = 2 * nz
    w = lax.axis_index("wide")
    z = lax.axis_index("narrow")
    c, x, y = w % 2, (w // 2) % 2, (w // 4) % 2
    sib, xn, yn = {"wide": w + 1 - 2 * c}, {"wide": w + 2 - 4 * x}, {"wide": w + 4 - 8 * y}
    zup, zdn = {"narrow": z + 1}, {"narrow": z - 1}
    has_up, has_dn = z < nz - 1, z > 0
    mid = (z > 0) & (z < nz - 1)
    yx, yx_x, yx_y, yx_d = y * 2 + x, y * 2 + 1 - x, (1 - y) * 2 + x, (1 - y) * 2 + 1 - x
    pos, pos_x, pos_y, pos_d = c * 4 + yx, c * 4 + yx_x, c * 4 + yx_y, c * 4 + yx_d
    zp = [None] + [{"narrow": (z + k) % nz} for k in range(1, nz)]
    gp = [None] + [{"wide": (w + 8 * k) % g.nw} for k in range(1, g.groups)]
    gouts = (ga, gb, gc)

    zside = z // 2
    zend = z + zside * (nz - 1 - 2 * z)

    def swap01(k):
        return k + zend * (1 - k // 2) * (1 - 2 * (k % 2))

    def zk(k):
        b = swap01(k)
        return b + zside * (nz - 1 - 2 * b)

    def zk_inv(zz):
        return swap01(zz + zside * (nz - 1 - 2 * zz))

    def rcopy(src, dst, si, ri, dev):
        return pltpu.make_async_remote_copy(src, dst, ss.at[si], rs.at[ri], device_id=dev, device_id_type=MESH)

    barrier = pltpu.get_barrier_semaphore()
    partners = [sib, xn, yn] + zp[1:] + gp[1:]
    for p in partners:
        pl.semaphore_signal(barrier, inc=1, device_id=p, device_id_type=MESH)

    def wrow(p, zz, q):
        return (p * nz + zz) * d + q * pr

    xr = g.xr
    hr = (pr - xr) // 2
    agu = g.agu

    def ag_pk(n):
        if isinstance(n, int) and n < nz - 1:
            return 0, n + 1
        m = n - (nz - 1)
        return 1 + m % 2, 1 + m // 2

    def own_loads():
        cps = [(first_piece.at[pl.ds(j * hs, hs)], wq.at[j, rds(z * hs, hs, 16)]) for j in range(3)]
        cps += [(first_piece.at[pl.ds(3 * hs, hs)], wo.at[rds(z * hs, hs, 16)]), (w_up, ffw.at[0]), (w_down, ffw.at[1])]
        return [pltpu.make_async_copy(src, dst, ls.at[i]) for i, (src, dst) in enumerate(cps)]

    def ag_block(n, q, lo, size):
        p, k = ag_pk(n)
        return wbuf.at[rds(wrow(p, zk(k), q) + lo, size)]

    def ag_xy(n):
        b = ag_block(n, pos, 0, pr)
        return rcopy(b, b, g.agx + n, g.agx + n, xn), rcopy(b, b, g.agy + n, g.agy + n, yn)

    def ag_d(n):
        bx, by = ag_block(n, pos_x, xr, hr), ag_block(n, pos_y, xr + hr, hr)
        return rcopy(bx, bx, g.agdy + n, g.agdy + n, yn), rcopy(by, by, g.agdx + n, g.agdx + n, xn)

    def ag_c(n):
        b = ag_block(n, c * 4, 0, 4 * pr)
        return rcopy(b, b, g.agc + n, g.agc + n, sib)

    def agz(p, zz, up, own=False):
        pair = []
        for sem, q, lo, size in ((g.agz, pos, 0, pr), (g.age, pos_d, pr, xr)):
            to = wbuf.at[rds(wrow(p, zz, q), size)]
            src = part.at[pl.ds(p * (pr + xr) + lo, size)] if own else to
            ri = sem + p * nz + zz
            pair.append(rcopy(src, to, ri + (0 if up else 3 * nz), ri, zup if up else zdn))
        return pair

    def start(cps):
        for cp in cps:
            cp.start()

    def agz_own(p):
        pl.when(has_up)(lambda: start(agz(p, z, True, True)))
        pl.when(has_dn)(lambda: start(agz(p, z, False, True)))

    def ag_z(n):
        p, k = ag_pk(n)
        zz = zk(k)

        @pl.when(mid)
        def _():
            for i, cp in enumerate(agz(p, zz, True)):
                cp.wait_recv()
                pl.when(zz < z)(lambda: agz(p, zz, True)[i].start())
                pl.when(zz > z)(lambda: agz(p, zz, False)[i].start())

    def ag_s1(n):
        p, k = ag_pk(n)
        pl.when(jnp.logical_not(mid))(lambda: agz(p, zk(k), True)[0].wait_recv())
        start(ag_xy(n))

    def ag_s2(n):
        cx, cy = ag_xy(n)
        dy, dx = ag_d(n)
        cx.wait_recv()
        dy.start()
        cy.wait_recv()
        dx.start()

    def ag_s3(n):
        p, k = ag_pk(n)
        pl.when(jnp.logical_not(mid))(lambda: agz(p, zk(k), True)[1].wait_recv())
        dy, dx = ag_d(n)
        dy.wait_recv()
        dx.wait_recv()
        ag_c(n).start()

    def ag_load(n):
        p, k = ag_pk(n)
        return [
            pltpu.make_async_copy(
                wbuf.at[rds(wrow(p, zk(k), 4 * i), 4 * pr)], cst.at[pl.ds(i * 4 * pr, 4 * pr)], ls.at[10 + i]
            )
            for i in range(2)
        ]

    def ag_conv_start(n):
        ag_c(n).wait_recv()
        start(ag_load(n))

    def ag_conv(n):
        for cp in ag_load(n):
            cp.wait()
        p, k = ag_pk(n)
        if isinstance(n, int) and n < nz - 1:
            zz = zk(k)
            for j in range(3):
                wq[j, rds(zz * hs, hs, 16), :] = cst[j * hs : (j + 1) * hs, :].astype(bf16)
            wo[rds(zz * hs, hs, 16), :] = cst[3 * hs : 4 * hs, :].astype(bf16)
        else:
            ffw[2 * k + p - 1] = cst[...].astype(bf16)

    def ag_step(n):
        static = isinstance(n, int)
        when(n < agu, lambda: ag_s2(n))
        if static:
            when(n + 2 < agu, lambda: ag_s1(n + 2))
            when(n + 3 < agu, lambda: ag_z(n + 3))
        when(n - 1 >= 0, lambda: when(n - 1 < agu, lambda: ag_s3(n - 1)))
        if not static or (n >= 2 and n != nz):
            when(n - 2 < agu, lambda: ag_conv(n - 2))
        if not static or n >= 1:
            when(n - 1 < agu, lambda: ag_conv_start(n - 1))
        if static and n == nz - 1:
            ag_conv(n - 1)

    def ru_pk(u):
        if isinstance(u, int):
            return (2 - (ff_units - 1 - u) % 2, (ff_units - 1 - u) // 2) if u < ff_units else (0, units - 1 - u)
        late = u // ff_units
        return (
            (1 - late) * (2 - (2 * ff_units - 1 - u) % 2),
            (1 - late) * ((ff_units - 1 - u + late * ff_units) // 2) + late * (units - 1 - u),
        )

    def slot_row(u):
        return ((2 * ff_units - 1 - u) % 4) * d

    def sum_row(u, q):
        if isinstance(u, int):
            base = 4 * d + u * 4 * pr if u < ff_units else slot_row(u) + c * 4 * pr
        else:
            late = u // ff_units
            base = (1 - late) * (4 * d + u * 4 * pr) + late * (slot_row(u) + c * 4 * pr)
        return base + q * pr

    def rs_core(u):
        return rcopy(
            rsb.at[rds(slot_row(u) + (1 - c) * 4 * pr, 4 * pr)], crecv.at[rds(u * 4 * pr, 4 * pr)], g.rc + u, g.rc + u, sib
        )

    def rs_d(u):
        a = rcopy(rsb.at[rds(sum_row(u, yx_d), half)], dxr.at[rds(u * half, half)], g.rdx + u, g.rdx + u, xn)
        b = rcopy(rsb.at[rds(sum_row(u, yx_d) + half, half)], dyr.at[rds(u * half, half)], g.rdy + u, g.rdy + u, yn)
        return a, b

    def rs_p(u):
        a = rcopy(rsb.at[rds(sum_row(u, yx_x), pr)], pxr.at[rds(u * pr, pr)], g.rpx + u, g.rpx + u, xn)
        b = rcopy(rsb.at[rds(sum_row(u, yx_y), pr)], pyr.at[rds(u * pr, pr)], g.rpy + u, g.rpy + u, yn)
        return a, b

    def rs_z(u, zz, up):
        p, _ = ru_pk(u)
        i = (p * nz + zz) * 2 + (0 if up else 1)
        return rcopy(rsb.at[rds(sum_row(u, yx), pr)], zr.at[rds(i * pr, pr)], g.rz + i, g.rz + i, zup if up else zdn)

    def rs_z_load(p, zz, up, slot):
        i = (p * nz + zz) * 2 + (0 if up else 1)
        src = zr.at[rds(i * pr, pr)]
        return (
            rcopy(src, src, g.rz + i, g.rz + i, sib),
            pltpu.make_async_copy(src, zst.at[pl.ds(slot * pr, pr)], ls.at[18 + slot]),
        )

    def l1(u):
        return pltpu.make_async_copy(crecv.at[rds(u * 4 * pr, 4 * pr)], rst, ls.at[12])

    def step1a(u):
        rs_core(u).wait_recv()
        l1(u).start()

    def step1b(u):
        l1(u).wait()
        src = slot_row(u) + c * 4 * pr
        rsb[rds(sum_row(u, 0), 4 * pr), :] = rsb[rds(src, 4 * pr), :] + rst[...]

    def step1c(u):
        for cp in rs_d(u):
            cp.start()

    def l2(u):
        return (
            pltpu.make_async_copy(dxr.at[rds(u * half, half)], dst.at[pl.ds(0, half)], ls.at[13]),
            pltpu.make_async_copy(dyr.at[rds(u * half, half)], dst.at[pl.ds(half, half)], ls.at[14]),
        )

    def step2a(u):
        for cp, ld in zip(rs_d(u), l2(u)):
            cp.wait_recv()
            ld.start()

    def step2b(u):
        for ld in l2(u):
            ld.wait()
        rsb[rds(sum_row(u, yx_y), half), :] += dst[0:half, :]
        rsb[rds(sum_row(u, yx_x) + half, half), :] += dst[half:pr, :]
        for cp in rs_p(u):
            cp.start()

    def l3(u):
        return (
            pltpu.make_async_copy(pxr.at[rds(u * pr, pr)], pst.at[pl.ds(0, pr)], ls.at[15]),
            pltpu.make_async_copy(pyr.at[rds(u * pr, pr)], pst.at[pl.ds(pr, pr)], ls.at[16]),
        )

    def step3a(u):
        for cp, ld in zip(rs_p(u), l3(u)):
            cp.wait_recv()
            ld.start()

    def zdir(u):
        _, k = ru_pk(u)
        zz = zk(k)
        return zz, zz > z, zz < z

    def step3b(u):
        for ld in l3(u):
            ld.wait()
        rsb[rds(sum_row(u, yx), pr), :] += pst[0:pr, :] + pst[pr : 2 * pr, :]
        zz, up, dn = zdir(u)
        pl.when(up & (z == 0))(lambda: rs_z(u, zz, True).start())
        pl.when(dn & (z == nz - 1))(lambda: rs_z(u, zz, False).start())

    def step_z(u):
        p, _ = ru_pk(u)
        zz, up, dn = zdir(u)
        for cond, flag in ((up, True), (dn, False)):
            @pl.when(cond & mid)
            def _():
                got, ld = rs_z_load(p, zz, flag, 0)
                got.wait_recv()
                ld.start()
                ld.wait()
                rsb[rds(sum_row(u, yx), pr), :] += zst[0:pr, :]
                rs_z(u, zz, flag).start()

    own_unit = {0: units - 1, 1: ff_units - 2, 2: ff_units - 1}

    def fin_xy(p):
        src = fin.at[pl.ds(p * pr, pr)]
        to = gouts[p].at[rds(pos * pr, pr)]
        return rcopy(src, to, g.fx + p, g.fx + p, xn), rcopy(src, to, g.fy + p, g.fy + p, yn)

    def fin_own(p):
        return pltpu.make_async_copy(fin.at[pl.ds(p * pr, pr)], gouts[p].at[rds(pos * pr, pr)], ls.at[5 + p])

    def fin_d(p):
        bx, by = gouts[p].at[rds(pos_x * pr, half)], gouts[p].at[rds(pos_y * pr + half, half)]
        return rcopy(bx, bx, g.fdy + p, g.fdy + p, yn), rcopy(by, by, g.fdx + p, g.fdx + p, xn)

    def fin_c(p):
        b = gouts[p].at[rds(c * 4 * pr, 4 * pr)]
        return rcopy(b, b, g.fc + p, g.fc + p, sib)

    def fin_g(p, k):
        return rcopy(
            fin.at[pl.ds(p * pr, pr)], grecv.at[pl.ds((p * g.groups + g.groups - k) * pr, pr)],
            g.fg + p * g.groups + k, g.fg + p * g.groups + g.groups - k, gp[k],
        )

    def step4(p):
        sl = slice(p * pr, (p + 1) * pr)
        fin[sl, :] = rsb[rds(sum_row(own_unit[p], yx), pr), :]
        ins = ((has_dn, True, 0), (has_up, False, 1))
        for cond, flag, slot in ins:
            @pl.when(cond)
            def _():
                got, ld = rs_z_load(p, z, flag, slot)
                got.wait_recv()
                ld.start()

        for cond, flag, slot in ins:
            @pl.when(cond)
            def _():
                rs_z_load(p, z, flag, slot)[1].wait()
                fin[sl, :] += zst[slot * pr : (slot + 1) * pr, :]

        if g.groups > 1:
            total = fin[sl, :]
            for k in range(1, g.groups):
                fin_g(p, k).start()
            for k in range(1, g.groups):
                fin_g(p, k).wait()
            for k in range(1, g.groups):
                src = grecv.at[pl.ds((p * g.groups + k) * pr, pr)]
                cp = pltpu.make_async_copy(src, zst.at[pl.ds(0, pr)], ls.at[3])
                cp.start()
                cp.wait()
                total = total + zst[0:pr, :]
            fin[sl, :] = total
        fin_own(p).start()
        for cp in fin_xy(p):
            cp.start()

    def step5(p):
        cx, cy = fin_xy(p)
        dy, dx = fin_d(p)
        cx.wait_recv()
        dy.start()
        cy.wait_recv()
        dx.start()

    def step6(p):
        dy, dx = fin_d(p)
        dy.wait_recv()
        dx.wait_recv()
        fin_own(p).wait()
        fin_c(p).start()

    def sm_copy(i):
        if i < g.wbits:
            b = 1 << i
            dev = {"wide": w + b - 2 * b * ((w // b) % 2)}
        else:
            b = 1 << (i - g.wbits)
            dev = {"narrow": z + b - 2 * b * ((z // b) % 2)}
        return rcopy(sm, smr.at[pl.ds(16 * i, 16)], g.sm + i, g.sm + i, dev)

    def sm_finish(i):
        sm_copy(i).wait()
        sm[...] += smr[16 * i : 16 * (i + 1), :]

    ck = t // g.chunks

    def pg_copy(zz, q, up):
        to = pg.at[rds(zz * t + q * ck, ck)]
        ri = g.pg + zz * g.chunks + q
        return rcopy(to, to, ri + (0 if up else nz * g.chunks), ri, zup if up else zdn)

    def pg_send(zz, q, up):
        pg_copy(zz, q, up).start()

    def pg_step(s):
        @pl.when(s < g.chunks)
        def _():
            pl.when(has_up)(lambda: pg_send(z, s, True))
            pl.when(has_dn)(lambda: pg_send(z, s, False))

        j = s - g.chunks
        for up, zz, count, more in (
            (True, z - 1 - j // g.chunks, g.chunks * z, has_up),
            (False, z + 1 + j // g.chunks, g.chunks * (nz - 1 - z), has_dn),
        ):
            @pl.when((j >= 0) & (j < count) & more)
            def _():
                pg_copy(zz, j % g.chunks, up).wait_recv()
                pg_send(zz, j % g.chunks, up)

    embed, gain1, bias1, b_out, gain2, bias2, b_down = [vecs[i : i + 1, :] for i in range(7)]

    def tiles(fn):
        def body(i, carry):
            fn(rds(i * RT, RT, RT), i * RT)
            return carry

        lax.fori_loop(0, t // RT, body, 0)

    def patches_copy(clip):
        return pltpu.make_async_copy(patches.at[rds(clip * t, t, 16)], bg, ls.at[8])

    def first_norm(clip, keep):
        listed = midx[pl.ds(clip, 1), :]

        def fn(sl, at):
            place = lax.broadcasted_iota(jnp.int32, (RT, listed.shape[1]), 0) + at
            m = jnp.max(jnp.where(listed == place, 1.0, 0.0), axis=1, keepdims=True)
            v = jnp.where(m > 0.5, embed, bg[sl, :].astype(f32))
            res[sl, :] = v
            xhat, inverse = normalise(v)
            if keep:
                mown[sl, :] = m
                xh1[sl, :] = xhat
                r1[sl, :] = inverse
            normed[sl, :] = (xhat * gain1 + bias1).astype(bf16)

        tiles(fn)

    def project():
        biases = []
        for i in (1, 2):
            total = zball[i : i + 1, :]
            for k in range(1, nz):
                total = total + zball[8 * k + i : 8 * k + i + 1, :]
            biases.append(total)
        n = normed[...]
        qkv[0] = ((nt(n, wq[0]) + biases[0]).astype(bf16) * bf16(HD**-0.5)).astype(bf16)
        qkv[1] = nt(n, wq[1]).astype(bf16)
        qkv[2] = (nt(n, wq[2]) + biases[1]).astype(bf16)

    def head_masks():
        lane = lax.broadcasted_iota(jnp.int32, (1, 2 * HD), 1)
        first = (lane < HD).astype(f32)
        return first.astype(bf16), (1.0 - first).astype(bf16)

    def attend(i):
        sl = rds(i * 2 * HD, 2 * HD, 2 * HD)
        qp, kp, vp = qkv[0, :, sl], qkv[1, :, sl], qkv[2, :, sl]
        vt = vp.T
        outs = []
        for h, hm in enumerate(head_masks()):
            probs = softmax_t(nt(kp * hm, qp)).astype(bf16)
            outs.append(nn(vt[h * HD : (h + 1) * HD, :], probs))
        ctx[:, sl] = jnp.concatenate(outs, axis=0).T.astype(bf16)

    def attend_range(lo, hi):
        def body(i, carry):
            attend(i)
            return carry

        lax.fori_loop(lo, hi, body, 0)

    def second_norm(keep):
        acc[...] = nn(ctx[...], wo[...])

        def fn(sl, at):
            v = res[sl, :] + acc[sl, :] + b_out
            res[sl, :] = v
            xhat, inverse = normalise(v)
            if keep:
                xh2[sl, :] = xhat
                r2[sl, :] = inverse
            hid[sl, :] = (xhat * gain2 + bias2).astype(bf16)
            acc[sl, :] = jnp.zeros((RT, d), f32)

        tiles(fn)

    def feed(k, keep):
        bias = zball[rds(zk(k) * 8, 8), :][0:1, :]
        slope[...] = nn(hid[...], ffw[2 * k])

        def fn(sl, at):
            v = slope[sl, :] + bias
            cdf = 0.5 * (1.0 + lax.erf(v * (0.5**0.5)))
            act[sl, :] = (v * cdf).astype(bf16)
            if keep:
                slope[sl, :] = cdf + v * jnp.exp(-0.5 * v * v) * ((0.5 / math.pi) ** 0.5)

        tiles(fn)
        acc[...] += nn(act[...], ffw[2 * k + 1])

    def write_out(clip):
        def fn(sl, at):
            act[sl, :] = (res[sl, :] + acc[sl, :] + b_down).astype(bf16)

        tiles(fn)
        cp = pltpu.make_async_copy(act, out.at[rds(clip * t, t, 16)], ls.at[8])
        cp.start()
        cp.wait()

    def feed_back(k):
        acc2 = nt(cotv[...], ffw[2 * k + 1])
        b = (acc2 * slope[...]).astype(bf16)
        bg[...] = b
        sm[pl.ds(9 + zk(k), 1), :] = jnp.sum(b.astype(f32), axis=0, keepdims=True)
        part_sum = nt(bg[...], ffw[2 * k])

        @pl.when(k == 0)
        def _():
            hg[...] = part_sum

        @pl.when(k > 0)
        def _():
            hg[...] += part_sum

    sm[...] = jnp.zeros((16, d), f32)
    cot_copy = pltpu.make_async_copy(cot_hbm.at[rds(z * t, t, 16)], cotv, ls.at[9])
    patches_copy(z).start()
    own = own_loads()
    start(own)
    cot_copy.start()
    zball[rds(z * 8, 8), :] = zb[...]
    pl.semaphore_wait(barrier, len(partners))
    agz_own(0)
    zb_copies = [
        rcopy(zb, zball.at[rds(z * 8, 8)], g.zb + k, g.zb + nz - k, zp[k]) for k in range(1, nz)
    ]
    start(zb_copies)
    patches_copy(z).wait()
    first_norm(z, True)
    ag_z(0)
    ag_s1(0)
    ag_z(1)
    pl.when(mid)(lambda: ag_s1(1))
    ag_z(2)
    agz_own(1)
    agz_own(2)
    ag_s2(0)
    pl.when(jnp.logical_not(mid))(lambda: ag_s1(1))
    ag_s1(2)
    ag_z(3)
    for n in range(1, nz):
        ag_step(n)
    for cp in own:
        cp.wait()
    for k in range(1, nz):
        rcopy(zb, zball.at[rds(((z + k) % nz) * 8, 8)], g.zb + k, g.zb + k, zp[k]).wait_recv()
    pairs = nz * hs // (2 * HD)
    project()
    for i in range(3):
        ag_step(nz + i)
        attend_range(i * pairs // 3, (i + 1) * pairs // 3)
    second_norm(True)
    cot_copy.wait()

    def ff_body(k, carry):
        ud, uu = ff_units - 1 - 2 * k, ff_units - 2 - 2 * k
        ag_step(nz + 3 + k)

        @pl.when(k >= 2)
        def _():
            rs_core(ud + 4).wait_send()
            rs_core(uu + 4).wait_send()

        pl.when(k >= 1)(lambda: step1a(ud + 2))
        feed(k, True)
        rsb[rds(slot_row(ud), d), :] = tn(act[...], cotv[...])
        rs_core(ud).start()

        @pl.when(k >= 1)
        def _():
            step1b(ud + 2)
            step1c(ud + 2)
            step1a(uu + 2)

        feed_back(k)

        @pl.when(k >= 1)
        def _():
            step1b(uu + 2)
            step1c(uu + 2)

        rsb[rds(slot_row(uu), d), :] = tn(hid[...], bg[...])
        rs_core(uu).start()
        return carry

    lax.fori_loop(0, nz, ff_body, 0)
    for u in (1, 0):
        step1a(u)
        step1b(u)
        step1c(u)
    step2a(ff_units - 1)

    none = jnp.zeros((1, d), f32)

    def mid_back(i, carry):
        sg, sb, so, sc = carry
        sl = rds(i * RT, RT, RT)
        up, xhat = hg[sl, :], xh2[sl, :]
        cf = cotv[sl, :].astype(f32)
        mg = cf + norm_back(up, xhat, r2[sl, :], gain2)
        v = res[sl, :] + acc[sl, :] + b_down
        hid[sl, :] = v.astype(bf16)
        res[sl, :] = mg
        act[sl, :] = mg.astype(bf16)
        return (
            sg + jnp.sum(up * xhat, axis=0, keepdims=True),
            sb + jnp.sum(up, axis=0, keepdims=True),
            so + jnp.sum(mg, axis=0, keepdims=True),
            sc + jnp.sum(cf, axis=0, keepdims=True),
        )

    sg, sb, so, sc = lax.fori_loop(0, t // RT, mid_back, (none, none, none, none))
    sm[3:4, :], sm[4:5, :], sm[5:6, :], sm[6:7, :] = so, sg, sb, sc
    out_own = pltpu.make_async_copy(hid, out.at[rds(z * t, t, 16)], ls.at[8])
    out_own.start()
    bg[...] = nt(act[...], wo[...]).astype(bf16)
    step2b(ff_units - 1)

    def att_back(i, carry):
        sl = rds(i * 2 * HD, 2 * HD, 2 * HD)
        qp, kp, vp, cg = qkv[0, :, sl], qkv[1, :, sl], qkv[2, :, sl], bg[:, sl]
        kt = kp.T
        masks = head_masks()
        dv = dk = None
        dq = []
        for h, hm in enumerate(masks):
            probs = softmax_t(nt(kp * hm, qp))
            dp = nt(vp * hm, cg)
            delta = jnp.sum(probs * dp, axis=0, keepdims=True)
            ds = (probs * (dp - delta)).astype(bf16)
            hf = hm.astype(f32)
            dv_h = nn(probs.astype(bf16), cg) * hf
            dk_h = nn(ds, qp) * hf
            dv = dv_h if dv is None else dv + dv_h
            dk = dk_h if dk is None else dk + dk_h
            dq.append(nn(kt[h * HD : (h + 1) * HD, :], ds))
        dqkv[0, :, sl] = (jnp.concatenate(dq, axis=0).T * (HD**-0.5)).astype(bf16)
        dqkv[1, :, sl] = dk.astype(bf16)
        dqkv[2, :, sl] = dv.astype(bf16)
        pl.when(i > 0)(lambda: step2b(i - 1))
        step2a(i)
        return carry

    lax.fori_loop(0, pairs, att_back, 0)
    acc[...] = nn(dqkv[0], wq[0]) + nn(dqkv[1], wq[1]) + nn(dqkv[2], wq[2])
    step2b(pairs - 1)

    def first_back(i, carry):
        se, sg, sb = carry
        sl = rds(i * RT, RT, RT)
        up, xhat = acc[sl, :], xh1[sl, :]
        m = mown[sl, :] > 0.5
        rg = res[sl, :] + norm_back(up, xhat, r1[sl, :], gain1)
        hg[sl, :] = jnp.where(m, 0.0, rg)
        return (
            se + jnp.sum(jnp.where(m, rg, 0.0), axis=0, keepdims=True),
            sg + jnp.sum(up * xhat, axis=0, keepdims=True),
            sb + jnp.sum(up, axis=0, keepdims=True),
        )

    se, sg, sb = lax.fori_loop(0, t // RT, first_back, (none, none, none))
    sm[0:1, :], sm[1:2, :], sm[2:3, :] = se, sg, sb
    pg_own = pltpu.make_async_copy(hg, pg.at[rds(z * t, t)], ls.at[9])
    pg_own.start()
    for j, r in ((0, 7), (2, 8)):
        sm[r : r + 1, :] = jnp.sum(dqkv[j].astype(f32), axis=0, keepdims=True)

    for u in range(4):
        rs_core(u).wait_send()
    pg_own.wait()
    pg_step(0)
    pg_step(1)
    for j in range(4):
        if j < 3:
            big = tn(dqkv[j], normed[...])
        else:
            big = tn(ctx[...], act[...])
        for zz in range(nz):
            rsb[rds(zk_inv(zz) * d + j * hs, hs), :] = big[zz * hs : (zz + 1) * hs, :]
    for u in range(ff_units, units):
        rs_core(u).start()
    out_own.wait()

    nsm = g.wbits + g.zbits
    segs = 7

    last = units - ff_units
    lead = 3

    def step2_unit(s, fn):
        when(s == 0, lambda: fn(pairs))
        when((s >= lead) & (s < lead + last), lambda: fn(ff_units - lead + s))

    def service_in(s):
        when(s < last, lambda: step1a(ff_units + s))
        step2_unit(s, step2a)
        when(s < units, lambda: step3a(s))
        when(s < units - 2, lambda: pg_step(s + 2))

    def service_out(s):
        @pl.when(s < last)
        def _():
            step1b(ff_units + s)
            step1c(ff_units + s)

        step2_unit(s, step2b)
        when(s < units, lambda: step3b(s))
        when((s >= 3) & (s < units + 3), lambda: step_z(s - 3))
        for i in range(nsm):
            when(s == 3 * i, lambda: sm_copy(i).start())
            when(s == 3 * i + 2, lambda: sm_finish(i))
        for p, at in ((1, ff_units + 2), (2, ff_units + 3), (0, units + 3)):
            when(s == at, lambda: step4(p))
            when(s == at + 1, lambda: step5(p))
            when(s == at + 2, lambda: step6(p))

    def rest(s, carry):
        clip = (z + 1 + s // segs) % nz
        seg = s % segs
        service_in(s)

        @pl.when(seg == 0)
        def _():
            patches_copy(clip).start()
            patches_copy(clip).wait()
            first_norm(clip, False)
            project()

        pl.when(seg == 1)(lambda: attend_range(0, pairs // 2))

        @pl.when(seg == 2)
        def _():
            attend_range(pairs // 2, pairs)
            second_norm(False)

        pl.when(seg >= 3)(lambda: feed(seg - 3, False))
        pl.when(seg == segs - 1)(lambda: write_out(clip))
        service_out(s)
        return carry

    lax.fori_loop(0, segs * (nz - 1), rest, 0)
    so_copy = pltpu.make_async_copy(sm, small_out, ls.at[9])
    so_copy.start()

    for cp in zb_copies:
        cp.wait_send()
    for zz in range(nz):
        for q in range(g.chunks):
            pl.when((zz != z) & jnp.logical_not(mid))(lambda: pg_copy(zz, q, True).wait_recv())
            pl.when((zz <= z) & has_up)(lambda: pg_copy(zz, q, True).wait_send())
            pl.when((zz >= z) & has_dn)(lambda: pg_copy(zz, q, False).wait_send())
        for p in range(3):
            for i in range(2):
                pl.when((zz <= z) & has_up)(lambda: agz(p, zz, True)[i].wait_send())
                pl.when((zz >= z) & has_dn)(lambda: agz(p, zz, False)[i].wait_send())
    for p in range(3):
        fin_c(p).wait()
        for cp in fin_xy(p) + fin_d(p):
            cp.wait_send()
    for n in range(agu):
        for cp in ag_xy(n) + ag_d(n) + (ag_c(n),):
            cp.wait_send()
    for n in range(units):
        for cp in rs_d(n) + rs_p(n):
            cp.wait_send()
        if ru_pk(n)[1] > 0:
            zz, up, dn = zdir(n)
            pl.when(up)(lambda: rs_z(n, zz, True).wait_send())
            pl.when(dn)(lambda: rs_z(n, zz, False).wait_send())
    for u in range(ff_units, units):
        rs_core(u).wait_send()
    so_copy.wait()


def closing_kernel(nz, hs, out_in, pg, ga, gb, gc, small, out, patch_grad, qkv_g, out_g, up_g, down_g, qv, up_b, *vectors):
    i = pl.program_id(0)
    out[...] = out_in[...]
    patch_grad[...] = pg[...].astype(bf16)
    up_g[...] = gb[...]
    down_g[...] = gc[...]
    for j in range(3):
        @pl.when(i == j)
        def _():
            qkv_g[j] = ga[j * hs : (j + 1) * hs, :].T

    @pl.when(i == 3)
    def _():
        out_g[...] = ga[3 * hs : 4 * hs, :]
        z = lax.axis_index("narrow")
        for zz in range(nz):
            @pl.when(z == zz)
            def _():
                qv[...] = small[7:9, zz * hs : (zz + 1) * hs]
                up_b[...] = small[9 + zz : 10 + zz, :]

        for k, ref in enumerate(vectors):
            ref[...] = small[k : k + 1, :]


def make(mesh):
    def on_device(
        patches, mask_index, mask_count, mask_embed, norm1_gain, norm1_bias, w_qkv, b_qv, w_out, b_out,
        norm2_gain, norm2_bias, w_up, b_up, w_down, b_down, cotangent,
    ):
        rows, d = patches.shape
        nz = mesh.shape["narrow"]
        t, hs, fs = rows // nz, w_qkv.shape[2], w_up.shape[1]
        assert t == PATCHES and fs == d and 4 * hs == d
        g = make_cfg(mesh, d, t, hs)
        pr = g.pr
        w, z = lax.axis_index("wide"), lax.axis_index("narrow")
        c, x, y = w % 2, (w // 2) % 2, (w // 4) % 2
        pos, pos_d = c * 4 + y * 2 + x, c * 4 + (1 - y) * 2 + 1 - x
        first_piece = jnp.concatenate([jnp.swapaxes(w_qkv, 1, 2).reshape(3 * hs, d), w_out])
        shares = []
        for a in (first_piece, w_up, w_down):
            shares += [lax.dynamic_slice_in_dim(a, pos * pr, pr, 0), lax.dynamic_slice_in_dim(a, pos_d * pr, g.xr, 0)]
        part = jnp.concatenate(shares).astype(f32)
        zb = jnp.zeros((8, d), f32).at[0].set(b_up)
        zb = lax.dynamic_update_slice(zb, b_qv, (1, z * hs))
        slots = jnp.arange(mask_index.shape[1], dtype=jnp.int32)
        midx = jnp.where(slots[None, :] < mask_count[:, None], mask_index, -1)
        vecs = jnp.concatenate(
            [mask_embed, norm1_gain, norm1_bias, b_out, norm2_gain, norm2_bias, b_down, b_down]
        ).reshape(8, d)
        hbm = pl.BlockSpec(memory_space=pl.ANY)
        vm = pl.BlockSpec(memory_space=pltpu.VMEM)
        u = g.units

        def o(r, dt=f32):
            return jax.ShapeDtypeStruct((r, d), dt)

        out_shape = (
            o(rows, bf16), o(rows), o(d), o(d), o(d), o(16),
            o(u * d), o(u * 4 * pr), o(u * pr // 2), o(u * pr // 2), o(u * pr), o(u * pr), o(2 * u * pr), o(3 * g.groups * pr),
        )
        v = pltpu.VMEM
        scratch = [
            v((3, d, d), bf16), v((d, d), bf16), v((2 * nz, d, d), bf16),
            v((t, d), f32), v((t, d), f32), v((t, d), f32), v((t, d), bf16), v((3, t, d), bf16),
            v((t, d), bf16), v((t, d), bf16), v((t, d), bf16), v((t, d), f32), v((t, d), bf16), v((t, d), f32),
            v((t, d), f32), v((t, d), bf16), v((3, t, d), bf16), v((t, 1), f32), v((t, 1), f32), v((t, 1), f32),
            v((4 * d + 2 * nz * 4 * pr, d), f32), v((d, d), f32), v((4 * pr, d), f32), v((pr, d), f32), v((2 * pr, d), f32),
            v((2 * pr, d), f32), v((nz * 8, d), f32), v((16, d), f32), v(((g.wbits + g.zbits) * 16, d), f32),
            v((3 * pr, d), f32),
            pltpu.SemaphoreType.DMA((g.nsem,)), pltpu.SemaphoreType.DMA((g.nsem,)), pltpu.SemaphoreType.DMA((20,)),
        ]
        outs = pl.pallas_call(
            functools.partial(layer_kernel, g),
            out_shape=out_shape,
            in_specs=[vm, hbm, hbm, hbm, vm, vm, vm, hbm, hbm],
            out_specs=[hbm] * len(out_shape),
            scratch_shapes=scratch,
            compiler_params=pltpu.CompilerParams(
                collective_id=1, has_side_effects=True, vmem_limit_bytes=64 * 2**20 - 2**17
            ),
            name="layer",
        )(
            part, first_piece, w_up, w_down, zb, midx, vecs, patches, cotangent,
        )
        steps = 8

        def cut(r):
            return pl.BlockSpec((r // steps, d), lambda i: (i, 0))

        def whole(*shape):
            return pl.BlockSpec(shape, lambda i: (0,) * len(shape))

        closed = pl.pallas_call(
            functools.partial(closing_kernel, nz, hs),
            grid=(steps,),
            out_shape=(
                o(rows, bf16), o(rows, bf16), jax.ShapeDtypeStruct((3, d, hs), f32), o(hs), o(d), o(d),
                jax.ShapeDtypeStruct((2, hs), f32), o(1),
            ) + (o(1),) * 7,
            in_specs=[cut(rows), cut(rows), whole(d, d), cut(d), cut(d), whole(16, d)],
            out_specs=(
                cut(rows), cut(rows), whole(3, d, hs), whole(hs, d), cut(d), cut(d), whole(2, hs), whole(1, d),
            ) + (whole(1, d),) * 7,
            compiler_params=pltpu.CompilerParams(vmem_limit_bytes=64 * 2**20 - 2**17),
            name="closing",
        )(*outs[:6])
        output, patch_grad, qkv_o, out_o, up_o, down_o, qvb, upb = closed[:8]
        small = [a.reshape(d) for a in closed[8:]]
        return (
            output, patch_grad, small[0], small[1], small[2], qkv_o, qvb, out_o, small[3],
            small[4], small[5], up_o, upb.reshape(d), down_o, small[6],
        )

    return on_device


def solution(mesh):
    return jax.shard_map(
        make(mesh),
        mesh=mesh,
        in_specs=(
            P("wide", None), P("wide", None), P("wide"), P(), P(), P(), P(None, None, "narrow"), P(None, "narrow"),
            P("narrow", None), P(), P(), P(), P(None, "narrow"), P("narrow"), P("narrow", None), P(), P("wide", None),
        ),
        out_specs=(
            P("wide", None), P("wide", None), P(), P(), P(), P(None, None, "narrow"), P(None, "narrow"),
            P("narrow", None), P(), P(), P(), P(None, "narrow"), P("narrow"), P("narrow", None), P(),
        ),
        check_vma=False,
    )
```

```python
import functools
import math

import jax
import jax.numpy as jnp
from jax import lax
from jax.experimental import pallas as pl
from jax.experimental.pallas import tpu as pltpu
from jax.sharding import PartitionSpec as P

HD = 64
PATCHES = 512
EPS = 1e-06
f32 = jnp.float32
bf16 = jnp.bfloat16
MESH = pl.DeviceIdType.MESH
RT = 128


def nn(a, b):
    return lax.dot_general(a, b, (((1,), (0,)), ((), ())), preferred_element_type=f32)


def nt(a, b):
    return lax.dot_general(a, b, (((1,), (1,)), ((), ())), preferred_element_type=f32)


def tn(a, b):
    return lax.dot_general(a, b, (((0,), (0,)), ((), ())), preferred_element_type=f32)


def rds(start, size, unit=8):
    if isinstance(start, int):
        return pl.ds(start, size)
    return pl.ds(pl.multiple_of(start, unit), size)


def normalise(v):
    centred = v - jnp.mean(v, axis=-1, keepdims=True)
    inverse = lax.rsqrt(jnp.mean(centred * centred, axis=-1, keepdims=True) + EPS)
    return centred * inverse, inverse


def norm_back(upstream, xhat, inverse, gain):
    weighted = upstream * gain
    return inverse * (
        weighted
        - jnp.mean(weighted, axis=-1, keepdims=True)
        - xhat * jnp.mean(weighted * xhat, axis=-1, keepdims=True)
    )


def softmax_t(scores):
    e = jnp.exp(scores - jnp.max(scores, axis=0, keepdims=True))
    return e * (1.0 / jnp.sum(e, axis=0, keepdims=True))


class Cfg:
    pass


def make_cfg(mesh, d, t, hs):
    g = Cfg()
    g.nw, g.nz = mesh.shape["wide"], mesh.shape["narrow"]
    assert g.nz == 4
    g.groups = g.nw // 8
    g.d, g.t, g.hs = d, t, hs
    g.pr = d // 8
    g.units = 3 * g.nz
    g.agu = 3 * (g.nz - 1)
    g.xr = g.pr // 3
    g.wbits = g.nw.bit_length() - 1
    g.zbits = g.nz.bit_length() - 1
    g.chunks = 4
    n = 0
    for name, count in (
        ("agz", 6 * g.nz), ("age", 6 * g.nz), ("agx", g.agu), ("agy", g.agu), ("agdx", g.agu), ("agdy", g.agu), ("agc", g.agu),
        ("rc", g.units), ("rdx", g.units), ("rdy", g.units), ("rpx", g.units), ("rpy", g.units), ("rz", 6 * g.nz),
        ("fx", 3), ("fy", 3), ("fdx", 3), ("fdy", 3), ("fc", 3), ("zb", g.nz), ("pg", 2 * g.nz * g.chunks),
        ("sm", g.wbits + g.zbits), ("fg", 3 * g.groups),
    ):
        setattr(g, name, n)
        n += count
    g.nsem = n
    return g


def when(cond, fn):
    if isinstance(cond, bool):
        if cond:
            fn()
    else:
        pl.when(cond)(fn)


def layer_kernel(
    g,
    qkv_t, w_out, w_up, w_down, b_up, b_qv, mask_index, mask_count, embed_ref, gain1_ref, bias1_ref, b_out_ref, gain2_ref,
    bias2_ref, b_down_ref, patches, cot_hbm,
    out, pg, ga, gb, gc, small_out, wbuf, crecv, dxr, dyr, pxr, pyr, zr, grecv,
    wq, wo, ffw, res, xh1, xh2, normed, qkv, ctx, hid, act, slope, cotv, acc, hg, bg, dqkv, r1, r2, mown, rsb, cst, rst,
    zst, part, pbf, zb, zball, sm, smr, fin, ss, rs, ls,
):
    nz, d, t, hs, pr, units = g.nz, g.d, g.t, g.hs, g.pr, g.units
    half = pr // 2
    ff_units = 2 * nz
    w = lax.axis_index("wide")
    z = lax.axis_index("narrow")
    c, x, y = w % 2, (w // 2) % 2, (w // 4) % 2
    sib, xn, yn = {"wide": w + 1 - 2 * c}, {"wide": w + 2 - 4 * x}, {"wide": w + 4 - 8 * y}
    zup, zdn = {"narrow": z + 1}, {"narrow": z - 1}
    has_up, has_dn = z < nz - 1, z > 0
    mid = (z > 0) & (z < nz - 1)
    yx, yx_x, yx_y, yx_d = y * 2 + x, y * 2 + 1 - x, (1 - y) * 2 + x, (1 - y) * 2 + 1 - x
    pos, pos_x, pos_y, pos_d = c * 4 + yx, c * 4 + yx_x, c * 4 + yx_y, c * 4 + yx_d
    zp = [None] + [{"narrow": (z + k) % nz} for k in range(1, nz)]
    gp = [None] + [{"wide": (w + 8 * k) % g.nw} for k in range(1, g.groups)]
    gouts = (ga, gb, gc)

    zside = z // 2
    zend = z + zside * (nz - 1 - 2 * z)

    def swap01(k):
        return k + zend * (1 - k // 2) * (1 - 2 * (k % 2))

    def zk(k):
        b = swap01(k)
        return b + zside * (nz - 1 - 2 * b)

    def zk_inv(zz):
        return swap01(zz + zside * (nz - 1 - 2 * zz))

    def rcopy(src, dst, si, ri, dev):
        return pltpu.make_async_remote_copy(src, dst, ss.at[si], rs.at[ri], device_id=dev, device_id_type=MESH)

    barrier = pltpu.get_barrier_semaphore()
    partners = [sib, xn, yn] + zp[1:] + gp[1:]
    for p in partners:
        pl.semaphore_signal(barrier, inc=1, device_id=p, device_id_type=MESH)

    def wrow(p, zz, q):
        return (p * nz + zz) * d + q * pr

    xr = g.xr
    hr = (pr - xr) // 2
    agu = g.agu

    def ag_pk(n):
        if isinstance(n, int) and n < nz - 1:
            return 0, n + 1
        m = n - (nz - 1)
        return 1 + m % 2, 1 + m // 2

    def own_loads():
        cps = [(qkv_t.at[pl.ds(j * hs, hs)], wq.at[j, rds(z * hs, hs, 16)]) for j in range(3)]
        cps += [(w_out, wo.at[rds(z * hs, hs, 16)]), (w_up, ffw.at[0]), (w_down, ffw.at[1])]
        return [pltpu.make_async_copy(src, dst, ls.at[i]) for i, (src, dst) in enumerate(cps)]

    def ag_block(n, q, lo, size):
        p, k = ag_pk(n)
        return wbuf.at[rds(wrow(p, zk(k), q) + lo, size)]

    def ag_xy(n):
        b = ag_block(n, pos, 0, pr)
        return rcopy(b, b, g.agx + n, g.agx + n, xn), rcopy(b, b, g.agy + n, g.agy + n, yn)

    def ag_d(n):
        bx, by = ag_block(n, pos_x, xr, hr), ag_block(n, pos_y, xr + hr, hr)
        return rcopy(bx, bx, g.agdy + n, g.agdy + n, yn), rcopy(by, by, g.agdx + n, g.agdx + n, xn)

    def ag_c(n):
        b = ag_block(n, c * 4, 0, 4 * pr)
        return rcopy(b, b, g.agc + n, g.agc + n, sib)

    def agz(p, zz, up, own=False):
        pair = []
        for sem, q, lo, size in ((g.agz, pos, 0, pr), (g.age, pos_d, pr, xr)):
            to = wbuf.at[rds(wrow(p, zz, q), size)]
            src = part.at[pl.ds(p * (pr + xr) + lo, size)] if own else to
            ri = sem + p * nz + zz
            pair.append(rcopy(src, to, ri + (0 if up else 3 * nz), ri, zup if up else zdn))
        return pair

    def start(cps):
        for cp in cps:
            cp.start()

    def agz_own(p):
        pl.when(has_up)(lambda: start(agz(p, z, True, True)))
        pl.when(has_dn)(lambda: start(agz(p, z, False, True)))

    def ag_z(n):
        p, k = ag_pk(n)
        zz = zk(k)

        @pl.when(mid)
        def _():
            for i, cp in enumerate(agz(p, zz, True)):
                cp.wait_recv()
                pl.when(zz < z)(lambda: agz(p, zz, True)[i].start())
                pl.when(zz > z)(lambda: agz(p, zz, False)[i].start())

    def ag_s1(n):
        p, k = ag_pk(n)
        pl.when(jnp.logical_not(mid))(lambda: agz(p, zk(k), True)[0].wait_recv())
        start(ag_xy(n))

    def ag_s2(n):
        cx, cy = ag_xy(n)
        dy, dx = ag_d(n)
        cx.wait_recv()
        dy.start()
        cy.wait_recv()
        dx.start()

    def ag_s3(n):
        p, k = ag_pk(n)
        pl.when(jnp.logical_not(mid))(lambda: agz(p, zk(k), True)[1].wait_recv())
        dy, dx = ag_d(n)
        dy.wait_recv()
        dx.wait_recv()
        ag_c(n).start()

    def ag_load(n):
        p, k = ag_pk(n)
        return [
            pltpu.make_async_copy(
                wbuf.at[rds(wrow(p, zk(k), 4 * i), 4 * pr)], cst.at[pl.ds(i * 4 * pr, 4 * pr)], ls.at[10 + i]
            )
            for i in range(2)
        ]

    def ag_conv_start(n):
        ag_c(n).wait_recv()
        start(ag_load(n))

    def ag_conv(n):
        for cp in ag_load(n):
            cp.wait()
        p, k = ag_pk(n)
        if isinstance(n, int) and n < nz - 1:
            zz = zk(k)
            for j in range(3):
                wq[j, rds(zz * hs, hs, 16), :] = cst[j * hs : (j + 1) * hs, :].astype(bf16)
            wo[rds(zz * hs, hs, 16), :] = cst[3 * hs : 4 * hs, :].astype(bf16)
        else:
            ffw[2 * k + p - 1] = cst[...].astype(bf16)

    def ag_step(n):
        static = isinstance(n, int)
        when(n < agu, lambda: ag_s2(n))
        if static:
            when(n + 2 < agu, lambda: ag_s1(n + 2))
            when(n + 3 < agu, lambda: ag_z(n + 3))
        when(n - 1 >= 0, lambda: when(n - 1 < agu, lambda: ag_s3(n - 1)))
        if not static or (n >= 2 and n != nz):
            when(n - 2 < agu, lambda: ag_conv(n - 2))
        if not static or n >= 1:
            when(n - 1 < agu, lambda: ag_conv_start(n - 1))
        if static and n == nz - 1:
            ag_conv(n - 1)

    def ru_pk(u):
        if isinstance(u, int):
            return (2 - (ff_units - 1 - u) % 2, (ff_units - 1 - u) // 2) if u < ff_units else (0, units - 1 - u)
        late = u // ff_units
        return (
            (1 - late) * (2 - (2 * ff_units - 1 - u) % 2),
            (1 - late) * ((ff_units - 1 - u + late * ff_units) // 2) + late * (units - 1 - u),
        )

    def slot_row(u):
        return ((2 * ff_units - 1 - u) % 4) * d

    def sum_row(u, q):
        if isinstance(u, int):
            base = 4 * d + u * 4 * pr if u < ff_units else slot_row(u) + c * 4 * pr
        else:
            late = u // ff_units
            base = (1 - late) * (4 * d + u * 4 * pr) + late * (slot_row(u) + c * 4 * pr)
        return base + q * pr

    def rs_core(u):
        return rcopy(
            rsb.at[rds(slot_row(u) + (1 - c) * 4 * pr, 4 * pr)], crecv.at[rds(u * 4 * pr, 4 * pr)], g.rc + u, g.rc + u, sib
        )

    def rs_d(u):
        a = rcopy(rsb.at[rds(sum_row(u, yx_d), half)], dxr.at[rds(u * half, half)], g.rdx + u, g.rdx + u, xn)
        b = rcopy(rsb.at[rds(sum_row(u, yx_d) + half, half)], dyr.at[rds(u * half, half)], g.rdy + u, g.rdy + u, yn)
        return a, b

    def rs_p(u):
        a = rcopy(rsb.at[rds(sum_row(u, yx_x), pr)], pxr.at[rds(u * pr, pr)], g.rpx + u, g.rpx + u, xn)
        b = rcopy(rsb.at[rds(sum_row(u, yx_y), pr)], pyr.at[rds(u * pr, pr)], g.rpy + u, g.rpy + u, yn)
        return a, b

    def rs_z(u, zz, up):
        p, _ = ru_pk(u)
        i = (p * nz + zz) * 2 + (0 if up else 1)
        return rcopy(rsb.at[rds(sum_row(u, yx), pr)], zr.at[rds(i * pr, pr)], g.rz + i, g.rz + i, zup if up else zdn)

    def rs_z_load(p, zz, up, slot):
        i = (p * nz + zz) * 2 + (0 if up else 1)
        src = zr.at[rds(i * pr, pr)]
        return (
            rcopy(src, src, g.rz + i, g.rz + i, sib),
            pltpu.make_async_copy(src, zst.at[pl.ds(slot * pr, pr)], ls.at[18 + slot]),
        )

    def l1(u):
        return pltpu.make_async_copy(crecv.at[rds(u * 4 * pr, 4 * pr)], rst, ls.at[12])

    def step1a(u):
        rs_core(u).wait_recv()
        l1(u).start()

    def step1b(u):
        l1(u).wait()
        src = slot_row(u) + c * 4 * pr
        rsb[rds(sum_row(u, 0), 4 * pr), :] = rsb[rds(src, 4 * pr), :] + rst[...]

    def step1c(u):
        start(rs_d(u))

    def step1(us):
        cps = [
            pltpu.make_async_copy(crecv.at[rds(u * 4 * pr, 4 * pr)], cst.at[pl.ds(i * 4 * pr, 4 * pr)], ls.at[36 + i])
            for i, u in enumerate(us)
        ]
        for u, cp in zip(us, cps):
            rs_core(u).wait_recv()
            cp.start()
        for i, (u, cp) in enumerate(zip(us, cps)):
            cp.wait()
            rsb[rds(sum_row(u, 0), 4 * pr), :] = (
                rsb[rds(slot_row(u) + c * 4 * pr, 4 * pr), :] + cst[i * 4 * pr : (i + 1) * 4 * pr, :]
            )
            step1c(u)

    def l2(u, i):
        return (
            pltpu.make_async_copy(dxr.at[rds(u * half, half)], rst.at[pl.ds(i * pr, half)], ls.at[20 + 2 * i]),
            pltpu.make_async_copy(dyr.at[rds(u * half, half)], rst.at[pl.ds(i * pr + half, half)], ls.at[21 + 2 * i]),
        )

    def step2_in(us):
        for i, u in enumerate(us):
            for cp, ld in zip(rs_d(u), l2(u, i)):
                cp.wait_recv()
                ld.start()

    def step2_out(us):
        for i, u in enumerate(us):
            for ld in l2(u, i):
                ld.wait()
            rsb[rds(sum_row(u, yx_y), half), :] += rst[i * pr : i * pr + half, :]
            rsb[rds(sum_row(u, yx_x) + half, half), :] += rst[i * pr + half : (i + 1) * pr, :]
            start(rs_p(u))

    def l3(u, i):
        return (
            pltpu.make_async_copy(pxr.at[rds(u * pr, pr)], cst.at[pl.ds(2 * i * pr, pr)], ls.at[28 + 2 * i]),
            pltpu.make_async_copy(pyr.at[rds(u * pr, pr)], cst.at[pl.ds((2 * i + 1) * pr, pr)], ls.at[29 + 2 * i]),
        )

    def zdir(u):
        _, k = ru_pk(u)
        zz = zk(k)
        return zz, zz > z, zz < z

    def step3_in(us):
        for i, u in enumerate(us):
            for cp, ld in zip(rs_p(u), l3(u, i)):
                cp.wait_recv()
                ld.start()

    def step3_out(us):
        for i, u in enumerate(us):
            for ld in l3(u, i):
                ld.wait()
            rsb[rds(sum_row(u, yx), pr), :] += (
                cst[2 * i * pr : (2 * i + 1) * pr, :] + cst[(2 * i + 1) * pr : (2 * i + 2) * pr, :]
            )
            if ru_pk(u)[1] > 0:
                zz, up, dn = zdir(u)
                pl.when(up & (z == 0))(lambda: rs_z(u, zz, True).start())
                pl.when(dn & (z == nz - 1))(lambda: rs_z(u, zz, False).start())

    def step_z(u):
        p, _ = ru_pk(u)
        zz, up, dn = zdir(u)
        for cond, flag in ((up, True), (dn, False)):
            @pl.when(cond & mid)
            def _():
                got, ld = rs_z_load(p, zz, flag, 0)
                got.wait_recv()
                ld.start()
                ld.wait()
                rsb[rds(sum_row(u, yx), pr), :] += zst[0:pr, :]
                rs_z(u, zz, flag).start()

    own_unit = {0: units - 1, 1: ff_units - 2, 2: ff_units - 1}

    def fin_xy(p):
        src = fin.at[pl.ds(p * pr, pr)]
        to = gouts[p].at[rds(pos * pr, pr)]
        return rcopy(src, to, g.fx + p, g.fx + p, xn), rcopy(src, to, g.fy + p, g.fy + p, yn)

    def fin_own(p):
        return pltpu.make_async_copy(fin.at[pl.ds(p * pr, pr)], gouts[p].at[rds(pos * pr, pr)], ls.at[5 + p])

    def fin_d(p):
        bx, by = gouts[p].at[rds(pos_x * pr, half)], gouts[p].at[rds(pos_y * pr + half, half)]
        return rcopy(bx, bx, g.fdy + p, g.fdy + p, yn), rcopy(by, by, g.fdx + p, g.fdx + p, xn)

    def fin_c(p):
        b = gouts[p].at[rds(c * 4 * pr, 4 * pr)]
        return rcopy(b, b, g.fc + p, g.fc + p, sib)

    def fin_g(p, k):
        return rcopy(
            fin.at[pl.ds(p * pr, pr)], grecv.at[pl.ds((p * g.groups + g.groups - k) * pr, pr)],
            g.fg + p * g.groups + k, g.fg + p * g.groups + g.groups - k, gp[k],
        )

    def step4(p):
        sl = slice(p * pr, (p + 1) * pr)
        fin[sl, :] = rsb[rds(sum_row(own_unit[p], yx), pr), :]
        ins = ((has_dn, True, 0), (has_up, False, 1))
        for cond, flag, slot in ins:
            @pl.when(cond)
            def _():
                got, ld = rs_z_load(p, z, flag, slot)
                got.wait_recv()
                ld.start()

        for cond, flag, slot in ins:
            @pl.when(cond)
            def _():
                rs_z_load(p, z, flag, slot)[1].wait()
                fin[sl, :] += zst[slot * pr : (slot + 1) * pr, :]

        if g.groups > 1:
            total = fin[sl, :]
            for k in range(1, g.groups):
                fin_g(p, k).start()
            for k in range(1, g.groups):
                fin_g(p, k).wait()
            for k in range(1, g.groups):
                src = grecv.at[pl.ds((p * g.groups + k) * pr, pr)]
                cp = pltpu.make_async_copy(src, zst.at[pl.ds(0, pr)], ls.at[3])
                cp.start()
                cp.wait()
                total = total + zst[0:pr, :]
            fin[sl, :] = total
        fin_own(p).start()
        for cp in fin_xy(p):
            cp.start()

    def step5(p):
        cx, cy = fin_xy(p)
        dy, dx = fin_d(p)
        cx.wait_recv()
        dy.start()
        cy.wait_recv()
        dx.start()

    def step6(p):
        dy, dx = fin_d(p)
        dy.wait_recv()
        dx.wait_recv()
        fin_own(p).wait()
        fin_c(p).start()

    def sm_copy(i):
        if i < g.wbits:
            b = 1 << i
            dev = {"wide": w + b - 2 * b * ((w // b) % 2)}
        else:
            b = 1 << (i - g.wbits)
            dev = {"narrow": z + b - 2 * b * ((z // b) % 2)}
        return rcopy(sm, smr.at[pl.ds(16 * i, 16)], g.sm + i, g.sm + i, dev)

    def sm_finish(i):
        sm_copy(i).wait()
        sm[...] += smr[16 * i : 16 * (i + 1), :]

    ck = t // g.chunks

    def pg_copy(zz, q, up):
        to = pg.at[rds(zz * t + q * ck, ck)]
        ri = g.pg + zz * g.chunks + q
        return rcopy(to, to, ri + (0 if up else nz * g.chunks), ri, zup if up else zdn)

    def pg_send(zz, q, up):
        pg_copy(zz, q, up).start()

    def pg_step(s):
        if s < g.chunks:
            pl.when(has_up)(lambda: pg_send(z, s, True))
            pl.when(has_dn)(lambda: pg_send(z, s, False))
            return
        j = s - g.chunks
        for up, zz, count, more in (
            (True, z - 1 - j // g.chunks, g.chunks * z, has_up),
            (False, z + 1 + j // g.chunks, g.chunks * (nz - 1 - z), has_dn),
        ):
            @pl.when((j < count) & more)
            def _():
                pg_copy(zz, j % g.chunks, up).wait_recv()
                pg_send(zz, j % g.chunks, up)

    embed, gain1, bias1, b_out, gain2, bias2, b_down = [
        ref[...].reshape(1, d)
        for ref in (embed_ref, gain1_ref, bias1_ref, b_out_ref, gain2_ref, bias2_ref, b_down_ref)
    ]

    def tiles(fn):
        def body(i, carry):
            fn(rds(i * RT, RT, RT), i * RT)
            return carry

        lax.fori_loop(0, t // RT, body, 0)

    def patches_copy(clip):
        return pltpu.make_async_copy(patches.at[rds(clip * t, t, 16)], bg, ls.at[8])

    def first_norm(clip, keep):
        slots = lax.broadcasted_iota(jnp.int32, (1, mask_index.shape[1]), 1)
        listed = jnp.where(slots < mask_count[clip], mask_index[pl.ds(clip, 1), :], -1)

        def fn(sl, at):
            place = lax.broadcasted_iota(jnp.int32, (RT, listed.shape[1]), 0) + at
            m = jnp.max(jnp.where(listed == place, 1.0, 0.0), axis=1, keepdims=True)
            v = jnp.where(m > 0.5, embed, bg[sl, :].astype(f32))
            res[sl, :] = v
            xhat, inverse = normalise(v)
            if keep:
                mown[sl, :] = m
                xh1[sl, :] = xhat
                r1[sl, :] = inverse
            normed[sl, :] = (xhat * gain1 + bias1).astype(bf16)

        tiles(fn)

    def project():
        biases = []
        for i in (1, 2):
            total = zball[i : i + 1, :]
            for k in range(1, nz):
                total = total + zball[8 * k + i : 8 * k + i + 1, :]
            biases.append(total)
        n = normed[...]
        qkv[0] = ((nt(n, wq[0]) + biases[0]).astype(bf16) * bf16(HD**-0.5)).astype(bf16)
        qkv[1] = nt(n, wq[1]).astype(bf16)
        qkv[2] = (nt(n, wq[2]) + biases[1]).astype(bf16)

    def head_masks():
        lane = lax.broadcasted_iota(jnp.int32, (1, 2 * HD), 1)
        first = (lane < HD).astype(f32)
        return first.astype(bf16), (1.0 - first).astype(bf16)

    def attend(i):
        sl = rds(i * 2 * HD, 2 * HD, 2 * HD)
        qp, kp, vp = qkv[0, :, sl], qkv[1, :, sl], qkv[2, :, sl]
        vt = vp.T
        outs = []
        for h, hm in enumerate(head_masks()):
            probs = softmax_t(nt(kp * hm, qp)).astype(bf16)
            outs.append(nn(vt[h * HD : (h + 1) * HD, :], probs))
        ctx[:, sl] = jnp.concatenate(outs, axis=0).T.astype(bf16)

    def attend_range(lo, hi):
        def body(i, carry):
            attend(i)
            return carry

        lax.fori_loop(lo, hi, body, 0)

    def second_norm(keep):
        acc[...] = nn(ctx[...], wo[...])

        def fn(sl, at):
            v = res[sl, :] + acc[sl, :] + b_out
            res[sl, :] = v
            xhat, inverse = normalise(v)
            if keep:
                xh2[sl, :] = xhat
                r2[sl, :] = inverse
            hid[sl, :] = (xhat * gain2 + bias2).astype(bf16)
            acc[sl, :] = jnp.zeros((RT, d), f32)

        tiles(fn)

    def feed(k, keep):
        bias = zball[rds(zk(k) * 8, 8), :][0:1, :]
        slope[...] = nn(hid[...], ffw[2 * k])

        def fn(sl, at):
            v = slope[sl, :] + bias
            cdf = 0.5 * (1.0 + lax.erf(v * (0.5**0.5)))
            act[sl, :] = (v * cdf).astype(bf16)
            if keep:
                slope[sl, :] = cdf + v * jnp.exp(-0.5 * v * v) * ((0.5 / math.pi) ** 0.5)

        tiles(fn)
        acc[...] += nn(act[...], ffw[2 * k + 1])

    def write_out(clip):
        def fn(sl, at):
            act[sl, :] = (res[sl, :] + acc[sl, :] + b_down).astype(bf16)

        tiles(fn)
        cp = pltpu.make_async_copy(act, out.at[rds(clip * t, t, 16)], ls.at[8])
        cp.start()
        cp.wait()

    def feed_back(k):
        acc2 = nt(cotv[...], ffw[2 * k + 1])
        b = (acc2 * slope[...]).astype(bf16)
        bg[...] = b
        sm[pl.ds(9 + zk(k), 1), :] = jnp.sum(b.astype(f32), axis=0, keepdims=True)
        part_sum = nt(bg[...], ffw[2 * k])

        @pl.when(k == 0)
        def _():
            hg[...] = part_sum

        @pl.when(k > 0)
        def _():
            hg[...] += part_sum

    sm[...] = jnp.zeros((16, d), f32)
    cot_copy = pltpu.make_async_copy(cot_hbm.at[rds(z * t, t, 16)], cotv, ls.at[9])
    shares = []
    first_rows = 3 * hs // pr
    for p, src in enumerate((qkv_t, w_up, w_down)):
        for q, lo, size in ((pos, 0, pr), (pos_d, pr, xr)):
            i = len(shares)
            to = pbf.at[pl.ds(p * (pr + xr) + lo, size)]

            def share(ref, row):
                return pltpu.make_async_copy(ref.at[rds(row, size, 16)], to, ls.at[20 + i])

            if p == 0:
                pl.when(q < first_rows)(lambda: share(qkv_t, q * pr).start())
                pl.when(q >= first_rows)(lambda: share(w_out, (q - first_rows) * pr).start())
                shares.append(share(w_out, 0))
            else:
                shares.append(share(src, q * pr))
                shares[-1].start()
    patches_copy(z).start()
    own = own_loads()
    start(own)
    cot_copy.start()
    zb[...] = jnp.zeros((8, d), f32)
    zb[0:1, :] = b_up[...].reshape(1, d)
    for zz in range(nz):
        @pl.when(z == zz)
        def _():
            zb[1:3, zz * hs : (zz + 1) * hs] = b_qv[...]

    zball[rds(z * 8, 8), :] = zb[...]
    for cp in shares:
        cp.wait()
    part[...] = pbf[...].astype(f32)
    pl.semaphore_wait(barrier, len(partners))
    agz_own(0)
    zb_copies = [
        rcopy(zb, zball.at[rds(z * 8, 8)], g.zb + k, g.zb + nz - k, zp[k]) for k in range(1, nz)
    ]
    start(zb_copies)
    patches_copy(z).wait()
    first_norm(z, True)
    ag_z(0)
    ag_s1(0)
    ag_z(1)
    pl.when(mid)(lambda: ag_s1(1))
    ag_z(2)
    agz_own(1)
    agz_own(2)
    ag_s2(0)
    pl.when(jnp.logical_not(mid))(lambda: ag_s1(1))
    ag_s1(2)
    ag_z(3)
    for n in range(1, nz):
        ag_step(n)
    for cp in own:
        cp.wait()
    for k in range(1, nz):
        rcopy(zb, zball.at[rds(((z + k) % nz) * 8, 8)], g.zb + k, g.zb + k, zp[k]).wait_recv()
    pairs = nz * hs // (2 * HD)
    project()
    for i in range(3):
        ag_step(nz + i)
        attend_range(i * pairs // 3, (i + 1) * pairs // 3)
    second_norm(True)
    cot_copy.wait()

    def ff_body(k, carry):
        ud, uu = ff_units - 1 - 2 * k, ff_units - 2 - 2 * k
        ag_step(nz + 3 + k)

        @pl.when(k >= 2)
        def _():
            rs_core(ud + 4).wait_send()
            rs_core(uu + 4).wait_send()

        pl.when(k >= 1)(lambda: step1a(ud + 2))
        feed(k, True)
        rsb[rds(slot_row(ud), d), :] = tn(act[...], cotv[...])
        rs_core(ud).start()

        @pl.when(k >= 1)
        def _():
            step1b(ud + 2)
            step1c(ud + 2)
            step1a(uu + 2)

        feed_back(k)

        @pl.when(k >= 1)
        def _():
            step1b(uu + 2)
            step1c(uu + 2)

        rsb[rds(slot_row(uu), d), :] = tn(hid[...], bg[...])
        rs_core(uu).start()
        return carry

    lax.fori_loop(0, nz, ff_body, 0)
    step1((1, 0))
    step2_in((3, 2))

    none = jnp.zeros((1, d), f32)

    def mid_back(i, carry):
        sg, sb, so, sc = carry
        sl = rds(i * RT, RT, RT)
        up, xhat = hg[sl, :], xh2[sl, :]
        cf = cotv[sl, :].astype(f32)
        mg = cf + norm_back(up, xhat, r2[sl, :], gain2)
        v = res[sl, :] + acc[sl, :] + b_down
        hid[sl, :] = v.astype(bf16)
        res[sl, :] = mg
        act[sl, :] = mg.astype(bf16)
        return (
            sg + jnp.sum(up * xhat, axis=0, keepdims=True),
            sb + jnp.sum(up, axis=0, keepdims=True),
            so + jnp.sum(mg, axis=0, keepdims=True),
            sc + jnp.sum(cf, axis=0, keepdims=True),
        )

    sg, sb, so, sc = lax.fori_loop(0, t // RT, mid_back, (none, none, none, none))
    step2_out((3, 2))
    sm[3:4, :], sm[4:5, :], sm[5:6, :], sm[6:7, :] = so, sg, sb, sc
    out_own = pltpu.make_async_copy(hid, out.at[rds(z * t, t, 16)], ls.at[8])
    out_own.start()
    bg[...] = nt(act[...], wo[...]).astype(bf16)

    def att_back(i, carry):
        sl = rds(i * 2 * HD, 2 * HD, 2 * HD)
        qp, kp, vp, cg = qkv[0, :, sl], qkv[1, :, sl], qkv[2, :, sl], bg[:, sl]
        kt = kp.T
        masks = head_masks()
        dv = dk = None
        dq = []
        for h, hm in enumerate(masks):
            probs = softmax_t(nt(kp * hm, qp))
            dp = nt(vp * hm, cg)
            delta = jnp.sum(probs * dp, axis=0, keepdims=True)
            ds = (probs * (dp - delta)).astype(bf16)
            hf = hm.astype(f32)
            dv_h = nn(probs.astype(bf16), cg) * hf
            dk_h = nn(ds, qp) * hf
            dv = dv_h if dv is None else dv + dv_h
            dk = dk_h if dk is None else dk + dk_h
            dq.append(nn(kt[h * HD : (h + 1) * HD, :], ds))
        dqkv[0, :, sl] = (jnp.concatenate(dq, axis=0).T * (HD**-0.5)).astype(bf16)
        dqkv[1, :, sl] = dk.astype(bf16)
        dqkv[2, :, sl] = dv.astype(bf16)
        return carry

    lax.fori_loop(0, pairs, att_back, 0)
    acc[...] = nn(dqkv[0], wq[0]) + nn(dqkv[1], wq[1]) + nn(dqkv[2], wq[2])


    def first_back(i, carry):
        se, sg, sb = carry
        sl = rds(i * RT, RT, RT)
        up, xhat = acc[sl, :], xh1[sl, :]
        m = mown[sl, :] > 0.5
        rg = res[sl, :] + norm_back(up, xhat, r1[sl, :], gain1)
        hg[sl, :] = jnp.where(m, 0.0, rg)
        return (
            se + jnp.sum(jnp.where(m, rg, 0.0), axis=0, keepdims=True),
            sg + jnp.sum(up * xhat, axis=0, keepdims=True),
            sb + jnp.sum(up, axis=0, keepdims=True),
        )

    se, sg, sb = lax.fori_loop(0, t // RT, first_back, (none, none, none))
    sm[0:1, :], sm[1:2, :], sm[2:3, :] = se, sg, sb
    pg_own = pltpu.make_async_copy(hg, pg.at[rds(z * t, t)], ls.at[9])
    pg_own.start()
    for j, r in ((0, 7), (2, 8)):
        sm[r : r + 1, :] = jnp.sum(dqkv[j].astype(f32), axis=0, keepdims=True)

    nsm = g.wbits + g.zbits
    sm_order = [0] + list(range(g.wbits, nsm)) + list(range(1, g.wbits))
    sm_copy(sm_order[0]).start()

    for u in range(4):
        rs_core(u).wait_send()
    step2_in((1, 0, 5, 4))
    pg_own.wait()
    pg_step(0)
    pg_step(1)
    pg_step(2)
    step2_out((1, 0, 5, 4))
    step2_in((7, 6))
    step2_out((7, 6))
    for j in range(4):
        if j < 3:
            big = tn(dqkv[j], normed[...])
        else:
            big = tn(ctx[...], act[...])
        for zz in range(nz):
            rsb[rds(zk_inv(zz) * d + j * hs, hs), :] = big[zz * hs : (zz + 1) * hs, :]
    for u in range(ff_units, units):
        rs_core(u).start()
    out_own.wait()
    step1((8, 9))
    step1((10, 11))

    segs = 7

    attn = tuple(range(ff_units, units))
    plan_in = {
        0: [lambda: step3_in((3, 2, 1, 0))],
        2: [lambda: step3_in((5, 4, 7, 6))],
        4: [lambda: step2_in(attn)],
        8: [lambda: step3_in((8, 9))],
        9: [lambda: step3_in((10, 11))],
    }
    plan_out = {
        0: [lambda: step3_out((3, 2, 1, 0))],
        2: [lambda: step3_out((5, 4, 7, 6))],
        4: [lambda: step_z(1), lambda: step_z(0), lambda: step2_out(attn)],
        7: [lambda: step_z(3), lambda: step_z(2)],
        8: [lambda: step3_out((8, 9))],
        9: [lambda: step3_out((10, 11)), lambda: step_z(5), lambda: step_z(4)],
        11: [lambda: step_z(8)],
        12: [lambda: step4(1), lambda: step4(2)],
        13: [lambda: step_z(9)],
        14: [lambda: step5(1), lambda: step5(2)],
        15: [lambda: step_z(10)],
        16: [lambda: step6(1), lambda: step6(2)],
        17: [lambda: step4(0)],
        18: [lambda: step5(0)],
        19: [lambda: step6(0)],
    }

    def run_plan(plan, s):
        for at, fns in plan.items():
            @pl.when(s == at)
            def _():
                for fn in fns:
                    fn()

    def service(s):
        run_plan(plan_out, s)
        for i, at in enumerate((0, 2, 4, 5, 7, 9, 10, 12, 14)):
            when(s == at, lambda: pg_step(i + 3))
        for i in range(nsm):
            @pl.when(s == 4 * i)
            def _():
                sm_finish(sm_order[i])
                if i + 1 < nsm:
                    sm_copy(sm_order[i + 1]).start()

    def rest(s, carry):
        clip = (z + 1 + s // segs) % nz
        seg = s % segs
        run_plan(plan_in, s)

        @pl.when(seg == 0)
        def _():
            patches_copy(clip).start()
            patches_copy(clip).wait()
            first_norm(clip, False)
            project()

        pl.when(seg == 1)(lambda: attend_range(0, pairs // 2))

        @pl.when(seg == 2)
        def _():
            attend_range(pairs // 2, pairs)
            second_norm(False)

        pl.when(seg >= 3)(lambda: feed(seg - 3, False))
        pl.when(seg == segs - 1)(lambda: write_out(clip))
        service(s)
        return carry

    lax.fori_loop(0, segs * (nz - 1), rest, 0)
    for i in range(nsm):
        if 4 * i >= segs * (nz - 1):
            sm_finish(sm_order[i])
            if i + 1 < nsm:
                sm_copy(sm_order[i + 1]).start()
    so_copy = pltpu.make_async_copy(sm, small_out, ls.at[9])
    so_copy.start()

    for cp in zb_copies:
        cp.wait_send()
    for zz in range(nz):
        for q in range(g.chunks):
            pl.when((zz != z) & jnp.logical_not(mid))(lambda: pg_copy(zz, q, True).wait_recv())
            pl.when((zz <= z) & has_up)(lambda: pg_copy(zz, q, True).wait_send())
            pl.when((zz >= z) & has_dn)(lambda: pg_copy(zz, q, False).wait_send())
        for p in range(3):
            for i in range(2):
                pl.when((zz <= z) & has_up)(lambda: agz(p, zz, True)[i].wait_send())
                pl.when((zz >= z) & has_dn)(lambda: agz(p, zz, False)[i].wait_send())
    for p in range(3):
        fin_c(p).wait()
        for cp in fin_xy(p) + fin_d(p):
            cp.wait_send()
    for n in range(agu):
        for cp in ag_xy(n) + ag_d(n) + (ag_c(n),):
            cp.wait_send()
    for n in range(units):
        for cp in rs_d(n) + rs_p(n):
            cp.wait_send()
        if ru_pk(n)[1] > 0:
            zz, up, dn = zdir(n)
            pl.when(up)(lambda: rs_z(n, zz, True).wait_send())
            pl.when(dn)(lambda: rs_z(n, zz, False).wait_send())
    for u in range(ff_units, units):
        rs_core(u).wait_send()
    so_copy.wait()


def closing_kernel(nz, hs, out_in, pg, ga, gb, gc, small, out, patch_grad, qkv_g, out_g, up_g, down_g, qv, up_b, *vectors):
    i = pl.program_id(0)
    out[...] = out_in[...]
    patch_grad[...] = pg[...].astype(bf16)
    up_g[...] = gb[...]
    down_g[...] = gc[...]
    for j in range(3):
        @pl.when(i == j)
        def _():
            qkv_g[j] = ga[j * hs : (j + 1) * hs, :]

    @pl.when(i == 3)
    def _():
        out_g[...] = ga[3 * hs : 4 * hs, :]
        z = lax.axis_index("narrow")
        for zz in range(nz):
            @pl.when(z == zz)
            def _():
                qv[...] = small[7:9, zz * hs : (zz + 1) * hs]
                up_b[...] = small[9 + zz : 10 + zz, :].reshape(up_b.shape)

        for k, ref in enumerate(vectors):
            ref[...] = small[k : k + 1, :].reshape(ref.shape)


def make(mesh):
    def on_device(
        patches, mask_index, mask_count, mask_embed, norm1_gain, norm1_bias, w_qkv, b_qv, w_out, b_out,
        norm2_gain, norm2_bias, w_up, b_up, w_down, b_down, cotangent,
    ):
        rows, d = patches.shape
        nz = mesh.shape["narrow"]
        t, hs, fs = rows // nz, w_qkv.shape[2], w_up.shape[1]
        assert t == PATCHES and fs == d and 4 * hs == d
        g = make_cfg(mesh, d, t, hs)
        pr = g.pr
        qkv_t = jnp.swapaxes(w_qkv, 1, 2).reshape(3 * hs, d)
        hbm = pl.BlockSpec(memory_space=pl.ANY)
        vm = pl.BlockSpec(memory_space=pltpu.VMEM)
        u = g.units

        def o(r, dt=f32):
            return jax.ShapeDtypeStruct((r, d), dt)

        out_shape = (
            o(rows, bf16), o(rows), o(d), o(d), o(d), o(16),
            o(u * d), o(u * 4 * pr), o(u * pr // 2), o(u * pr // 2), o(u * pr), o(u * pr), o(2 * u * pr), o(3 * g.groups * pr),
        )
        v = pltpu.VMEM
        scratch = [
            v((3, d, d), bf16), v((d, d), bf16), v((2 * nz, d, d), bf16),
            v((t, d), f32), v((t, d), f32), v((t, d), f32), v((t, d), bf16), v((3, t, d), bf16),
            v((t, d), bf16), v((t, d), bf16), v((t, d), bf16), v((t, d), f32), v((t, d), bf16), v((t, d), f32),
            v((t, d), f32), v((t, d), bf16), v((3, t, d), bf16), v((t, 1), f32), v((t, 1), f32), v((t, 1), f32),
            v((4 * d + 2 * nz * 4 * pr, d), f32), v((d, d), f32), v((4 * pr, d), f32),
            v((2 * pr, d), f32), v((3 * (pr + g.xr), d), f32), v((3 * (pr + g.xr), d), bf16), v((8, d), f32),
            v((nz * 8, d), f32), v((16, d), f32), v(((g.wbits + g.zbits) * 16, d), f32),
            v((3 * pr, d), f32),
            pltpu.SemaphoreType.DMA((g.nsem,)), pltpu.SemaphoreType.DMA((g.nsem,)), pltpu.SemaphoreType.DMA((40,)),
        ]
        outs = pl.pallas_call(
            functools.partial(layer_kernel, g),
            out_shape=out_shape,
            in_specs=[hbm, hbm, hbm, hbm, vm, vm, vm, pl.BlockSpec(memory_space=pltpu.SMEM)] + [vm] * 7 + [hbm, hbm],
            out_specs=[hbm] * len(out_shape),
            scratch_shapes=scratch,
            compiler_params=pltpu.CompilerParams(
                collective_id=1, has_side_effects=True, vmem_limit_bytes=64 * 2**20 - 2**17
            ),
            name="layer",
        )(
            qkv_t, w_out, w_up, w_down, b_up, b_qv, mask_index, mask_count, mask_embed, norm1_gain, norm1_bias, b_out,
            norm2_gain, norm2_bias, b_down, patches, cotangent,
        )
        steps = 8

        def cut(r):
            return pl.BlockSpec((r // steps, d), lambda i: (i, 0))

        def whole(*shape):
            return pl.BlockSpec(shape, lambda i: (0,) * len(shape))

        closed = pl.pallas_call(
            functools.partial(closing_kernel, nz, hs),
            grid=(steps,),
            out_shape=(
                o(rows, bf16), o(rows, bf16), jax.ShapeDtypeStruct((3, hs, d), f32), o(hs), o(d), o(d),
                jax.ShapeDtypeStruct((2, hs), f32),
            ) + (jax.ShapeDtypeStruct((d,), f32),) * 8,
            in_specs=[cut(rows), cut(rows), whole(d, d), cut(d), cut(d), whole(16, d)],
            out_specs=(
                cut(rows), cut(rows), whole(3, hs, d), whole(hs, d), cut(d), cut(d), whole(2, hs),
            ) + (whole(d),) * 8,
            compiler_params=pltpu.CompilerParams(vmem_limit_bytes=64 * 2**20 - 2**17),
            name="closing",
        )(*outs[:6])
        output, patch_grad, qkv_o, out_o, up_o, down_o, qvb, upb = closed[:8]
        small = closed[8:]
        return (
            output, patch_grad, small[0], small[1], small[2], jnp.swapaxes(qkv_o, 1, 2), qvb, out_o, small[3],
            small[4], small[5], up_o, upb, down_o, small[6],
        )

    return on_device


def solution(mesh):
    return jax.shard_map(
        make(mesh),
        mesh=mesh,
        in_specs=(
            P("wide", None), P("wide", None), P("wide"), P(), P(), P(), P(None, None, "narrow"), P(None, "narrow"),
            P("narrow", None), P(), P(), P(), P(None, "narrow"), P("narrow"), P("narrow", None), P(), P("wide", None),
        ),
        out_specs=(
            P("wide", None), P("wide", None), P(), P(), P(), P(None, None, "narrow"), P(None, "narrow"),
            P("narrow", None), P(), P(), P(), P(None, "narrow"), P("narrow"), P("narrow", None), P(),
        ),
        check_vma=False,
    )
```

```python
import functools
import math

import jax
import jax.numpy as jnp
from jax import lax
from jax.experimental import pallas as pl
from jax.experimental.pallas import tpu as pltpu
from jax.sharding import PartitionSpec as P

HD = 64
PATCHES = 512
EPS = 1e-06
f32 = jnp.float32
bf16 = jnp.bfloat16
MESH = pl.DeviceIdType.MESH
RT = 128


def nn(a, b):
    return lax.dot_general(a, b, (((1,), (0,)), ((), ())), preferred_element_type=f32)


def nt(a, b):
    return lax.dot_general(a, b, (((1,), (1,)), ((), ())), preferred_element_type=f32)


def tn(a, b):
    return lax.dot_general(a, b, (((0,), (0,)), ((), ())), preferred_element_type=f32)


def rds(start, size, unit=8):
    if isinstance(start, int):
        return pl.ds(start, size)
    return pl.ds(pl.multiple_of(start, unit), size)


def normalise(v):
    centred = v - jnp.mean(v, axis=-1, keepdims=True)
    inverse = lax.rsqrt(jnp.mean(centred * centred, axis=-1, keepdims=True) + EPS)
    return centred * inverse, inverse


def norm_back(upstream, xhat, inverse, gain):
    weighted = upstream * gain
    return inverse * (
        weighted
        - jnp.mean(weighted, axis=-1, keepdims=True)
        - xhat * jnp.mean(weighted * xhat, axis=-1, keepdims=True)
    )


def softmax_t(scores):
    e = jnp.exp(scores - jnp.max(scores, axis=0, keepdims=True))
    return e * (1.0 / jnp.sum(e, axis=0, keepdims=True))


class Cfg:
    pass


def make_cfg(mesh, d, t, hs):
    g = Cfg()
    g.nw, g.nz = mesh.shape["wide"], mesh.shape["narrow"]
    assert g.nz == 4
    g.groups = g.nw // 8
    g.d, g.t, g.hs = d, t, hs
    g.pr = d // 8
    g.units = 3 * g.nz
    g.agu = 3 * (g.nz - 1)
    g.xr = g.pr // 3
    g.wbits = g.nw.bit_length() - 1
    g.zbits = g.nz.bit_length() - 1
    g.chunks = 8
    n = 0
    for name, count in (
        ("agz", 6 * g.nz), ("age", 6 * g.nz), ("agx", g.agu), ("agy", g.agu), ("agdx", g.agu), ("agdy", g.agu), ("agc", g.agu),
        ("rc", g.units), ("rdx", g.units), ("rdy", g.units), ("rpx", g.units), ("rpy", g.units), ("rz", 6 * g.nz),
        ("fx", 3), ("fy", 3), ("fdx", 3), ("fdy", 3), ("fc", 3), ("zb", g.nz), ("pg", 2 * g.nz * g.chunks),
        ("sm", g.wbits + g.zbits), ("fg", 3 * g.groups),
    ):
        setattr(g, name, n)
        n += count
    g.nsem = n
    return g


def when(cond, fn):
    if isinstance(cond, bool):
        if cond:
            fn()
    else:
        pl.when(cond)(fn)


def layer_kernel(
    g,
    qkv_t, w_out, w_up, w_down, b_up, b_qv, mask_index, mask_count, embed_ref, gain1_ref, bias1_ref, b_out_ref, gain2_ref,
    bias2_ref, b_down_ref, patches, cot_hbm,
    out, pg, ga, gb, gc, small_out, wbuf, crecv, dxr, dyr, pxr, pyr, zr, grecv,
    wq, wo, ffw, res, xh1, xh2, normed, qkv, ctx, hid, act, slope, cotv, acc, hg, bg, dqkv, r1, r2, mown, rsb, cst, rst,
    zst, part, pbf, zb, zball, sm, smr, fin, ss, rs, ls,
):
    nz, d, t, hs, pr, units = g.nz, g.d, g.t, g.hs, g.pr, g.units
    half = pr // 2
    ff_units = 2 * nz
    w = lax.axis_index("wide")
    z = lax.axis_index("narrow")
    c, x, y = w % 2, (w // 2) % 2, (w // 4) % 2
    sib, xn, yn = {"wide": w + 1 - 2 * c}, {"wide": w + 2 - 4 * x}, {"wide": w + 4 - 8 * y}
    zup, zdn = {"narrow": z + 1}, {"narrow": z - 1}
    has_up, has_dn = z < nz - 1, z > 0
    mid = (z > 0) & (z < nz - 1)
    yx, yx_x, yx_y, yx_d = y * 2 + x, y * 2 + 1 - x, (1 - y) * 2 + x, (1 - y) * 2 + 1 - x
    pos, pos_x, pos_y, pos_d = c * 4 + yx, c * 4 + yx_x, c * 4 + yx_y, c * 4 + yx_d
    zp = [None] + [{"narrow": (z + k) % nz} for k in range(1, nz)]
    gp = [None] + [{"wide": (w + 8 * k) % g.nw} for k in range(1, g.groups)]
    gouts = (ga, gb, gc)

    zside = z // 2
    zend = z + zside * (nz - 1 - 2 * z)

    def swap01(k):
        return k + zend * (1 - k // 2) * (1 - 2 * (k % 2))

    def zk(k):
        b = swap01(k)
        return b + zside * (nz - 1 - 2 * b)

    def zk_inv(zz):
        return swap01(zz + zside * (nz - 1 - 2 * zz))

    def rcopy(src, dst, si, ri, dev):
        return pltpu.make_async_remote_copy(src, dst, ss.at[si], rs.at[ri], device_id=dev, device_id_type=MESH)

    barrier = pltpu.get_barrier_semaphore()
    partners = [sib, xn, yn] + zp[1:] + gp[1:]
    for p in partners:
        pl.semaphore_signal(barrier, inc=1, device_id=p, device_id_type=MESH)

    def wrow(p, zz, q):
        return (p * nz + zz) * d + q * pr

    xr = g.xr
    hr = (pr - xr) // 2
    agu = g.agu

    def ag_pk(n):
        if isinstance(n, int) and n < nz - 1:
            return 0, n + 1
        m = n - (nz - 1)
        return 1 + m % 2, 1 + m // 2

    def own_loads():
        cps = [(qkv_t.at[pl.ds(j * hs, hs)], wq.at[j, rds(z * hs, hs, 16)]) for j in range(3)]
        cps += [(w_out, wo.at[rds(z * hs, hs, 16)]), (w_up, ffw.at[0]), (w_down, ffw.at[1])]
        return [pltpu.make_async_copy(src, dst, ls.at[i]) for i, (src, dst) in enumerate(cps)]

    def ag_block(n, q, lo, size):
        p, k = ag_pk(n)
        return wbuf.at[rds(wrow(p, zk(k), q) + lo, size)]

    def ag_xy(n):
        b = ag_block(n, pos, 0, pr)
        return rcopy(b, b, g.agx + n, g.agx + n, xn), rcopy(b, b, g.agy + n, g.agy + n, yn)

    def ag_d(n):
        bx, by = ag_block(n, pos_x, xr, hr), ag_block(n, pos_y, xr + hr, hr)
        return rcopy(bx, bx, g.agdy + n, g.agdy + n, yn), rcopy(by, by, g.agdx + n, g.agdx + n, xn)

    def ag_c(n):
        b = ag_block(n, c * 4, 0, 4 * pr)
        return rcopy(b, b, g.agc + n, g.agc + n, sib)

    def agz(p, zz, up, own=False):
        pair = []
        for sem, q, lo, size in ((g.agz, pos, 0, pr), (g.age, pos_d, pr, xr)):
            to = wbuf.at[rds(wrow(p, zz, q), size)]
            src = part.at[pl.ds(p * (pr + xr) + lo, size)] if own else to
            ri = sem + p * nz + zz
            pair.append(rcopy(src, to, ri + (0 if up else 3 * nz), ri, zup if up else zdn))
        return pair

    def start(cps):
        for cp in cps:
            cp.start()

    def agz_own(p):
        pl.when(has_up)(lambda: start(agz(p, z, True, True)))
        pl.when(has_dn)(lambda: start(agz(p, z, False, True)))

    def ag_z(n):
        p, k = ag_pk(n)
        zz = zk(k)

        @pl.when(mid)
        def _():
            for i, cp in enumerate(agz(p, zz, True)):
                cp.wait_recv()
                pl.when(zz < z)(lambda: agz(p, zz, True)[i].start())
                pl.when(zz > z)(lambda: agz(p, zz, False)[i].start())

    def ag_s1(n):
        p, k = ag_pk(n)
        pl.when(jnp.logical_not(mid))(lambda: agz(p, zk(k), True)[0].wait_recv())
        start(ag_xy(n))

    def ag_s2(n):
        cx, cy = ag_xy(n)
        dy, dx = ag_d(n)
        cx.wait_recv()
        dy.start()
        cy.wait_recv()
        dx.start()

    def ag_s3(n):
        p, k = ag_pk(n)
        pl.when(jnp.logical_not(mid))(lambda: agz(p, zk(k), True)[1].wait_recv())
        dy, dx = ag_d(n)
        dy.wait_recv()
        dx.wait_recv()
        ag_c(n).start()

    def ag_load(n):
        p, k = ag_pk(n)
        return [
            pltpu.make_async_copy(
                wbuf.at[rds(wrow(p, zk(k), 4 * i), 4 * pr)], cst.at[pl.ds(i * 4 * pr, 4 * pr)], ls.at[10 + i]
            )
            for i in range(2)
        ]

    def ag_conv_start(n):
        ag_c(n).wait_recv()
        start(ag_load(n))

    def ag_conv(n):
        for cp in ag_load(n):
            cp.wait()
        p, k = ag_pk(n)
        if isinstance(n, int) and n < nz - 1:
            zz = zk(k)
            for j in range(3):
                wq[j, rds(zz * hs, hs, 16), :] = cst[j * hs : (j + 1) * hs, :].astype(bf16)
            wo[rds(zz * hs, hs, 16), :] = cst[3 * hs : 4 * hs, :].astype(bf16)
        else:
            ffw[2 * k + p - 1] = cst[...].astype(bf16)

    def ag_step(n):
        static = isinstance(n, int)
        when(n < agu, lambda: ag_s2(n))
        if static:
            when(n + 2 < agu, lambda: ag_s1(n + 2))
            when(n + 3 < agu, lambda: ag_z(n + 3))
        when(n - 1 >= 0, lambda: when(n - 1 < agu, lambda: ag_s3(n - 1)))
        if not static or (n >= 2 and n != nz):
            when(n - 2 < agu, lambda: ag_conv(n - 2))
        if not static or n >= 1:
            when(n - 1 < agu, lambda: ag_conv_start(n - 1))
        if static and n == nz - 1:
            ag_conv(n - 1)

    def ru_pk(u):
        if isinstance(u, int):
            return (2 - (ff_units - 1 - u) % 2, (ff_units - 1 - u) // 2) if u < ff_units else (0, units - 1 - u)
        late = u // ff_units
        return (
            (1 - late) * (2 - (2 * ff_units - 1 - u) % 2),
            (1 - late) * ((ff_units - 1 - u + late * ff_units) // 2) + late * (units - 1 - u),
        )

    def slot_row(u):
        return ((2 * ff_units - 1 - u) % 4) * d

    def sum_row(u, q):
        if isinstance(u, int):
            base = 4 * d + u * 4 * pr if u < ff_units else slot_row(u) + c * 4 * pr
        else:
            late = u // ff_units
            base = (1 - late) * (4 * d + u * 4 * pr) + late * (slot_row(u) + c * 4 * pr)
        return base + q * pr

    def rs_core(u):
        return rcopy(
            rsb.at[rds(slot_row(u) + (1 - c) * 4 * pr, 4 * pr)], crecv.at[rds(u * 4 * pr, 4 * pr)], g.rc + u, g.rc + u, sib
        )

    def rs_d(u):
        a = rcopy(rsb.at[rds(sum_row(u, yx_d), half)], dxr.at[rds(u * half, half)], g.rdx + u, g.rdx + u, xn)
        b = rcopy(rsb.at[rds(sum_row(u, yx_d) + half, half)], dyr.at[rds(u * half, half)], g.rdy + u, g.rdy + u, yn)
        return a, b

    def rs_p(u):
        a = rcopy(rsb.at[rds(sum_row(u, yx_x), pr)], pxr.at[rds(u * pr, pr)], g.rpx + u, g.rpx + u, xn)
        b = rcopy(rsb.at[rds(sum_row(u, yx_y), pr)], pyr.at[rds(u * pr, pr)], g.rpy + u, g.rpy + u, yn)
        return a, b

    def rs_z(u, zz, up):
        p, _ = ru_pk(u)
        i = (p * nz + zz) * 2 + (0 if up else 1)
        return rcopy(rsb.at[rds(sum_row(u, yx), pr)], zr.at[rds(i * pr, pr)], g.rz + i, g.rz + i, zup if up else zdn)

    def rs_z_load(p, zz, up, slot):
        i = (p * nz + zz) * 2 + (0 if up else 1)
        src = zr.at[rds(i * pr, pr)]
        return (
            rcopy(src, src, g.rz + i, g.rz + i, sib),
            pltpu.make_async_copy(src, zst.at[pl.ds(slot * pr, pr)], ls.at[18 + slot]),
        )

    def l1(u):
        return pltpu.make_async_copy(crecv.at[rds(u * 4 * pr, 4 * pr)], rst, ls.at[12])

    def step1a(u):
        rs_core(u).wait_recv()
        l1(u).start()

    def step1b(u):
        l1(u).wait()
        src = slot_row(u) + c * 4 * pr
        rsb[rds(sum_row(u, 0), 4 * pr), :] = rsb[rds(src, 4 * pr), :] + rst[...]

    def step1c(u):
        start(rs_d(u))

    def step1(us):
        cps = [
            pltpu.make_async_copy(crecv.at[rds(u * 4 * pr, 4 * pr)], cst.at[pl.ds(i * 4 * pr, 4 * pr)], ls.at[36 + i])
            for i, u in enumerate(us)
        ]
        for u, cp in zip(us, cps):
            rs_core(u).wait_recv()
            cp.start()
        for i, (u, cp) in enumerate(zip(us, cps)):
            cp.wait()
            rsb[rds(sum_row(u, 0), 4 * pr), :] = (
                rsb[rds(slot_row(u) + c * 4 * pr, 4 * pr), :] + cst[i * 4 * pr : (i + 1) * 4 * pr, :]
            )
            step1c(u)

    def l2(u, i):
        return (
            pltpu.make_async_copy(dxr.at[rds(u * half, half)], rst.at[pl.ds(i * pr, half)], ls.at[20 + 2 * i]),
            pltpu.make_async_copy(dyr.at[rds(u * half, half)], rst.at[pl.ds(i * pr + half, half)], ls.at[21 + 2 * i]),
        )

    def step2_in(us):
        for i, u in enumerate(us):
            for cp, ld in zip(rs_d(u), l2(u, i)):
                cp.wait_recv()
                ld.start()

    def step2_out(us):
        for i, u in enumerate(us):
            for ld in l2(u, i):
                ld.wait()
            rsb[rds(sum_row(u, yx_y), half), :] += rst[i * pr : i * pr + half, :]
            rsb[rds(sum_row(u, yx_x) + half, half), :] += rst[i * pr + half : (i + 1) * pr, :]
            start(rs_p(u))

    def l3(u, i):
        return (
            pltpu.make_async_copy(pxr.at[rds(u * pr, pr)], cst.at[pl.ds(2 * i * pr, pr)], ls.at[28 + 2 * i]),
            pltpu.make_async_copy(pyr.at[rds(u * pr, pr)], cst.at[pl.ds((2 * i + 1) * pr, pr)], ls.at[29 + 2 * i]),
        )

    def zdir(u):
        _, k = ru_pk(u)
        zz = zk(k)
        return zz, zz > z, zz < z

    def step3_in(us):
        for i, u in enumerate(us):
            for cp, ld in zip(rs_p(u), l3(u, i)):
                cp.wait_recv()
                ld.start()

    def step3_out(us):
        for i, u in enumerate(us):
            for ld in l3(u, i):
                ld.wait()
            rsb[rds(sum_row(u, yx), pr), :] += (
                cst[2 * i * pr : (2 * i + 1) * pr, :] + cst[(2 * i + 1) * pr : (2 * i + 2) * pr, :]
            )
            if ru_pk(u)[1] > 0:
                zz, up, dn = zdir(u)
                pl.when(up & (z == 0))(lambda: rs_z(u, zz, True).start())
                pl.when(dn & (z == nz - 1))(lambda: rs_z(u, zz, False).start())

    def step_z(u):
        p, _ = ru_pk(u)
        zz, up, dn = zdir(u)
        for cond, flag in ((up, True), (dn, False)):
            @pl.when(cond & mid)
            def _():
                got, ld = rs_z_load(p, zz, flag, 0)
                got.wait_recv()
                ld.start()
                ld.wait()
                rsb[rds(sum_row(u, yx), pr), :] += zst[0:pr, :]
                rs_z(u, zz, flag).start()

    own_unit = {0: units - 1, 1: ff_units - 2, 2: ff_units - 1}

    def fin_xy(p):
        src = fin.at[pl.ds(p * pr, pr)]
        to = gouts[p].at[rds(pos * pr, pr)]
        return rcopy(src, to, g.fx + p, g.fx + p, xn), rcopy(src, to, g.fy + p, g.fy + p, yn)

    def fin_own(p):
        return pltpu.make_async_copy(fin.at[pl.ds(p * pr, pr)], gouts[p].at[rds(pos * pr, pr)], ls.at[5 + p])

    def fin_d(p):
        bx, by = gouts[p].at[rds(pos_x * pr, half)], gouts[p].at[rds(pos_y * pr + half, half)]
        return rcopy(bx, bx, g.fdy + p, g.fdy + p, yn), rcopy(by, by, g.fdx + p, g.fdx + p, xn)

    def fin_c(p):
        b = gouts[p].at[rds(c * 4 * pr, 4 * pr)]
        return rcopy(b, b, g.fc + p, g.fc + p, sib)

    def fin_g(p, k):
        return rcopy(
            fin.at[pl.ds(p * pr, pr)], grecv.at[pl.ds((p * g.groups + g.groups - k) * pr, pr)],
            g.fg + p * g.groups + k, g.fg + p * g.groups + g.groups - k, gp[k],
        )

    def step4(p):
        sl = slice(p * pr, (p + 1) * pr)
        fin[sl, :] = rsb[rds(sum_row(own_unit[p], yx), pr), :]
        ins = ((has_dn, True, 0), (has_up, False, 1))
        for cond, flag, slot in ins:
            @pl.when(cond)
            def _():
                got, ld = rs_z_load(p, z, flag, slot)
                got.wait_recv()
                ld.start()

        for cond, flag, slot in ins:
            @pl.when(cond)
            def _():
                rs_z_load(p, z, flag, slot)[1].wait()
                fin[sl, :] += zst[slot * pr : (slot + 1) * pr, :]

        if g.groups > 1:
            total = fin[sl, :]
            for k in range(1, g.groups):
                fin_g(p, k).start()
            for k in range(1, g.groups):
                fin_g(p, k).wait()
            for k in range(1, g.groups):
                src = grecv.at[pl.ds((p * g.groups + k) * pr, pr)]
                cp = pltpu.make_async_copy(src, zst.at[pl.ds(0, pr)], ls.at[3])
                cp.start()
                cp.wait()
                total = total + zst[0:pr, :]
            fin[sl, :] = total
        fin_own(p).start()
        for cp in fin_xy(p):
            cp.start()

    def step5(p):
        cx, cy = fin_xy(p)
        dy, dx = fin_d(p)
        cx.wait_recv()
        dy.start()
        cy.wait_recv()
        dx.start()

    def step6(p):
        dy, dx = fin_d(p)
        dy.wait_recv()
        dx.wait_recv()
        fin_own(p).wait()
        fin_c(p).start()

    def sm_copy(i):
        if i < g.wbits:
            b = 1 << i
            dev = {"wide": w + b - 2 * b * ((w // b) % 2)}
        else:
            b = 1 << (i - g.wbits)
            dev = {"narrow": z + b - 2 * b * ((z // b) % 2)}
        return rcopy(sm, smr.at[pl.ds(16 * i, 16)], g.sm + i, g.sm + i, dev)

    def sm_finish(i):
        sm_copy(i).wait()
        sm[...] += smr[16 * i : 16 * (i + 1), :]

    ck = t // g.chunks

    def pg_copy(zz, q, up):
        to = pg.at[rds(zz * t + q * ck, ck)]
        ri = g.pg + zz * g.chunks + q
        return rcopy(to, to, ri + (0 if up else nz * g.chunks), ri, zup if up else zdn)

    def pg_send(zz, q, up):
        pg_copy(zz, q, up).start()

    def pg_step(s):
        if s < g.chunks:
            pl.when(has_up)(lambda: pg_send(z, s, True))
            pl.when(has_dn)(lambda: pg_send(z, s, False))
            return
        j = s - g.chunks
        for up, zz, count, more in (
            (True, z - 1 - j // g.chunks, g.chunks * z, has_up),
            (False, z + 1 + j // g.chunks, g.chunks * (nz - 1 - z), has_dn),
        ):
            @pl.when((j < count) & more)
            def _():
                pg_copy(zz, j % g.chunks, up).wait_recv()
                pg_send(zz, j % g.chunks, up)

    embed, gain1, bias1, b_out, gain2, bias2, b_down = [
        ref[...].reshape(1, d)
        for ref in (embed_ref, gain1_ref, bias1_ref, b_out_ref, gain2_ref, bias2_ref, b_down_ref)
    ]

    def tiles(fn):
        def body(i, carry):
            fn(rds(i * RT, RT, RT), i * RT)
            return carry

        lax.fori_loop(0, t // RT, body, 0)

    def patches_copy(clip):
        return pltpu.make_async_copy(patches.at[rds(clip * t, t, 16)], bg, ls.at[8])

    def first_norm(clip, keep):
        slots = lax.broadcasted_iota(jnp.int32, (1, mask_index.shape[1]), 1)
        listed = jnp.where(slots < mask_count[clip], mask_index[pl.ds(clip, 1), :], -1)

        def fn(sl, at):
            place = lax.broadcasted_iota(jnp.int32, (RT, listed.shape[1]), 0) + at
            m = jnp.max(jnp.where(listed == place, 1.0, 0.0), axis=1, keepdims=True)
            v = jnp.where(m > 0.5, embed, bg[sl, :].astype(f32))
            res[sl, :] = v
            xhat, inverse = normalise(v)
            if keep:
                mown[sl, :] = m
                xh1[sl, :] = xhat
                r1[sl, :] = inverse
            normed[sl, :] = (xhat * gain1 + bias1).astype(bf16)

        tiles(fn)

    def project():
        biases = []
        for i in (1, 2):
            total = zball[i : i + 1, :]
            for k in range(1, nz):
                total = total + zball[8 * k + i : 8 * k + i + 1, :]
            biases.append(total)
        n = normed[...]
        qkv[0] = ((nt(n, wq[0]) + biases[0]).astype(bf16) * bf16(HD**-0.5)).astype(bf16)
        qkv[1] = nt(n, wq[1]).astype(bf16)
        qkv[2] = (nt(n, wq[2]) + biases[1]).astype(bf16)

    def head_masks():
        lane = lax.broadcasted_iota(jnp.int32, (1, 2 * HD), 1)
        first = (lane < HD).astype(f32)
        return first.astype(bf16), (1.0 - first).astype(bf16)

    def attend(i):
        sl = rds(i * 2 * HD, 2 * HD, 2 * HD)
        qp, kp, vp = qkv[0, :, sl], qkv[1, :, sl], qkv[2, :, sl]
        vt = vp.T
        outs = []
        for h, hm in enumerate(head_masks()):
            probs = softmax_t(nt(kp * hm, qp)).astype(bf16)
            outs.append(nn(vt[h * HD : (h + 1) * HD, :], probs))
        ctx[:, sl] = jnp.concatenate(outs, axis=0).T.astype(bf16)

    def attend_range(lo, hi):
        def body(i, carry):
            attend(i)
            return carry

        lax.fori_loop(lo, hi, body, 0)

    def second_norm(keep):
        acc[...] = nn(ctx[...], wo[...])

        def fn(sl, at):
            v = res[sl, :] + acc[sl, :] + b_out
            res[sl, :] = v
            xhat, inverse = normalise(v)
            if keep:
                xh2[sl, :] = xhat
                r2[sl, :] = inverse
            hid[sl, :] = (xhat * gain2 + bias2).astype(bf16)
            acc[sl, :] = jnp.zeros((RT, d), f32)

        tiles(fn)

    def feed(k, keep):
        bias = zball[rds(zk(k) * 8, 8), :][0:1, :]
        slope[...] = nn(hid[...], ffw[2 * k])

        def fn(sl, at):
            v = slope[sl, :] + bias
            cdf = 0.5 * (1.0 + lax.erf(v * (0.5**0.5)))
            act[sl, :] = (v * cdf).astype(bf16)
            if keep:
                slope[sl, :] = cdf + v * jnp.exp(-0.5 * v * v) * ((0.5 / math.pi) ** 0.5)

        tiles(fn)
        acc[...] += nn(act[...], ffw[2 * k + 1])

    def out_copy(clip):
        return pltpu.make_async_copy(act, out.at[rds(clip * t, t, 16)], ls.at[38])

    def write_out(clip):
        def fn(sl, at):
            act[sl, :] = (res[sl, :] + acc[sl, :] + b_down).astype(bf16)

        tiles(fn)
        out_copy(clip).start()

    def feed_back(k):
        acc2 = nt(cotv[...], ffw[2 * k + 1])
        b = (acc2 * slope[...]).astype(bf16)
        bg[...] = b
        sm[pl.ds(9 + zk(k), 1), :] = jnp.sum(b.astype(f32), axis=0, keepdims=True)
        part_sum = nt(bg[...], ffw[2 * k])

        @pl.when(k == 0)
        def _():
            hg[...] = part_sum

        @pl.when(k > 0)
        def _():
            hg[...] += part_sum

    sm[...] = jnp.zeros((16, d), f32)
    cot_copy = pltpu.make_async_copy(cot_hbm.at[rds(z * t, t, 16)], cotv, ls.at[9])
    shares = []
    first_rows = 3 * hs // pr
    for p, src in enumerate((qkv_t, w_up, w_down)):
        for q, lo, size in ((pos, 0, pr), (pos_d, pr, xr)):
            i = len(shares)
            to = pbf.at[pl.ds(p * (pr + xr) + lo, size)]

            def share(ref, row):
                return pltpu.make_async_copy(ref.at[rds(row, size, 16)], to, ls.at[20 + i])

            if p == 0:
                pl.when(q < first_rows)(lambda: share(qkv_t, q * pr).start())
                pl.when(q >= first_rows)(lambda: share(w_out, (q - first_rows) * pr).start())
                shares.append(share(w_out, 0))
            else:
                shares.append(share(src, q * pr))
                shares[-1].start()
    patches_copy(z).start()
    own = own_loads()
    start(own)
    cot_copy.start()
    zb[...] = jnp.zeros((8, d), f32)
    zb[0:1, :] = b_up[...].reshape(1, d)
    for zz in range(nz):
        @pl.when(z == zz)
        def _():
            zb[1:3, zz * hs : (zz + 1) * hs] = b_qv[...]

    zball[rds(z * 8, 8), :] = zb[...]
    for cp in shares:
        cp.wait()
    part[...] = pbf[...].astype(f32)
    pl.semaphore_wait(barrier, len(partners))
    agz_own(0)
    zb_copies = [
        rcopy(zb, zball.at[rds(z * 8, 8)], g.zb + k, g.zb + nz - k, zp[k]) for k in range(1, nz)
    ]
    start(zb_copies)
    patches_copy(z).wait()
    first_norm(z, True)
    ag_z(0)
    ag_s1(0)
    ag_z(1)
    pl.when(mid)(lambda: ag_s1(1))
    ag_z(2)
    agz_own(1)
    agz_own(2)
    ag_s2(0)
    pl.when(jnp.logical_not(mid))(lambda: ag_s1(1))
    ag_s1(2)
    ag_z(3)
    for n in range(1, nz):
        ag_step(n)
    for cp in own:
        cp.wait()
    for k in range(1, nz):
        rcopy(zb, zball.at[rds(((z + k) % nz) * 8, 8)], g.zb + k, g.zb + k, zp[k]).wait_recv()
    pairs = nz * hs // (2 * HD)
    project()
    for i in range(3):
        ag_step(nz + i)
        attend_range(i * pairs // 3, (i + 1) * pairs // 3)
    second_norm(True)
    cot_copy.wait()

    def ff_body(k, carry):
        ud, uu = ff_units - 1 - 2 * k, ff_units - 2 - 2 * k
        ag_step(nz + 3 + k)

        @pl.when(k >= 2)
        def _():
            rs_core(ud + 4).wait_send()
            rs_core(uu + 4).wait_send()

        pl.when(k >= 1)(lambda: step1a(ud + 2))
        feed(k, True)
        rsb[rds(slot_row(ud), d), :] = tn(act[...], cotv[...])
        rs_core(ud).start()

        @pl.when(k >= 1)
        def _():
            step1b(ud + 2)
            step1c(ud + 2)
            step1a(uu + 2)

        feed_back(k)

        @pl.when(k >= 1)
        def _():
            step1b(uu + 2)
            step1c(uu + 2)

        rsb[rds(slot_row(uu), d), :] = tn(hid[...], bg[...])
        rs_core(uu).start()
        return carry

    lax.fori_loop(0, nz, ff_body, 0)
    step1((1, 0))
    step2_in((3, 2))

    none = jnp.zeros((1, d), f32)

    def mid_back(i, carry):
        sg, sb, so, sc = carry
        sl = rds(i * RT, RT, RT)
        up, xhat = hg[sl, :], xh2[sl, :]
        cf = cotv[sl, :].astype(f32)
        mg = cf + norm_back(up, xhat, r2[sl, :], gain2)
        v = res[sl, :] + acc[sl, :] + b_down
        hid[sl, :] = v.astype(bf16)
        res[sl, :] = mg
        act[sl, :] = mg.astype(bf16)
        return (
            sg + jnp.sum(up * xhat, axis=0, keepdims=True),
            sb + jnp.sum(up, axis=0, keepdims=True),
            so + jnp.sum(mg, axis=0, keepdims=True),
            sc + jnp.sum(cf, axis=0, keepdims=True),
        )

    sg, sb, so, sc = lax.fori_loop(0, t // RT, mid_back, (none, none, none, none))
    step2_out((3, 2))
    sm[3:4, :], sm[4:5, :], sm[5:6, :], sm[6:7, :] = so, sg, sb, sc
    out_own = pltpu.make_async_copy(hid, out.at[rds(z * t, t, 16)], ls.at[8])
    out_own.start()
    bg[...] = nt(act[...], wo[...]).astype(bf16)

    def att_back(i, carry):
        sl = rds(i * 2 * HD, 2 * HD, 2 * HD)
        qp, kp, vp, cg = qkv[0, :, sl], qkv[1, :, sl], qkv[2, :, sl], bg[:, sl]
        kt = kp.T
        masks = head_masks()
        dv = dk = None
        dq = []
        for h, hm in enumerate(masks):
            probs = softmax_t(nt(kp * hm, qp))
            dp = nt(vp * hm, cg)
            delta = jnp.sum(probs * dp, axis=0, keepdims=True)
            ds = (probs * (dp - delta)).astype(bf16)
            hf = hm.astype(f32)
            dv_h = nn(probs.astype(bf16), cg) * hf
            dk_h = nn(ds, qp) * hf
            dv = dv_h if dv is None else dv + dv_h
            dk = dk_h if dk is None else dk + dk_h
            dq.append(nn(kt[h * HD : (h + 1) * HD, :], ds))
        dqkv[0, :, sl] = (jnp.concatenate(dq, axis=0).T * (HD**-0.5)).astype(bf16)
        dqkv[1, :, sl] = dk.astype(bf16)
        dqkv[2, :, sl] = dv.astype(bf16)
        return carry

    lax.fori_loop(0, pairs, att_back, 0)
    acc[...] = nn(dqkv[0], wq[0]) + nn(dqkv[1], wq[1]) + nn(dqkv[2], wq[2])


    step2_in((1, 0, 5, 4))

    def first_back(i, carry):
        se, sg, sb = carry
        sl = rds(i * RT, RT, RT)
        up, xhat = acc[sl, :], xh1[sl, :]
        m = mown[sl, :] > 0.5
        rg = res[sl, :] + norm_back(up, xhat, r1[sl, :], gain1)
        hg[sl, :] = jnp.where(m, 0.0, rg)
        return (
            se + jnp.sum(jnp.where(m, rg, 0.0), axis=0, keepdims=True),
            sg + jnp.sum(up * xhat, axis=0, keepdims=True),
            sb + jnp.sum(up, axis=0, keepdims=True),
        )

    se, sg, sb = lax.fori_loop(0, t // RT, first_back, (none, none, none))
    sm[0:1, :], sm[1:2, :], sm[2:3, :] = se, sg, sb
    pg_own = pltpu.make_async_copy(hg, pg.at[rds(z * t, t)], ls.at[9])
    pg_own.start()
    for j, r in ((0, 7), (2, 8)):
        sm[r : r + 1, :] = jnp.sum(dqkv[j].astype(f32), axis=0, keepdims=True)

    nsm = g.wbits + g.zbits
    sm_order = [0] + list(range(g.wbits, nsm)) + list(range(1, g.wbits))
    sm_copy(sm_order[0]).start()

    for u in range(4):
        rs_core(u).wait_send()
    pg_own.wait()
    pg_step(0)
    pg_step(1)
    pg_step(2)
    step2_out((1, 0, 5, 4))
    step2_in((7, 6))
    for j in range(4):
        if j == 1:
            step2_out((7, 6))
        if j < 3:
            big = tn(dqkv[j], normed[...])
        else:
            big = tn(ctx[...], act[...])
        for zz in range(nz):
            rsb[rds(zk_inv(zz) * d + j * hs, hs), :] = big[zz * hs : (zz + 1) * hs, :]
    for u in range(ff_units, units):
        rs_core(u).start()
    out_own.wait()
    patches_copy((z + 1) % nz).start()

    segs = 7

    attn = tuple(range(ff_units, units))
    plan_in = {
        0: [lambda: step3_in((3, 2, 1, 0)), lambda: step1a(8)],
        1: [lambda: step1a(9)],
        2: [lambda: step1a(10)],
        3: [lambda: step1a(11)],
        4: [lambda: step3_in((5, 4, 7, 6))],
        5: [lambda: step2_in(attn)],
        9: [lambda: step3_in((8, 9))],
        10: [lambda: step3_in((10, 11))],
    }
    plan_out = {
        0: [lambda: step3_out((3, 2, 1, 0)), lambda: step1b(8), lambda: step1c(8)],
        1: [lambda: step1b(9), lambda: step1c(9)],
        2: [lambda: step1b(10), lambda: step1c(10)],
        3: [lambda: step1b(11), lambda: step1c(11)],
        4: [lambda: step3_out((5, 4, 7, 6)), lambda: step_z(1), lambda: step_z(0)],
        5: [lambda: step2_out(attn)],
        6: [lambda: step_z(3), lambda: step_z(2)],
        8: [lambda: step_z(5), lambda: step_z(4)],
        9: [lambda: step3_out((8, 9))],
        10: [lambda: step3_out((10, 11))],
        11: [lambda: step_z(8), lambda: step4(1), lambda: step4(2)],
        12: [lambda: step_z(9)],
        13: [lambda: step5(1), lambda: step5(2), lambda: step_z(10)],
        14: [lambda: step6(1), lambda: step6(2)],
        15: [lambda: step4(0)],
        17: [lambda: step5(0)],
        18: [lambda: step6(0)],
    }

    def run_plan(plan, s):
        for at, fns in plan.items():
            @pl.when(s == at)
            def _():
                for fn in fns:
                    fn()

    def service(s):
        run_plan(plan_out, s)
        for i, at in enumerate((0, 1, 2, 2, 3, 4, 5, 6, 6, 7, 8, 9, 10, 10, 11, 12, 13, 14, 15, 16, 17)):
            when(s == at, lambda: pg_step(i + 3))
        for i in range(nsm):
            @pl.when(s == 4 * i)
            def _():
                sm_finish(sm_order[i])
                if i + 1 < nsm:
                    sm_copy(sm_order[i + 1]).start()

    def rest(s, carry):
        clip = (z + 1 + s // segs) % nz
        seg = s % segs
        run_plan(plan_in, s)

        @pl.when(seg == 0)
        def _():
            patches_copy(clip).wait()
            first_norm(clip, False)
            project()

        @pl.when((seg == 1) & (s < segs * (nz - 2)))
        def _():
            patches_copy((clip + 1) % nz).start()

        pl.when((seg == 1) & (s >= segs))(lambda: out_copy((clip + nz - 1) % nz).wait())
        pl.when(seg == 1)(lambda: attend_range(0, pairs // 2))

        @pl.when(seg == 2)
        def _():
            attend_range(pairs // 2, pairs)
            second_norm(False)

        pl.when(seg >= 3)(lambda: feed(seg - 3, False))
        pl.when(seg == segs - 1)(lambda: write_out(clip))
        service(s)
        return carry

    lax.fori_loop(0, segs * (nz - 1), rest, 0)
    out_copy((z + nz - 1) % nz).wait()
    for i in range(nsm):
        if 4 * i >= segs * (nz - 1):
            sm_finish(sm_order[i])
            if i + 1 < nsm:
                sm_copy(sm_order[i + 1]).start()
    so_copy = pltpu.make_async_copy(sm, small_out, ls.at[9])
    so_copy.start()

    for cp in zb_copies:
        cp.wait_send()
    for zz in range(nz):
        for q in range(g.chunks):
            pl.when((zz != z) & jnp.logical_not(mid))(lambda: pg_copy(zz, q, True).wait_recv())
            pl.when((zz <= z) & has_up)(lambda: pg_copy(zz, q, True).wait_send())
            pl.when((zz >= z) & has_dn)(lambda: pg_copy(zz, q, False).wait_send())
        for p in range(3):
            for i in range(2):
                pl.when((zz <= z) & has_up)(lambda: agz(p, zz, True)[i].wait_send())
                pl.when((zz >= z) & has_dn)(lambda: agz(p, zz, False)[i].wait_send())
    for p in range(3):
        fin_c(p).wait()
        for cp in fin_xy(p) + fin_d(p):
            cp.wait_send()
    for n in range(agu):
        for cp in ag_xy(n) + ag_d(n) + (ag_c(n),):
            cp.wait_send()
    for n in range(units):
        for cp in rs_d(n) + rs_p(n):
            cp.wait_send()
        if ru_pk(n)[1] > 0:
            zz, up, dn = zdir(n)
            pl.when(up)(lambda: rs_z(n, zz, True).wait_send())
            pl.when(dn)(lambda: rs_z(n, zz, False).wait_send())
    for u in range(ff_units, units):
        rs_core(u).wait_send()
    so_copy.wait()


def closing_kernel(nz, hs, out_in, pg, ga, gb, gc, small, out, patch_grad, qkv_g, out_g, up_g, down_g, qv, up_b, *vectors):
    i = pl.program_id(0)
    out[...] = out_in[...]
    patch_grad[...] = pg[...].astype(bf16)
    up_g[...] = gb[...]
    down_g[...] = gc[...]
    first = 3 * hs // ga.shape[0]

    @pl.when(i < first)
    def _():
        qkv_g[...] = ga[...]

    @pl.when(i >= first)
    def _():
        out_g[...] = ga[...]

    @pl.when(i == 0)
    def _():
        z = lax.axis_index("narrow")
        for zz in range(nz):
            @pl.when(z == zz)
            def _():
                qv[...] = small[7:9, zz * hs : (zz + 1) * hs]
                up_b[...] = small[9 + zz : 10 + zz, :].reshape(up_b.shape)

        for k, ref in enumerate(vectors):
            ref[...] = small[k : k + 1, :].reshape(ref.shape)


def make(mesh):
    def on_device(
        patches, mask_index, mask_count, mask_embed, norm1_gain, norm1_bias, w_qkv, b_qv, w_out, b_out,
        norm2_gain, norm2_bias, w_up, b_up, w_down, b_down, cotangent,
    ):
        rows, d = patches.shape
        nz = mesh.shape["narrow"]
        t, hs, fs = rows // nz, w_qkv.shape[2], w_up.shape[1]
        assert t == PATCHES and fs == d and 4 * hs == d
        g = make_cfg(mesh, d, t, hs)
        pr = g.pr
        qkv_t = jnp.swapaxes(w_qkv, 1, 2).reshape(3 * hs, d)
        hbm = pl.BlockSpec(memory_space=pl.ANY)
        vm = pl.BlockSpec(memory_space=pltpu.VMEM)
        u = g.units

        def o(r, dt=f32):
            return jax.ShapeDtypeStruct((r, d), dt)

        out_shape = (
            o(rows, bf16), o(rows), o(d), o(d), o(d), o(16),
            o(u * d), o(u * 4 * pr), o(u * pr // 2), o(u * pr // 2), o(u * pr), o(u * pr), o(2 * u * pr), o(3 * g.groups * pr),
        )
        v = pltpu.VMEM
        scratch = [
            v((3, d, d), bf16), v((d, d), bf16), v((2 * nz, d, d), bf16),
            v((t, d), f32), v((t, d), f32), v((t, d), f32), v((t, d), bf16), v((3, t, d), bf16),
            v((t, d), bf16), v((t, d), bf16), v((t, d), bf16), v((t, d), f32), v((t, d), bf16), v((t, d), f32),
            v((t, d), f32), v((t, d), bf16), v((3, t, d), bf16), v((t, 1), f32), v((t, 1), f32), v((t, 1), f32),
            v((4 * d + 2 * nz * 4 * pr, d), f32), v((d, d), f32), v((4 * pr, d), f32),
            v((2 * pr, d), f32), v((3 * (pr + g.xr), d), f32), v((3 * (pr + g.xr), d), bf16), v((8, d), f32),
            v((nz * 8, d), f32), v((16, d), f32), v(((g.wbits + g.zbits) * 16, d), f32),
            v((3 * pr, d), f32),
            pltpu.SemaphoreType.DMA((g.nsem,)), pltpu.SemaphoreType.DMA((g.nsem,)), pltpu.SemaphoreType.DMA((40,)),
        ]
        outs = pl.pallas_call(
            functools.partial(layer_kernel, g),
            out_shape=out_shape,
            in_specs=[hbm, hbm, hbm, hbm, vm, vm, vm, pl.BlockSpec(memory_space=pltpu.SMEM)] + [vm] * 7 + [hbm, hbm],
            out_specs=[hbm] * len(out_shape),
            scratch_shapes=scratch,
            compiler_params=pltpu.CompilerParams(
                collective_id=1, has_side_effects=True, vmem_limit_bytes=64 * 2**20 - 2**17
            ),
            name="layer",
        )(
            qkv_t, w_out, w_up, w_down, b_up, b_qv, mask_index, mask_count, mask_embed, norm1_gain, norm1_bias, b_out,
            norm2_gain, norm2_bias, b_down, patches, cotangent,
        )
        steps = 8
        first = 3 * hs * steps // d

        def cut(r):
            return pl.BlockSpec((r // steps, d), lambda i: (i, 0))

        def whole(*shape):
            return pl.BlockSpec(shape, lambda i: (0,) * len(shape))

        closed = pl.pallas_call(
            functools.partial(closing_kernel, nz, hs),
            grid=(steps,),
            out_shape=(
                o(rows, bf16), o(rows, bf16), o(3 * hs), o(hs), o(d), o(d),
                jax.ShapeDtypeStruct((2, hs), f32),
            ) + (jax.ShapeDtypeStruct((d,), f32),) * 8,
            in_specs=[cut(rows), cut(rows), cut(d), cut(d), cut(d), whole(16, d)],
            out_specs=(
                cut(rows), cut(rows),
                pl.BlockSpec((d // steps, d), lambda i: (jnp.minimum(i, first - 1), 0)),
                pl.BlockSpec((d // steps, d), lambda i: (jnp.maximum(i - first, 0), 0)),
                cut(d), cut(d), whole(2, hs),
            ) + (whole(d),) * 8,
            compiler_params=pltpu.CompilerParams(vmem_limit_bytes=64 * 2**20 - 2**17),
            name="closing",
        )(*outs[:6])
        output, patch_grad, qkv_o, out_o, up_o, down_o, qvb, upb = closed[:8]
        small = closed[8:]
        return (
            output, patch_grad, small[0], small[1], small[2], jnp.swapaxes(qkv_o.reshape(3, hs, d), 1, 2), qvb, out_o, small[3],
            small[4], small[5], up_o, upb, down_o, small[6],
        )

    return on_device


def solution(mesh):
    return jax.shard_map(
        make(mesh),
        mesh=mesh,
        in_specs=(
            P("wide", None), P("wide", None), P("wide"), P(), P(), P(), P(None, None, "narrow"), P(None, "narrow"),
            P("narrow", None), P(), P(), P(), P(None, "narrow"), P("narrow"), P("narrow", None), P(), P("wide", None),
        ),
        out_specs=(
            P("wide", None), P("wide", None), P(), P(), P(), P(None, None, "narrow"), P(None, "narrow"),
            P("narrow", None), P(), P(), P(), P(None, "narrow"), P("narrow"), P("narrow", None), P(),
        ),
        check_vma=False,
    )
```

```python
import functools
import math

import jax
import jax.numpy as jnp
from jax import lax
from jax.experimental import pallas as pl
from jax.experimental.pallas import tpu as pltpu
from jax.sharding import PartitionSpec as P

HD = 64
PATCHES = 512
EPS = 1e-06
f32 = jnp.float32
bf16 = jnp.bfloat16
MESH = pl.DeviceIdType.MESH
RT = 128


def nn(a, b):
    return lax.dot_general(a, b, (((1,), (0,)), ((), ())), preferred_element_type=f32)


def nt(a, b):
    return lax.dot_general(a, b, (((1,), (1,)), ((), ())), preferred_element_type=f32)


def tn(a, b):
    return lax.dot_general(a, b, (((0,), (0,)), ((), ())), preferred_element_type=f32)


def rds(start, size, unit=8):
    if isinstance(start, int):
        return pl.ds(start, size)
    return pl.ds(pl.multiple_of(start, unit), size)


def normalise(v):
    centred = v - jnp.mean(v, axis=-1, keepdims=True)
    inverse = lax.rsqrt(jnp.mean(centred * centred, axis=-1, keepdims=True) + EPS)
    return centred * inverse, inverse


def norm_back(upstream, xhat, inverse, gain):
    weighted = upstream * gain
    return inverse * (
        weighted
        - jnp.mean(weighted, axis=-1, keepdims=True)
        - xhat * jnp.mean(weighted * xhat, axis=-1, keepdims=True)
    )


def softmax_t(scores):
    e = jnp.exp(scores - jnp.max(scores, axis=0, keepdims=True))
    return e * (1.0 / jnp.sum(e, axis=0, keepdims=True))


class Cfg:
    pass


def make_cfg(mesh, d, t, hs):
    g = Cfg()
    g.nw, g.nz = mesh.shape["wide"], mesh.shape["narrow"]
    assert g.nz == 4
    g.groups = g.nw // 8
    g.d, g.t, g.hs = d, t, hs
    g.pr = d // 8
    g.units = 3 * g.nz
    g.agu = 3 * (g.nz - 1)
    g.xr = g.pr // 3
    g.wbits = g.nw.bit_length() - 1
    g.zbits = g.nz.bit_length() - 1
    g.chunks = 8
    n = 0
    for name, count in (
        ("agz", 6 * g.nz), ("age", 6 * g.nz), ("agx", g.agu), ("agy", g.agu), ("agdx", g.agu), ("agdy", g.agu), ("agc", g.agu),
        ("rc", g.units), ("rdx", g.units), ("rdy", g.units), ("rpx", g.units), ("rpy", g.units), ("rz", 6 * g.nz),
        ("fx", 3), ("fy", 3), ("fdx", 3), ("fdy", 3), ("fc", 3), ("zb", g.nz), ("pg", 2 * g.nz * g.chunks),
        ("sm", g.wbits + g.zbits), ("fg", 3 * g.groups),
    ):
        setattr(g, name, n)
        n += count
    g.nsem = n
    return g


def when(cond, fn):
    if isinstance(cond, bool):
        if cond:
            fn()
    else:
        pl.when(cond)(fn)


def layer_kernel(
    g,
    qkv_t, w_out, w_up, w_down, b_up, b_qv, mask_index, mask_count, embed_ref, gain1_ref, bias1_ref, b_out_ref, gain2_ref,
    bias2_ref, b_down_ref, patches, cot_hbm,
    out, pg, ga, gb, gc, small_out, wbuf, crecv, dxr, dyr, pxr, pyr, zr, grecv,
    wq, wo, ffw, res, xh1, xh2, normed, qkv, ctx, hid, act, slope, cotv, acc, hg, bg, dqkv, r1, r2, mown, rsb, cst, rst,
    zst, part, pbf, zb, zball, sm, smr, fin, ss, rs, ls,
):
    nz, d, t, hs, pr, units = g.nz, g.d, g.t, g.hs, g.pr, g.units
    half = pr // 2
    ff_units = 2 * nz
    w = lax.axis_index("wide")
    z = lax.axis_index("narrow")
    c, x, y = w % 2, (w // 2) % 2, (w // 4) % 2
    sib, xn, yn = {"wide": w + 1 - 2 * c}, {"wide": w + 2 - 4 * x}, {"wide": w + 4 - 8 * y}
    zup, zdn = {"narrow": z + 1}, {"narrow": z - 1}
    has_up, has_dn = z < nz - 1, z > 0
    mid = (z > 0) & (z < nz - 1)
    yx, yx_x, yx_y, yx_d = y * 2 + x, y * 2 + 1 - x, (1 - y) * 2 + x, (1 - y) * 2 + 1 - x
    pos, pos_x, pos_y, pos_d = c * 4 + yx, c * 4 + yx_x, c * 4 + yx_y, c * 4 + yx_d
    zp = [None] + [{"narrow": (z + k) % nz} for k in range(1, nz)]
    gp = [None] + [{"wide": (w + 8 * k) % g.nw} for k in range(1, g.groups)]
    gouts = (ga, gb, gc)

    zside = z // 2
    zend = z + zside * (nz - 1 - 2 * z)

    def swap01(k):
        return k + zend * (1 - k // 2) * (1 - 2 * (k % 2))

    def zk(k):
        b = swap01(k)
        return b + zside * (nz - 1 - 2 * b)

    def zk_inv(zz):
        return swap01(zz + zside * (nz - 1 - 2 * zz))

    def rcopy(src, dst, si, ri, dev):
        return pltpu.make_async_remote_copy(src, dst, ss.at[si], rs.at[ri], device_id=dev, device_id_type=MESH)

    barrier = pltpu.get_barrier_semaphore()
    partners = [sib, xn, yn] + zp[1:] + gp[1:]
    for p in partners:
        pl.semaphore_signal(barrier, inc=1, device_id=p, device_id_type=MESH)

    def wrow(p, zz, q):
        return (p * nz + zz) * d + q * pr

    xr = g.xr
    hr = (pr - xr) // 2
    agu = g.agu

    def ag_pk(n):
        if isinstance(n, int) and n < nz - 1:
            return 0, n + 1
        m = n - (nz - 1)
        return 1 + m % 2, 1 + m // 2

    def own_loads():
        cps = [(qkv_t.at[pl.ds(j * hs, hs)], wq.at[j, rds(z * hs, hs, 16)]) for j in range(3)]
        cps += [(w_out, wo.at[rds(z * hs, hs, 16)]), (w_up, ffw.at[0]), (w_down, ffw.at[1])]
        return [pltpu.make_async_copy(src, dst, ls.at[i]) for i, (src, dst) in enumerate(cps)]

    def ag_block(n, q, lo, size):
        p, k = ag_pk(n)
        return wbuf.at[rds(wrow(p, zk(k), q) + lo, size)]

    def ag_xy(n):
        b = ag_block(n, pos, 0, pr)
        return rcopy(b, b, g.agx + n, g.agx + n, xn), rcopy(b, b, g.agy + n, g.agy + n, yn)

    def ag_d(n):
        bx, by = ag_block(n, pos_x, xr, hr), ag_block(n, pos_y, xr + hr, hr)
        return rcopy(bx, bx, g.agdy + n, g.agdy + n, yn), rcopy(by, by, g.agdx + n, g.agdx + n, xn)

    def ag_c(n):
        b = ag_block(n, c * 4, 0, 4 * pr)
        return rcopy(b, b, g.agc + n, g.agc + n, sib)

    def agz(p, zz, up, own=False):
        pair = []
        for sem, q, lo, size in ((g.agz, pos, 0, pr), (g.age, pos_d, pr, xr)):
            to = wbuf.at[rds(wrow(p, zz, q), size)]
            src = part.at[pl.ds(p * (pr + xr) + lo, size)] if own else to
            ri = sem + p * nz + zz
            pair.append(rcopy(src, to, ri + (0 if up else 3 * nz), ri, zup if up else zdn))
        return pair

    def start(cps):
        for cp in cps:
            cp.start()

    def agz_own(p):
        pl.when(has_up)(lambda: start(agz(p, z, True, True)))
        pl.when(has_dn)(lambda: start(agz(p, z, False, True)))

    def ag_z(n):
        p, k = ag_pk(n)
        zz = zk(k)

        @pl.when(mid)
        def _():
            for i, cp in enumerate(agz(p, zz, True)):
                cp.wait_recv()
                pl.when(zz < z)(lambda: agz(p, zz, True)[i].start())
                pl.when(zz > z)(lambda: agz(p, zz, False)[i].start())

    def ag_s1(n):
        p, k = ag_pk(n)
        pl.when(jnp.logical_not(mid))(lambda: agz(p, zk(k), True)[0].wait_recv())
        start(ag_xy(n))

    def ag_s2(n):
        cx, cy = ag_xy(n)
        dy, dx = ag_d(n)
        cx.wait_recv()
        dy.start()
        cy.wait_recv()
        dx.start()

    def ag_s3(n):
        p, k = ag_pk(n)
        pl.when(jnp.logical_not(mid))(lambda: agz(p, zk(k), True)[1].wait_recv())
        dy, dx = ag_d(n)
        dy.wait_recv()
        dx.wait_recv()
        ag_c(n).start()

    def ag_load(n):
        p, k = ag_pk(n)
        return [
            pltpu.make_async_copy(
                wbuf.at[rds(wrow(p, zk(k), 4 * i), 4 * pr)], cst.at[pl.ds(i * 4 * pr, 4 * pr)], ls.at[10 + i]
            )
            for i in range(2)
        ]

    def ag_conv_start(n):
        ag_c(n).wait_recv()
        start(ag_load(n))

    def ag_conv(n):
        for cp in ag_load(n):
            cp.wait()
        p, k = ag_pk(n)
        if isinstance(n, int) and n < nz - 1:
            zz = zk(k)
            for j in range(3):
                wq[j, rds(zz * hs, hs, 16), :] = cst[j * hs : (j + 1) * hs, :].astype(bf16)
            wo[rds(zz * hs, hs, 16), :] = cst[3 * hs : 4 * hs, :].astype(bf16)
        else:
            ffw[2 * k + p - 1] = cst[...].astype(bf16)

    def ag_step(n):
        static = isinstance(n, int)
        when(n < agu, lambda: ag_s2(n))
        if static:
            when(n + 2 < agu, lambda: ag_s1(n + 2))
            when(n + 3 < agu, lambda: ag_z(n + 3))
        when(n - 1 >= 0, lambda: when(n - 1 < agu, lambda: ag_s3(n - 1)))
        if not static or (n >= 2 and n != nz):
            when(n - 2 < agu, lambda: ag_conv(n - 2))
        if not static or n >= 1:
            when(n - 1 < agu, lambda: ag_conv_start(n - 1))
        if static and n == nz - 1:
            ag_conv(n - 1)

    def ru_pk(u):
        if isinstance(u, int):
            return (2 - (ff_units - 1 - u) % 2, (ff_units - 1 - u) // 2) if u < ff_units else (0, units - 1 - u)
        late = u // ff_units
        return (
            (1 - late) * (2 - (2 * ff_units - 1 - u) % 2),
            (1 - late) * ((ff_units - 1 - u + late * ff_units) // 2) + late * (units - 1 - u),
        )

    def slot_row(u):
        return ((2 * ff_units - 1 - u) % 4) * d

    def sum_row(u, q):
        if isinstance(u, int):
            base = 4 * d + u * 4 * pr if u < ff_units else slot_row(u) + c * 4 * pr
        else:
            late = u // ff_units
            base = (1 - late) * (4 * d + u * 4 * pr) + late * (slot_row(u) + c * 4 * pr)
        return base + q * pr

    def rs_core(u):
        return rcopy(
            rsb.at[rds(slot_row(u) + (1 - c) * 4 * pr, 4 * pr)], crecv.at[rds(u * 4 * pr, 4 * pr)], g.rc + u, g.rc + u, sib
        )

    def rs_d(u):
        a = rcopy(rsb.at[rds(sum_row(u, yx_d), half)], dxr.at[rds(u * half, half)], g.rdx + u, g.rdx + u, xn)
        b = rcopy(rsb.at[rds(sum_row(u, yx_d) + half, half)], dyr.at[rds(u * half, half)], g.rdy + u, g.rdy + u, yn)
        return a, b

    def rs_p(u):
        a = rcopy(rsb.at[rds(sum_row(u, yx_x), pr)], pxr.at[rds(u * pr, pr)], g.rpx + u, g.rpx + u, xn)
        b = rcopy(rsb.at[rds(sum_row(u, yx_y), pr)], pyr.at[rds(u * pr, pr)], g.rpy + u, g.rpy + u, yn)
        return a, b

    def rs_z(u, zz, up):
        p, _ = ru_pk(u)
        i = (p * nz + zz) * 2 + (0 if up else 1)
        return rcopy(rsb.at[rds(sum_row(u, yx), pr)], zr.at[rds(i * pr, pr)], g.rz + i, g.rz + i, zup if up else zdn)

    def rs_z_load(p, zz, up, slot):
        i = (p * nz + zz) * 2 + (0 if up else 1)
        src = zr.at[rds(i * pr, pr)]
        return (
            rcopy(src, src, g.rz + i, g.rz + i, sib),
            pltpu.make_async_copy(src, zst.at[pl.ds(slot * pr, pr)], ls.at[18 + slot]),
        )

    def l1(u):
        return pltpu.make_async_copy(crecv.at[rds(u * 4 * pr, 4 * pr)], rst, ls.at[12])

    def step1a(u):
        rs_core(u).wait_recv()
        l1(u).start()

    def step1b(u):
        l1(u).wait()
        src = slot_row(u) + c * 4 * pr
        rsb[rds(sum_row(u, 0), 4 * pr), :] = rsb[rds(src, 4 * pr), :] + rst[...]

    def step1c(u):
        start(rs_d(u))

    def step1(us):
        cps = [
            pltpu.make_async_copy(crecv.at[rds(u * 4 * pr, 4 * pr)], cst.at[pl.ds(i * 4 * pr, 4 * pr)], ls.at[36 + i])
            for i, u in enumerate(us)
        ]
        for u, cp in zip(us, cps):
            rs_core(u).wait_recv()
            cp.start()
        for i, (u, cp) in enumerate(zip(us, cps)):
            cp.wait()
            rsb[rds(sum_row(u, 0), 4 * pr), :] = (
                rsb[rds(slot_row(u) + c * 4 * pr, 4 * pr), :] + cst[i * 4 * pr : (i + 1) * 4 * pr, :]
            )
            step1c(u)

    def l2(u, i):
        return (
            pltpu.make_async_copy(dxr.at[rds(u * half, half)], rst.at[pl.ds(i * pr, half)], ls.at[20 + 2 * i]),
            pltpu.make_async_copy(dyr.at[rds(u * half, half)], rst.at[pl.ds(i * pr + half, half)], ls.at[21 + 2 * i]),
        )

    def step2_in(us):
        for i, u in enumerate(us):
            for cp, ld in zip(rs_d(u), l2(u, i)):
                cp.wait_recv()
                ld.start()

    def step2_out(us):
        for i, u in enumerate(us):
            for ld in l2(u, i):
                ld.wait()
            rsb[rds(sum_row(u, yx_y), half), :] += rst[i * pr : i * pr + half, :]
            rsb[rds(sum_row(u, yx_x) + half, half), :] += rst[i * pr + half : (i + 1) * pr, :]
            start(rs_p(u))

    def l3(u, i):
        return (
            pltpu.make_async_copy(pxr.at[rds(u * pr, pr)], cst.at[pl.ds(2 * i * pr, pr)], ls.at[28 + 2 * i]),
            pltpu.make_async_copy(pyr.at[rds(u * pr, pr)], cst.at[pl.ds((2 * i + 1) * pr, pr)], ls.at[29 + 2 * i]),
        )

    def zdir(u):
        _, k = ru_pk(u)
        zz = zk(k)
        return zz, zz > z, zz < z

    def step3_in(us):
        for i, u in enumerate(us):
            for cp, ld in zip(rs_p(u), l3(u, i)):
                cp.wait_recv()
                ld.start()

    def step3_out(us):
        for i, u in enumerate(us):
            for ld in l3(u, i):
                ld.wait()
            rsb[rds(sum_row(u, yx), pr), :] += (
                cst[2 * i * pr : (2 * i + 1) * pr, :] + cst[(2 * i + 1) * pr : (2 * i + 2) * pr, :]
            )
            if ru_pk(u)[1] > 0:
                zz, up, dn = zdir(u)
                pl.when(up & (z == 0))(lambda: rs_z(u, zz, True).start())
                pl.when(dn & (z == nz - 1))(lambda: rs_z(u, zz, False).start())

    def step_z(u):
        p, _ = ru_pk(u)
        zz, up, dn = zdir(u)
        for cond, flag in ((up, True), (dn, False)):
            @pl.when(cond & mid)
            def _():
                got, ld = rs_z_load(p, zz, flag, 0)
                got.wait_recv()
                ld.start()
                ld.wait()
                rsb[rds(sum_row(u, yx), pr), :] += zst[0:pr, :]
                rs_z(u, zz, flag).start()

    own_unit = {0: units - 1, 1: ff_units - 2, 2: ff_units - 1}

    def fin_xy(p):
        src = fin.at[pl.ds(p * pr, pr)]
        to = gouts[p].at[rds(pos * pr, pr)]
        return rcopy(src, to, g.fx + p, g.fx + p, xn), rcopy(src, to, g.fy + p, g.fy + p, yn)

    def fin_own(p):
        return pltpu.make_async_copy(fin.at[pl.ds(p * pr, pr)], gouts[p].at[rds(pos * pr, pr)], ls.at[5 + p])

    def fin_d(p):
        bx, by = gouts[p].at[rds(pos_x * pr, half)], gouts[p].at[rds(pos_y * pr + half, half)]
        return rcopy(bx, bx, g.fdy + p, g.fdy + p, yn), rcopy(by, by, g.fdx + p, g.fdx + p, xn)

    def fin_c(p):
        b = gouts[p].at[rds(c * 4 * pr, 4 * pr)]
        return rcopy(b, b, g.fc + p, g.fc + p, sib)

    def fin_g(p, k):
        return rcopy(
            fin.at[pl.ds(p * pr, pr)], grecv.at[pl.ds((p * g.groups + g.groups - k) * pr, pr)],
            g.fg + p * g.groups + k, g.fg + p * g.groups + g.groups - k, gp[k],
        )

    def step4(p):
        sl = slice(p * pr, (p + 1) * pr)
        fin[sl, :] = rsb[rds(sum_row(own_unit[p], yx), pr), :]
        ins = ((has_dn, True, 0), (has_up, False, 1))
        for cond, flag, slot in ins:
            @pl.when(cond)
            def _():
                got, ld = rs_z_load(p, z, flag, slot)
                got.wait_recv()
                ld.start()

        for cond, flag, slot in ins:
            @pl.when(cond)
            def _():
                rs_z_load(p, z, flag, slot)[1].wait()
                fin[sl, :] += zst[slot * pr : (slot + 1) * pr, :]

        if g.groups > 1:
            total = fin[sl, :]
            for k in range(1, g.groups):
                fin_g(p, k).start()
            for k in range(1, g.groups):
                fin_g(p, k).wait()
            for k in range(1, g.groups):
                src = grecv.at[pl.ds((p * g.groups + k) * pr, pr)]
                cp = pltpu.make_async_copy(src, zst.at[pl.ds(0, pr)], ls.at[3])
                cp.start()
                cp.wait()
                total = total + zst[0:pr, :]
            fin[sl, :] = total
        fin_own(p).start()
        for cp in fin_xy(p):
            cp.start()

    def step5(p):
        cx, cy = fin_xy(p)
        dy, dx = fin_d(p)
        cx.wait_recv()
        dy.start()
        cy.wait_recv()
        dx.start()

    def step6(p):
        dy, dx = fin_d(p)
        dy.wait_recv()
        dx.wait_recv()
        fin_own(p).wait()
        fin_c(p).start()

    def sm_copy(i):
        if i < g.wbits:
            b = 1 << i
            dev = {"wide": w + b - 2 * b * ((w // b) % 2)}
        else:
            b = 1 << (i - g.wbits)
            dev = {"narrow": z + b - 2 * b * ((z // b) % 2)}
        return rcopy(sm, smr.at[pl.ds(16 * i, 16)], g.sm + i, g.sm + i, dev)

    def sm_finish(i):
        sm_copy(i).wait()
        sm[...] += smr[16 * i : 16 * (i + 1), :]

    ck = t // g.chunks

    def pg_copy(zz, q, up):
        to = pg.at[rds(zz * t + q * ck, ck)]
        ri = g.pg + zz * g.chunks + q
        return rcopy(to, to, ri + (0 if up else nz * g.chunks), ri, zup if up else zdn)

    def pg_send(zz, q, up):
        pg_copy(zz, q, up).start()

    def pg_step(s):
        if s < g.chunks:
            pl.when(has_up)(lambda: pg_send(z, s, True))
            pl.when(has_dn)(lambda: pg_send(z, s, False))
            return
        j = s - g.chunks
        for up, zz, count, more in (
            (True, z - 1 - j // g.chunks, g.chunks * z, has_up),
            (False, z + 1 + j // g.chunks, g.chunks * (nz - 1 - z), has_dn),
        ):
            @pl.when((j < count) & more)
            def _():
                pg_copy(zz, j % g.chunks, up).wait_recv()
                pg_send(zz, j % g.chunks, up)

    embed, gain1, bias1, b_out, gain2, bias2, b_down = [
        ref[...].reshape(1, d)
        for ref in (embed_ref, gain1_ref, bias1_ref, b_out_ref, gain2_ref, bias2_ref, b_down_ref)
    ]

    def tiles(fn):
        def body(i, carry):
            fn(rds(i * RT, RT, RT), i * RT)
            return carry

        lax.fori_loop(0, t // RT, body, 0)

    def patches_copy(clip):
        return pltpu.make_async_copy(patches.at[rds(clip * t, t, 16)], bg, ls.at[8])

    def first_norm(clip, keep):
        slots = lax.broadcasted_iota(jnp.int32, (1, mask_index.shape[1]), 1)
        listed = jnp.where(slots < mask_count[clip], mask_index[pl.ds(clip, 1), :], -1)

        def fn(sl, at):
            place = lax.broadcasted_iota(jnp.int32, (RT, listed.shape[1]), 0) + at
            m = jnp.max(jnp.where(listed == place, 1.0, 0.0), axis=1, keepdims=True)
            v = jnp.where(m > 0.5, embed, bg[sl, :].astype(f32))
            res[sl, :] = v
            xhat, inverse = normalise(v)
            if keep:
                mown[sl, :] = m
                xh1[sl, :] = xhat
                r1[sl, :] = inverse
            normed[sl, :] = (xhat * gain1 + bias1).astype(bf16)

        tiles(fn)

    def project():
        biases = []
        for i in (1, 2):
            total = zball[i : i + 1, :]
            for k in range(1, nz):
                total = total + zball[8 * k + i : 8 * k + i + 1, :]
            biases.append(total)
        n = normed[...]
        qkv[0] = ((nt(n, wq[0]) + biases[0]).astype(bf16) * bf16(HD**-0.5)).astype(bf16)
        qkv[1] = nt(n, wq[1]).astype(bf16)
        qkv[2] = (nt(n, wq[2]) + biases[1]).astype(bf16)

    def head_masks():
        lane = lax.broadcasted_iota(jnp.int32, (1, 2 * HD), 1)
        first = (lane < HD).astype(f32)
        return first.astype(bf16), (1.0 - first).astype(bf16)

    def attend(i):
        sl = rds(i * 2 * HD, 2 * HD, 2 * HD)
        qp, kp, vp = qkv[0, :, sl], qkv[1, :, sl], qkv[2, :, sl]
        vt = vp.T
        outs = []
        for h, hm in enumerate(head_masks()):
            probs = softmax_t(nt(kp * hm, qp)).astype(bf16)
            outs.append(nn(vt[h * HD : (h + 1) * HD, :], probs))
        ctx[:, sl] = jnp.concatenate(outs, axis=0).T.astype(bf16)

    def attend_range(lo, hi):
        def body(i, carry):
            attend(i)
            return carry

        lax.fori_loop(lo, hi, body, 0)

    def second_norm(keep):
        acc[...] = nn(ctx[...], wo[...])

        def fn(sl, at):
            v = res[sl, :] + acc[sl, :] + b_out
            res[sl, :] = v
            xhat, inverse = normalise(v)
            if keep:
                xh2[sl, :] = xhat
                r2[sl, :] = inverse
            hid[sl, :] = (xhat * gain2 + bias2).astype(bf16)
            acc[sl, :] = jnp.zeros((RT, d), f32)

        tiles(fn)

    def feed(k, keep):
        bias = zball[rds(zk(k) * 8, 8), :][0:1, :]
        slope[...] = nn(hid[...], ffw[2 * k])

        def fn(sl, at):
            v = slope[sl, :] + bias
            cdf = 0.5 * (1.0 + lax.erf(v * (0.5**0.5)))
            act[sl, :] = (v * cdf).astype(bf16)
            if keep:
                slope[sl, :] = cdf + v * jnp.exp(-0.5 * v * v) * ((0.5 / math.pi) ** 0.5)

        tiles(fn)
        acc[...] += nn(act[...], ffw[2 * k + 1])

    def out_copy(clip):
        return pltpu.make_async_copy(act, out.at[rds(clip * t, t, 16)], ls.at[38])

    def write_out(clip):
        def fn(sl, at):
            act[sl, :] = (res[sl, :] + acc[sl, :] + b_down).astype(bf16)

        tiles(fn)
        out_copy(clip).start()

    def feed_back(k):
        acc2 = nt(cotv[...], ffw[2 * k + 1])
        b = (acc2 * slope[...]).astype(bf16)
        bg[...] = b
        sm[pl.ds(9 + zk(k), 1), :] = jnp.sum(b.astype(f32), axis=0, keepdims=True)
        part_sum = nt(bg[...], ffw[2 * k])

        @pl.when(k == 0)
        def _():
            hg[...] = part_sum

        @pl.when(k > 0)
        def _():
            hg[...] += part_sum

    sm[...] = jnp.zeros((16, d), f32)
    cot_copy = pltpu.make_async_copy(cot_hbm.at[rds(z * t, t, 16)], cotv, ls.at[9])
    shares = []
    first_rows = 3 * hs // pr
    for p, src in enumerate((qkv_t, w_up, w_down)):
        for q, lo, size in ((pos, 0, pr), (pos_d, pr, xr)):
            i = len(shares)
            to = pbf.at[pl.ds(p * (pr + xr) + lo, size)]

            def share(ref, row):
                return pltpu.make_async_copy(ref.at[rds(row, size, 16)], to, ls.at[20 + i])

            if p == 0:
                pl.when(q < first_rows)(lambda: share(qkv_t, q * pr).start())
                pl.when(q >= first_rows)(lambda: share(w_out, (q - first_rows) * pr).start())
                shares.append(share(w_out, 0))
            else:
                shares.append(share(src, q * pr))
                shares[-1].start()
    patches_copy(z).start()
    own = own_loads()
    start(own)
    cot_copy.start()
    zb[...] = jnp.zeros((8, d), f32)
    zb[0:1, :] = b_up[...].reshape(1, d)
    for zz in range(nz):
        @pl.when(z == zz)
        def _():
            zb[1:3, zz * hs : (zz + 1) * hs] = b_qv[...]

    zball[rds(z * 8, 8), :] = zb[...]
    for cp in shares:
        cp.wait()
    part[...] = pbf[...].astype(f32)
    pl.semaphore_wait(barrier, len(partners))
    agz_own(0)
    zb_copies = [
        rcopy(zb, zball.at[rds(z * 8, 8)], g.zb + k, g.zb + nz - k, zp[k]) for k in range(1, nz)
    ]
    start(zb_copies)
    patches_copy(z).wait()
    first_norm(z, True)
    ag_z(0)
    ag_s1(0)
    ag_z(1)
    pl.when(mid)(lambda: ag_s1(1))
    ag_z(2)
    agz_own(1)
    agz_own(2)
    ag_s2(0)
    pl.when(jnp.logical_not(mid))(lambda: ag_s1(1))
    ag_s1(2)
    ag_z(3)
    for n in range(1, nz):
        ag_step(n)
    for cp in own:
        cp.wait()
    for k in range(1, nz):
        rcopy(zb, zball.at[rds(((z + k) % nz) * 8, 8)], g.zb + k, g.zb + k, zp[k]).wait_recv()
    pairs = nz * hs // (2 * HD)
    project()
    for i in range(3):
        ag_step(nz + i)
        attend_range(i * pairs // 3, (i + 1) * pairs // 3)
    second_norm(True)
    cot_copy.wait()

    def ff_body(k, carry):
        ud, uu = ff_units - 1 - 2 * k, ff_units - 2 - 2 * k
        ag_step(nz + 3 + k)

        @pl.when(k >= 2)
        def _():
            rs_core(ud + 4).wait_send()
            rs_core(uu + 4).wait_send()

        pl.when(k >= 1)(lambda: step1a(ud + 2))
        feed(k, True)
        rsb[rds(slot_row(ud), d), :] = tn(act[...], cotv[...])
        rs_core(ud).start()

        @pl.when(k >= 1)
        def _():
            step1b(ud + 2)
            step1c(ud + 2)
            step1a(uu + 2)

        feed_back(k)

        @pl.when(k >= 1)
        def _():
            step1b(uu + 2)
            step1c(uu + 2)

        rsb[rds(slot_row(uu), d), :] = tn(hid[...], bg[...])
        rs_core(uu).start()
        return carry

    lax.fori_loop(0, nz, ff_body, 0)
    step1((1, 0))
    step2_in((3, 2))

    none = jnp.zeros((1, d), f32)

    def mid_back(i, carry):
        sg, sb, so, sc = carry
        sl = rds(i * RT, RT, RT)
        up, xhat = hg[sl, :], xh2[sl, :]
        cf = cotv[sl, :].astype(f32)
        mg = cf + norm_back(up, xhat, r2[sl, :], gain2)
        v = res[sl, :] + acc[sl, :] + b_down
        hid[sl, :] = v.astype(bf16)
        res[sl, :] = mg
        act[sl, :] = mg.astype(bf16)
        return (
            sg + jnp.sum(up * xhat, axis=0, keepdims=True),
            sb + jnp.sum(up, axis=0, keepdims=True),
            so + jnp.sum(mg, axis=0, keepdims=True),
            sc + jnp.sum(cf, axis=0, keepdims=True),
        )

    sg, sb, so, sc = lax.fori_loop(0, t // RT, mid_back, (none, none, none, none))
    step2_out((3, 2))
    sm[3:4, :], sm[4:5, :], sm[5:6, :], sm[6:7, :] = so, sg, sb, sc
    out_own = pltpu.make_async_copy(hid, out.at[rds(z * t, t, 16)], ls.at[8])
    out_own.start()
    bg[...] = nt(act[...], wo[...]).astype(bf16)

    def att_back(i, carry):
        sl = rds(i * 2 * HD, 2 * HD, 2 * HD)
        qp, kp, vp, cg = qkv[0, :, sl], qkv[1, :, sl], qkv[2, :, sl], bg[:, sl]
        kt = kp.T
        masks = head_masks()
        dv = dk = None
        dq = []
        for h, hm in enumerate(masks):
            probs = softmax_t(nt(kp * hm, qp))
            dp = nt(vp * hm, cg)
            delta = jnp.sum(probs * dp, axis=0, keepdims=True)
            ds = (probs * (dp - delta)).astype(bf16)
            hf = hm.astype(f32)
            dv_h = nn(probs.astype(bf16), cg) * hf
            dk_h = nn(ds, qp) * hf
            dv = dv_h if dv is None else dv + dv_h
            dk = dk_h if dk is None else dk + dk_h
            dq.append(nn(kt[h * HD : (h + 1) * HD, :], ds))
        dqkv[0, :, sl] = (jnp.concatenate(dq, axis=0).T * (HD**-0.5)).astype(bf16)
        dqkv[1, :, sl] = dk.astype(bf16)
        dqkv[2, :, sl] = dv.astype(bf16)
        return carry

    lax.fori_loop(0, pairs, att_back, 0)
    acc[...] = nn(dqkv[0], wq[0]) + nn(dqkv[1], wq[1]) + nn(dqkv[2], wq[2])


    step2_in((1, 0, 5, 4))

    def first_back(i, carry):
        se, sg, sb = carry
        sl = rds(i * RT, RT, RT)
        up, xhat = acc[sl, :], xh1[sl, :]
        m = mown[sl, :] > 0.5
        rg = res[sl, :] + norm_back(up, xhat, r1[sl, :], gain1)
        hg[sl, :] = jnp.where(m, 0.0, rg)
        return (
            se + jnp.sum(jnp.where(m, rg, 0.0), axis=0, keepdims=True),
            sg + jnp.sum(up * xhat, axis=0, keepdims=True),
            sb + jnp.sum(up, axis=0, keepdims=True),
        )

    se, sg, sb = lax.fori_loop(0, t // RT, first_back, (none, none, none))
    sm[0:1, :], sm[1:2, :], sm[2:3, :] = se, sg, sb
    pg_own = pltpu.make_async_copy(hg, pg.at[rds(z * t, t)], ls.at[9])
    pg_own.start()
    for j, r in ((0, 7), (2, 8)):
        sm[r : r + 1, :] = jnp.sum(dqkv[j].astype(f32), axis=0, keepdims=True)

    nsm = g.wbits + g.zbits
    sm_order = [0] + list(range(g.wbits, nsm)) + list(range(1, g.wbits))
    sm_copy(sm_order[0]).start()

    for u in range(4):
        rs_core(u).wait_send()
    pg_own.wait()
    pg_step(0)
    pg_step(1)
    pg_step(2)
    step2_out((1, 0, 5, 4))
    step2_in((7, 6))
    for j in range(4):
        if j == 1:
            step2_out((7, 6))
        if j < 3:
            big = tn(dqkv[j], normed[...])
        else:
            big = tn(ctx[...], act[...])
        for zz in range(nz):
            rsb[rds(zk_inv(zz) * d + j * hs, hs), :] = big[zz * hs : (zz + 1) * hs, :]
    for u in range(ff_units, units):
        rs_core(u).start()
    out_own.wait()
    patches_copy((z + 1) % nz).start()

    segs = 7

    attn = tuple(range(ff_units, units))
    plan_in = {
        0: [lambda: step3_in((3, 2, 1, 0)), lambda: step1a(8)],
        1: [lambda: step1a(9)],
        2: [lambda: step1a(10)],
        3: [lambda: step1a(11)],
        4: [lambda: step3_in((5, 4, 7, 6))],
        5: [lambda: step2_in(attn)],
        9: [lambda: step3_in((8, 9))],
        10: [lambda: step3_in((10, 11))],
    }
    plan_out = {
        0: [lambda: step3_out((3, 2, 1, 0)), lambda: step1b(8), lambda: step1c(8)],
        1: [lambda: step1b(9), lambda: step1c(9)],
        2: [lambda: step1b(10), lambda: step1c(10)],
        3: [lambda: step1b(11), lambda: step1c(11)],
        4: [lambda: step3_out((5, 4, 7, 6)), lambda: step_z(1), lambda: step_z(0)],
        5: [lambda: step2_out(attn)],
        6: [lambda: step_z(3), lambda: step_z(2)],
        8: [lambda: step_z(5), lambda: step_z(4)],
        9: [lambda: step3_out((8, 9))],
        10: [lambda: step3_out((10, 11))],
        11: [lambda: step_z(8), lambda: step4(1), lambda: step4(2)],
        12: [lambda: step_z(9)],
        13: [lambda: step5(1), lambda: step5(2), lambda: step_z(10)],
        14: [lambda: step6(1), lambda: step6(2)],
        15: [lambda: step4(0)],
        17: [lambda: step5(0)],
        18: [lambda: step6(0)],
    }

    def run_plan(plan, s):
        for at, fns in plan.items():
            @pl.when(s == at)
            def _():
                for fn in fns:
                    fn()

    def service(s):
        run_plan(plan_out, s)
        for i, at in enumerate((0, 1, 2, 2, 3, 4, 5, 6, 6, 7, 8, 9, 10, 10, 11, 12, 13, 14, 15, 16, 17)):
            when(s == at, lambda: pg_step(i + 3))
        for i in range(nsm):
            @pl.when(s == 4 * i)
            def _():
                sm_finish(sm_order[i])
                if i + 1 < nsm:
                    sm_copy(sm_order[i + 1]).start()

    def rest(s, carry):
        clip = (z + 1 + s // segs) % nz
        seg = s % segs
        run_plan(plan_in, s)

        @pl.when(seg == 0)
        def _():
            patches_copy(clip).wait()
            first_norm(clip, False)
            project()

        @pl.when((seg == 1) & (s < segs * (nz - 2)))
        def _():
            patches_copy((clip + 1) % nz).start()

        pl.when((seg == 1) & (s >= segs))(lambda: out_copy((clip + nz - 1) % nz).wait())
        pl.when(seg == 1)(lambda: attend_range(0, pairs // 2))

        @pl.when(seg == 2)
        def _():
            attend_range(pairs // 2, pairs)
            second_norm(False)

        pl.when(seg >= 3)(lambda: feed(seg - 3, False))
        pl.when(seg == segs - 1)(lambda: write_out(clip))
        service(s)
        return carry

    lax.fori_loop(0, segs * (nz - 1), rest, 0)
    out_copy((z + nz - 1) % nz).wait()
    for i in range(nsm):
        if 4 * i >= segs * (nz - 1):
            sm_finish(sm_order[i])
            if i + 1 < nsm:
                sm_copy(sm_order[i + 1]).start()
    so_copy = pltpu.make_async_copy(sm, small_out, ls.at[9])
    so_copy.start()

    for cp in zb_copies:
        cp.wait_send()
    for zz in range(nz):
        for q in range(g.chunks):
            pl.when((zz != z) & jnp.logical_not(mid))(lambda: pg_copy(zz, q, True).wait_recv())
            pl.when((zz <= z) & has_up)(lambda: pg_copy(zz, q, True).wait_send())
            pl.when((zz >= z) & has_dn)(lambda: pg_copy(zz, q, False).wait_send())
        for p in range(3):
            for i in range(2):
                pl.when((zz <= z) & has_up)(lambda: agz(p, zz, True)[i].wait_send())
                pl.when((zz >= z) & has_dn)(lambda: agz(p, zz, False)[i].wait_send())
    for p in range(3):
        fin_c(p).wait()
        for cp in fin_xy(p) + fin_d(p):
            cp.wait_send()
    for n in range(agu):
        for cp in ag_xy(n) + ag_d(n) + (ag_c(n),):
            cp.wait_send()
    for n in range(units):
        for cp in rs_d(n) + rs_p(n):
            cp.wait_send()
        if ru_pk(n)[1] > 0:
            zz, up, dn = zdir(n)
            pl.when(up)(lambda: rs_z(n, zz, True).wait_send())
            pl.when(dn)(lambda: rs_z(n, zz, False).wait_send())
    for u in range(ff_units, units):
        rs_core(u).wait_send()
    so_copy.wait()


def closing_kernel(nz, hs, out_in, pg, ga, gb, gc, small, out, patch_grad, qkv_g, out_g, up_g, down_g, qv, up_b, *vectors):
    i = pl.program_id(0)
    out[...] = out_in[...]
    patch_grad[...] = pg[...].astype(bf16)
    up_g[...] = gb[...]
    down_g[...] = gc[...]
    first = 3 * hs // ga.shape[0]

    @pl.when(i < first)
    def _():
        qkv_g[...] = ga[...]

    @pl.when(i >= first)
    def _():
        out_g[...] = ga[...]

    @pl.when(i == 0)
    def _():
        z = lax.axis_index("narrow")
        for zz in range(nz):
            @pl.when(z == zz)
            def _():
                qv[...] = small[7:9, zz * hs : (zz + 1) * hs]
                up_b[...] = small[9 + zz : 10 + zz, :].reshape(up_b.shape)

        for k, ref in enumerate(vectors):
            ref[...] = small[k : k + 1, :].reshape(ref.shape)


def make(mesh):
    def on_device(
        patches, mask_index, mask_count, mask_embed, norm1_gain, norm1_bias, w_qkv, b_qv, w_out, b_out,
        norm2_gain, norm2_bias, w_up, b_up, w_down, b_down, cotangent,
    ):
        rows, d = patches.shape
        nz = mesh.shape["narrow"]
        t, hs, fs = rows // nz, w_qkv.shape[2], w_up.shape[1]
        assert t == PATCHES and fs == d and 4 * hs == d
        g = make_cfg(mesh, d, t, hs)
        pr = g.pr
        qkv_t = jnp.swapaxes(w_qkv, 1, 2).reshape(3 * hs, d)
        hbm = pl.BlockSpec(memory_space=pl.ANY)
        vm = pl.BlockSpec(memory_space=pltpu.VMEM)
        u = g.units

        def o(r, dt=f32):
            return jax.ShapeDtypeStruct((r, d), dt)

        out_shape = (
            o(rows, bf16), o(rows), o(d), o(d), o(d), o(16),
            o(u * d), o(u * 4 * pr), o(u * pr // 2), o(u * pr // 2), o(u * pr), o(u * pr), o(2 * u * pr), o(3 * g.groups * pr),
        )
        v = pltpu.VMEM
        scratch = [
            v((3, d, d), bf16), v((d, d), bf16), v((2 * nz, d, d), bf16),
            v((t, d), f32), v((t, d), f32), v((t, d), f32), v((t, d), bf16), v((3, t, d), bf16),
            v((t, d), bf16), v((t, d), bf16), v((t, d), bf16), v((t, d), f32), v((t, d), bf16), v((t, d), f32),
            v((t, d), f32), v((t, d), bf16), v((3, t, d), bf16), v((t, 1), f32), v((t, 1), f32), v((t, 1), f32),
            v((4 * d + 2 * nz * 4 * pr, d), f32), v((d, d), f32), v((4 * pr, d), f32),
            v((2 * pr, d), f32), v((3 * (pr + g.xr), d), f32), v((3 * (pr + g.xr), d), bf16), v((8, d), f32),
            v((nz * 8, d), f32), v((16, d), f32), v(((g.wbits + g.zbits) * 16, d), f32),
            v((3 * pr, d), f32),
            pltpu.SemaphoreType.DMA((g.nsem,)), pltpu.SemaphoreType.DMA((g.nsem,)), pltpu.SemaphoreType.DMA((40,)),
        ]
        outs = pl.pallas_call(
            functools.partial(layer_kernel, g),
            out_shape=out_shape,
            in_specs=[hbm, hbm, hbm, hbm, vm, vm, vm, pl.BlockSpec(memory_space=pltpu.SMEM)] + [vm] * 7 + [hbm, hbm],
            out_specs=[hbm] * len(out_shape),
            scratch_shapes=scratch,
            compiler_params=pltpu.CompilerParams(
                collective_id=1, has_side_effects=True, vmem_limit_bytes=64 * 2**20 - 2**17
            ),
            name="layer",
        )(
            qkv_t, w_out, w_up, w_down, b_up, b_qv, mask_index, mask_count, mask_embed, norm1_gain, norm1_bias, b_out,
            norm2_gain, norm2_bias, b_down, patches, cotangent,
        )
        steps = 4
        first = 3 * hs * steps // d

        def cut(r):
            return pl.BlockSpec((r // steps, d), lambda i: (i, 0))

        def whole(*shape):
            return pl.BlockSpec(shape, lambda i: (0,) * len(shape))

        closed = pl.pallas_call(
            functools.partial(closing_kernel, nz, hs),
            grid=(steps,),
            out_shape=(
                o(rows, bf16), o(rows, bf16), o(3 * hs), o(hs), o(d), o(d),
                jax.ShapeDtypeStruct((2, hs), f32),
            ) + (jax.ShapeDtypeStruct((d,), f32),) * 8,
            in_specs=[cut(rows), cut(rows), cut(d), cut(d), cut(d), whole(16, d)],
            out_specs=(
                cut(rows), cut(rows),
                pl.BlockSpec((d // steps, d), lambda i: (jnp.minimum(i, first - 1), 0)),
                pl.BlockSpec((d // steps, d), lambda i: (jnp.maximum(i - first, 0), 0)),
                cut(d), cut(d), whole(2, hs),
            ) + (whole(d),) * 8,
            compiler_params=pltpu.CompilerParams(vmem_limit_bytes=64 * 2**20 - 2**17),
            name="closing",
        )(*outs[:6])
        output, patch_grad, qkv_o, out_o, up_o, down_o, qvb, upb = closed[:8]
        small = closed[8:]
        return (
            output, patch_grad, small[0], small[1], small[2], jnp.swapaxes(qkv_o.reshape(3, hs, d), 1, 2), qvb, out_o, small[3],
            small[4], small[5], up_o, upb, down_o, small[6],
        )

    return on_device


def solution(mesh):
    return jax.shard_map(
        make(mesh),
        mesh=mesh,
        in_specs=(
            P("wide", None), P("wide", None), P("wide"), P(), P(), P(), P(None, None, "narrow"), P(None, "narrow"),
            P("narrow", None), P(), P(), P(), P(None, "narrow"), P("narrow"), P("narrow", None), P(), P("wide", None),
        ),
        out_specs=(
            P("wide", None), P("wide", None), P(), P(), P(), P(None, None, "narrow"), P(None, "narrow"),
            P("narrow", None), P(), P(), P(), P(None, "narrow"), P("narrow"), P("narrow", None), P(),
        ),
        check_vma=False,
    )
```
